32 devices in a mesh: dp: 8 (over z, y), blk: 4 (over x, core).
Axes of the slice: x: 2, y: 2, z: 4, core: 2. Of those that a mesh axis runs over, the one named last changes fastest.
Arguments:
- tokens: bfloat16 [16384, 768], P(('dp', 'blk')), may hold values from -6 to 6
- grad_out: bfloat16 [16384, 768], P(('dp', 'blk')), may hold values from -6 to 6
- segment: int32 [16384], P(('dp', 'blk')), may hold values from 0 to 3, as said below
- live_rows: int32 [16384], P(('dp', 'blk')), may hold values from 0 to 1, as said below
- coords: int32 [2, 16384], P(None, ('dp', 'blk')), may hold values from 0 to 85, as said below
- ln1_gain: bfloat16 [768], replicated, may hold values from 0.099609375 to 1.8984375
- ln1_bias: bfloat16 [768], replicated, may hold values from -3 to 3
- w_qkv: bfloat16 [768, 2304], replicated, may hold values from -0.21875 to 0.21875
- b_query: bfloat16 [768], replicated, may hold values from -3 to 3
- b_value: bfloat16 [768], replicated, may hold values from -3 to 3
- w_out: bfloat16 [768, 768], replicated, may hold values from -0.875 to 0.875
- b_out: bfloat16 [768], replicated, may hold values from -3 to 3
- scale_attn: bfloat16 [768], replicated, may hold values from 0.5 to 2
- ln2_gain: bfloat16 [768], replicated, may hold values from 0.099609375 to 1.8984375
- ln2_bias: bfloat16 [768], replicated, may hold values from -3 to 3
- w_fc1: bfloat16 [768, 3072], replicated, may hold values from -0.21875 to 0.21875
- b_fc1: bfloat16 [3072], replicated, may hold values from -3 to 3
- w_fc2: bfloat16 [3072, 768], replicated, may hold values from -0.21875 to 0.21875
- b_fc2: bfloat16 [768], replicated, may hold values from -3 to 3
- scale_mlp: bfloat16 [768], replicated, may hold values from 0.5 to 2
- table_rows: bfloat16 [12, 63], replicated, may hold values from -4 to 4
- table_cols: bfloat16 [12, 63], replicated, may hold values from -4 to 4
Outputs:
- out: bfloat16 [16384, 768], P(('dp', 'blk'))
- grad_tokens: float32 [16384, 768], P(('dp', 'blk'))
- grad_ln1_gain: float32 [768], replicated
- grad_ln1_bias: float32 [768], replicated
- grad_w_qkv: float32 [768, 2304], P('dp')
- grad_b_query: float32 [768], replicated
- grad_b_value: float32 [768], replicated
- grad_w_out: float32 [768, 768], P('dp')
- grad_b_out: float32 [768], replicated
- grad_scale_attn: float32 [768], replicated
- grad_ln2_gain: float32 [768], replicated
- grad_ln2_bias: float32 [768], replicated
- grad_w_fc1: float32 [768, 3072], P('dp')
- grad_b_fc1: float32 [3072], replicated
- grad_w_fc2: float32 [3072, 768], P('dp')
- grad_b_fc2: float32 [768], replicated
- grad_scale_mlp: float32 [768], replicated
- grad_table_rows: float32 [12, 63], replicated
- grad_table_cols: float32 [12, 63], replicated
- root_means: float32 [3], replicated
The draws below stay inside these ranges and needn't reach their ends.
Inputs may be any that keep to these rules, and one draw needn't show every extreme that they name: `segment`: within each group of 2048 rows the numbers never fall; page 0 starts at the group's first row and has more than 1536 rows; later pages have 197 rows; padding rows carry a number of their own after the last page. `live_rows`: the live rows of each group are a prefix of it. `coords`: A patch's row and column in its page, 0 on padding rows.
All inputs are finite; a program needn't handle non-finite values.
Results may differ from the reference program's by a relative error of at most 0.019.
Values may be sent and summed in bfloat16 or wider, within the bound.
A program may use at most 256 MiB of HBM per device.

```python
import math
import jax
import jax.numpy as jnp
from jax import lax

D = 768
H = 12
HD = 64
FF = 3072
RSPAN = 32
PAGE = 197
TOK_DEV = 512
NREL = 63
GROUP = 2048
TOKENS = 16384
N_DP = 8
N_BLK = 4


def page_layout(key):
    group_rows = TOK_DEV * N_BLK
    lowest = (N_BLK - 1) * TOK_DEV + 1
    narrow = RSPAN * 3 // 4
    long_rows = jax.random.randint(jax.random.fold_in(key, 11), (N_DP, 1), lowest, group_rows + 1)
    long_width = jax.random.randint(jax.random.fold_in(key, 12), (N_DP, 1), narrow, 2 * RSPAN + 1)
    chosen = jax.random.randint(jax.random.fold_in(key, 13), (), 0, N_DP)
    following = (chosen + 1) % N_DP
    group_ids = jnp.arange(N_DP, dtype=jnp.int32)[:, None]
    long_rows = jnp.where(group_ids == chosen, lowest, long_rows)
    long_rows = jnp.where(group_ids == following, group_rows, long_rows)
    long_width = jnp.where(group_ids == chosen, 2 * RSPAN, long_width)
    long_width = jnp.where(group_ids == following, narrow, long_width)
    short_width = max(2, RSPAN * 7 // 16)
    position = jnp.arange(group_rows, dtype=jnp.int32)[None, :]
    inside = position < long_rows
    offset_rows = jnp.maximum(position - long_rows, 0)
    shorts = (group_rows - long_rows) // PAGE
    used_rows = long_rows + shorts * PAGE
    live_flags = (position < used_rows).astype(jnp.int32)
    segment_ids = jnp.where(inside, 0, 1 + offset_rows // PAGE)
    in_page = jnp.where(inside, position, offset_rows % PAGE)
    page_width = jnp.where(inside, long_width, short_width)
    row_ids = jnp.where(live_flags > 0, in_page // page_width, 0)
    col_ids = jnp.where(live_flags > 0, in_page % page_width, 0)
    return (segment_ids.reshape(-1).astype(jnp.int32), live_flags.reshape(-1), jnp.stack([row_ids.reshape(-1), col_ids.reshape(-1)]).astype(jnp.int32))


def draw_segment(key, part):
    segment_ids, live_flags, positions = page_layout(key)
    return segment_ids


def draw_live_rows(key, part):
    segment_ids, live_flags, positions = page_layout(key)
    return live_flags


def draw_coords(key, part):
    segment_ids, live_flags, positions = page_layout(key)
    return positions


def draw_tokens(key, part):
    key = jax.random.fold_in(key, 5)
    position = jnp.arange(TOKENS, dtype=jnp.float32)[:, None] / TOKENS
    factor = 0.5 + position
    base = jnp.clip(jax.random.normal(key, (TOKENS, D), jnp.float32), -4.0, 4.0)
    return (base * factor).astype(jnp.bfloat16)


def level_of(own_key, dims, cuts, least, top_value):
    level = 1.0
    for dim, shards_of in cuts:
        draws = jax.random.uniform(jax.random.fold_in(jax.random.fold_in(own_key, 6), dim), (shards_of,), jnp.float32, least / len(cuts), top_value / len(cuts))
        level = level * jnp.repeat(jnp.exp(draws), dims[dim] // shards_of).reshape((-1,) + (1,) * (len(dims) - 1 - dim))
    return level


def gaussian(key, extent, scale, bound, shards=(), kind=jnp.bfloat16):
    entries = scale * jax.random.normal(key, extent, jnp.float32)
    if shards:
        entries = entries * level_of(key, extent, shards, -0.22, 0.18)
    return jnp.clip(entries, -bound, bound).astype(kind)


def setup_inputs(seed: int = 0) -> dict:
    seeds = jax.random.split(jax.random.key(seed), 23)
    return {
        "tokens": draw_tokens(jax.random.fold_in(seeds[22], 71), 0),
        "grad_out": gaussian(seeds[1], (TOKENS, D), 1.0, 6.0, ((0, 32),)),
        "segment": draw_segment(jax.random.fold_in(seeds[22], 71), 0),
        "live_rows": draw_live_rows(jax.random.fold_in(seeds[22], 71), 0),
        "coords": draw_coords(jax.random.fold_in(seeds[22], 71), 0),
        "ln1_gain": jnp.clip(1.0 + 0.18 * jax.random.normal(seeds[5], (D,), jnp.float32), 0.099609375, 1.8984375).astype(jnp.bfloat16),
        "ln1_bias": gaussian(seeds[6], (D,), 0.5, 3.0),
        "w_qkv": gaussian(seeds[7], (D, 3 * D), D ** -0.5, 0.21875),
        "b_query": gaussian(seeds[8], (D,), 0.5, 3.0),
        "b_value": gaussian(seeds[9], (D,), 0.5, 3.0),
        "w_out": gaussian(seeds[10], (D, D), (D // 16) ** -0.5, 0.875),
        "b_out": gaussian(seeds[11], (D,), 0.4, 3.0),
        "scale_attn": jnp.clip(jnp.exp(jax.random.uniform(seeds[12], (D,), jnp.float32, math.log(0.5), math.log(2.0))), 0.5, 2.0).astype(jnp.bfloat16),
        "ln2_gain": jnp.clip(1.0 + 0.18 * jax.random.normal(seeds[13], (D,), jnp.float32), 0.099609375, 1.8984375).astype(jnp.bfloat16),
        "ln2_bias": gaussian(seeds[14], (D,), 0.5, 3.0),
        "w_fc1": gaussian(seeds[15], (D, FF), D ** -0.5, 0.21875),
        "b_fc1": gaussian(seeds[16], (FF,), 0.5, 3.0),
        "w_fc2": gaussian(seeds[17], (FF, D), (FF // 4) ** -0.5, 0.21875),
        "b_fc2": gaussian(seeds[18], (D,), 0.4, 3.0),
        "scale_mlp": jnp.clip(jnp.exp(jax.random.uniform(seeds[19], (D,), jnp.float32, math.log(0.5), math.log(2.0))), 0.5, 2.0).astype(jnp.bfloat16),
        "table_rows": gaussian(seeds[20], (H, NREL), 1.0, 4.0),
        "table_cols": gaussian(seeds[21], (H, NREL), 1.0, 4.0),
    }


@jax.custom_vjp
def low(v):
    return lax.optimization_barrier(v.astype(jnp.bfloat16)).astype(jnp.float32)

@jax.custom_vjp
def low_back(v):
    return v

def low_keep(v):
    return (low(v), None)

def low_pass(kept, grad):
    return (grad,)

def back_keep(v):
    return (v, None)

def back_low(kept, grad):
    return (low(grad),)
low.defvjp(low_keep, low_pass)
low_back.defvjp(back_keep, back_low)
HIGH = lax.Precision.HIGHEST
eps = 1e-06

def matmul(left, right):
    return jnp.dot(left, right, precision=HIGH)

def layer_norm(inputs, ln_gain, ln_shift):
    average = lax.optimization_barrier(jnp.mean(inputs, axis=-1, keepdims=True))
    centered = inputs - average
    spread = lax.optimization_barrier(jnp.mean(centered * centered, axis=-1, keepdims=True))
    return centered * lax.rsqrt(spread + eps) * ln_gain + ln_shift

def relative_index(positions):
    offset = jnp.clip(positions[:, None] - positions[None, :], -(RSPAN - 1), RSPAN - 1)
    return offset + (RSPAN - 1)

def group_forward(params, inputs, group_seg, group_live, group_coords):
    ln1_gain, ln1_bias, w_qkv, b_query, b_value, w_out, b_out, scale_attn, ln2_gain, ln2_bias, w_fc1, b_fc1, w_fc2, b_fc2, scale_mlp, table_rows, table_cols = params
    live_col = group_live.astype(jnp.float32)[:, None]
    normed_one = low(layer_norm(inputs, ln1_gain, ln1_bias))
    packed = matmul(normed_one, w_qkv)
    query = low(low_back(packed[:, :D] + b_query))
    keys_all = low(low_back(packed[:, D:2 * D]))
    values_all = low(low_back(packed[:, 2 * D:] + b_value))
    query_heads = query.reshape(GROUP, H, HD)
    key_heads = keys_all.reshape(GROUP, H, HD)
    value_heads = values_all.reshape(GROUP, H, HD)
    rel_bias = table_rows[:, relative_index(group_coords[0])] + table_cols[:, relative_index(group_coords[1])]
    scores = jnp.einsum('qhd,khd->hqk', query_heads, key_heads, precision=HIGH) * HD ** (-0.5) + rel_bias
    scores = low_back(scores)
    allowed = (group_seg[:, None] == group_seg[None, :]) & (group_live[None, :] > 0)
    scores = jnp.where(allowed[None], scores, -1000000000.0)
    weights = low(jax.nn.softmax(scores, axis=-1))
    attended = jnp.einsum('hqk,khd->qhd', weights, value_heads, precision=HIGH).reshape(GROUP, D)
    attended = low(low_back(attended))
    branch_attn = low_back(matmul(attended, w_out) + b_out)
    attn_part = live_col * scale_attn * branch_attn
    stream = inputs + attn_part
    normed_two = low(layer_norm(stream, ln2_gain, ln2_bias))
    hidden_pre = low_back(matmul(normed_two, w_fc1) + b_fc1)
    hidden = low(jax.nn.gelu(hidden_pre, approximate=True))
    branch_mlp = low_back(matmul(hidden, w_fc2) + b_fc2)
    mlp_part = live_col * scale_mlp * branch_mlp
    return (stream + mlp_part, (attn_part, mlp_part))

def reference(tokens, grad_out, segment, live_rows, coords, ln1_gain, ln1_bias, w_qkv, b_query, b_value, w_out, b_out, scale_attn, ln2_gain, ln2_bias, w_fc1, b_fc1, w_fc2, b_fc2, scale_mlp, table_rows, table_cols):
    weights = (ln1_gain.astype(jnp.float32), ln1_bias.astype(jnp.float32), w_qkv.astype(jnp.float32), b_query.astype(jnp.float32), b_value.astype(jnp.float32), w_out.astype(jnp.float32), b_out.astype(jnp.float32), scale_attn.astype(jnp.float32), ln2_gain.astype(jnp.float32), ln2_bias.astype(jnp.float32), w_fc1.astype(jnp.float32), b_fc1.astype(jnp.float32), w_fc2.astype(jnp.float32), b_fc2.astype(jnp.float32), scale_mlp.astype(jnp.float32), table_rows.astype(jnp.float32), table_cols.astype(jnp.float32))
    source = tokens.astype(jnp.float32)
    cotangent = grad_out.astype(jnp.float32)
    start_carry = (jax.tree.map(jnp.zeros_like, weights), jnp.zeros((4,), jnp.float32))

    def one_group(carried, group_index):
        first_row = group_index * GROUP
        group_rows = lax.dynamic_slice_in_dim(source, first_row, GROUP, 0)
        group_cot = lax.dynamic_slice_in_dim(cotangent, first_row, GROUP, 0)
        group_seg = lax.dynamic_slice_in_dim(segment, first_row, GROUP, 0)
        group_live = lax.dynamic_slice_in_dim(live_rows, first_row, GROUP, 0)
        group_coords = lax.dynamic_slice_in_dim(coords, first_row, GROUP, 1)

        def forward(params, inputs):
            return group_forward(params, inputs, group_seg, group_live, group_coords)
        output, pullback, extras = jax.vjp(forward, weights, group_rows, has_aux=True)
        grad_params, grad_inputs = pullback(group_cot)
        attn_part, mlp_part = extras
        live_col = group_live.astype(jnp.float32)[:, None]
        stat_terms = jnp.stack([jnp.sum(live_col * group_rows * group_rows), jnp.sum(attn_part * attn_part), jnp.sum(mlp_part * mlp_part), jnp.sum(live_col)])
        summed = jax.tree.map(jnp.add, carried[0], grad_params)
        return ((summed, carried[1] + stat_terms), (output, grad_inputs))
    (grad_sums, stat_sums), (outputs, grad_inputs) = lax.scan(one_group, start_carry, jnp.arange(N_DP, dtype=jnp.int32))
    out = outputs.reshape(TOKENS, D).astype(jnp.bfloat16)
    grad_tokens = grad_inputs.reshape(TOKENS, D)
    root_means = jnp.sqrt(stat_sums[:3] / (stat_sums[3] * D))
    return (out, grad_tokens, grad_sums[0], grad_sums[1], grad_sums[2], grad_sums[3], grad_sums[4], grad_sums[5], grad_sums[6], grad_sums[7], grad_sums[8], grad_sums[9], grad_sums[10], grad_sums[11], grad_sums[12], grad_sums[13], grad_sums[14], grad_sums[15], grad_sums[16], root_means)
```

```python
import functools

import jax
import jax.numpy as jnp
from jax import lax
from jax.experimental import pallas as pl
from jax.experimental.pallas import tpu as pltpu
from jax.sharding import PartitionSpec as P

MESH = pl.DeviceIdType.MESH
BF16 = jnp.bfloat16
F32 = jnp.float32
EPS = 1e-06
MASKED = -1000000000.0
NT = ((1,), (1,))
TN = ((0,), (0,))
ROW0, COL0, SEG0, LIVE0, LSE0 = 64, 150, 236, 240, 241
VMEM_LIMIT = 62 << 20


def dot(left, right, dims=((1,), (0,))):
    return lax.dot_general(left, right, (dims, ((), ())), preferred_element_type=F32)


def split3(value):
    high = value.astype(BF16).astype(F32)
    rest = value - high
    middle = rest.astype(BF16).astype(F32)
    return high, middle, rest - middle


def lanes(shape):
    return lax.broadcasted_iota(jnp.int32, shape, len(shape) - 1)


def column_of(row):
    return jnp.transpose(jnp.broadcast_to(row, (8, row.shape[1])))[:, :1]


def place():
    me = lax.axis_index("blk")
    return lax.axis_index("dp"), me // 2, me % 2


def greet(peers):
    barrier = pltpu.get_barrier_semaphore()
    for peer in peers:
        pl.semaphore_signal(barrier, inc=1, device_id=peer, device_id_type=MESH)
    pl.semaphore_wait(barrier, len(peers))


def remote(src, dst, sems, index, peer):
    return pltpu.make_async_remote_copy(
        src_ref=src,
        dst_ref=dst,
        send_sem=sems[0].at[index],
        recv_sem=sems[1].at[index],
        device_id=peer,
        device_id_type=MESH,
    )


def at128(index):
    return pl.multiple_of(index, 128)


def forward_kernel(
    tokens, seg, live, coords, vectors, table_rows, table_cols, w_hbm,
    att_out, q_hbm, k_hbm, v_hbm, a_hbm, n_hbm,
    nrm, w_own, meta, squares, base, q_aug, k_aug, v_aug, acc, peak, score, top, att, att_low,
    att_in, rsend, rrecv, lsem,
):
    rows, width = tokens.shape
    heads, head_dim = q_aug.shape[0], 64
    cols = heads * head_dim
    dp, x, c = place()
    sibling = (dp, x * 2 + 1 - c)
    across = (dp, (1 - x) * 2 + c)
    diagonal = (dp, (1 - x) * 2 + 1 - c)
    rsem = (rsend, rrecv)
    loads = [
        pltpu.make_async_copy(
            w_hbm.at[:, pl.ds(at128(part * width + c * cols), cols)], w_own.at[part], lsem.at[part]
        )
        for part in range(3)
    ]
    for load in loads:
        load.start()

    source = tokens[...].astype(F32)
    average = jnp.mean(source, axis=-1, keepdims=True)
    centered = source - average
    spread = jnp.mean(centered * centered, axis=-1, keepdims=True)
    normed = centered * lax.rsqrt(spread + EPS) * vectors[LN1_GAIN : LN1_GAIN + 1, :]
    normed = normed + vectors[LN1_BIAS : LN1_BIAS + 1, :]
    own = pl.ds(pl.multiple_of(c * rows, rows), rows)
    nrm[own] = normed.astype(BF16)
    meta[c] = jnp.concatenate(
        [seg[...], live[...], coords[...], jnp.zeros((4, rows), jnp.int32)], axis=0
    )
    greet([sibling, across, diagonal])
    half = rows // 2
    sends = [
        remote(meta.at[c], meta.at[c], rsem, 0, sibling),
        remote(meta.at[c], meta.at[2 + c], rsem, 1, across),
        remote(meta.at[c], meta.at[2 + c], rsem, 2, diagonal),
        remote(nrm.at[own], nrm.at[own], rsem, 3, sibling),
    ]
    pieces, forwards = [], []
    for i in range(2):
        mine = pl.ds(pl.multiple_of(c * rows + i * half, half), half)
        there = pl.ds(pl.multiple_of((2 + c) * rows + i * half, half), half)
        pieces.append(remote(nrm.at[mine], nrm.at[there], rsem, 4 + i, across))
        forwards.append(remote(nrm.at[there], nrm.at[there], rsem, 6 + i, sibling))
    for copy in sends + pieces:
        copy.start()

    spans = table_rows.shape[1]
    limit = (spans - 1) // 2
    offset = lanes((spans, 256))
    offset = jnp.where(offset < 128, offset, offset - 256)
    entry = lax.broadcasted_iota(jnp.int32, (spans, 256), 0)
    pick = jnp.where(jnp.clip(-offset, -limit, limit) + limit == entry, 1.0, 0.0).astype(BF16)
    base[0] = jnp.pad(dot(table_rows[...], pick), ((0, 4), (0, 0)))
    base[1] = jnp.pad(dot(table_cols[...], pick), ((0, 4), (0, 0)))
    lane = lanes((256, 256))
    line = lax.broadcasted_iota(jnp.int32, (256, 256), 0)
    in_rows = (lane >= ROW0) & (lane < COL0) & (line >= ROW0) & (line < COL0)
    in_cols = (lane >= COL0) & (lane < SEG0) & (line >= COL0) & (line < SEG0)
    keep = (lane == line) & (lane >= SEG0) & (lane <= LIVE0)

    def make_square(h, unused):
        shifted = [
            pltpu.roll(
                jnp.broadcast_to(base[i, pl.ds(c * heads + h, 1), :], (256, 256)),
                0, 1, stride=1, stride_axis=0,
            )
            for i in range(2)
        ]
        square = jnp.where(in_rows, shifted[0], jnp.where(in_cols, shifted[1], 0.0))
        squares[h] = jnp.where(keep, 1.0, square).astype(BF16)
        return unused

    lax.fori_loop(0, heads, make_square, 0)
    for load in loads:
        load.wait()
    own_cols = pl.ds(at128(c * cols), cols)
    query_bias = vectors[B_QUERY : B_QUERY + 1, own_cols]
    value_bias = vectors[B_VALUE : B_VALUE + 1, own_cols]

    low128 = lanes((rows, 128)) < head_dim

    def project(slot, queries):
        here = pl.ds(pl.multiple_of(slot * rows, rows), rows)
        info = jnp.transpose(meta[slot].astype(F32)).astype(jnp.int32)
        page, alive, r, col = (info[:, i : i + 1] for i in range(4))
        spot = lanes((rows, 256))
        hot = (spot == r + ROW0) | (spot == col + COL0)
        key_side = jnp.where(hot | ((spot >= LSE0) & (spot < LSE0 + 3)), 1.0, 0.0)
        other = (spot >= SEG0) & (spot < LIVE0) & (spot != page + SEG0)
        dead = (spot == LIVE0) & (alive <= 0)
        key_side = jnp.where(other | dead, MASKED, key_side)
        if queries:
            query_side = jnp.where(hot | (spot == page + SEG0) | (spot == LIVE0), 1.0, 0.0)
            query_side = query_side.astype(BF16)
        inputs = nrm[here]
        ones = jnp.where((spot[:, :128] >= 64) & (spot[:, :128] < 67), 1.0, 0.0)
        keys = dot(inputs, w_own[1])
        values = dot(inputs, w_own[2]) + value_bias
        if queries:
            query = (dot(inputs, w_own[0]) + query_bias) * head_dim ** (-0.5)
        for h in range(heads):
            tile = slice(h // 2 * 128, h // 2 * 128 + 128)
            turn = (lambda v: v) if h % 2 == 0 else (lambda v: pltpu.roll(v, 64, 1))
            k_aug[h, here, :128] = jnp.where(low128, turn(keys[:, tile]), key_side[:, :128]).astype(BF16)
            k_aug[h, here, 128:] = key_side[:, 128:].astype(BF16)
            v_aug[h, here, :] = jnp.where(low128, turn(values[:, tile]), ones).astype(BF16)
            if queries:
                extra = dot(query_side, squares[h])
                q_aug[h, here, :128] = jnp.where(low128, turn(query[:, tile]), extra[:, :128]).astype(BF16)
                q_aug[h, here, 128:] = extra[:, 128:].astype(BF16)

    project(c, True)
    for i in (0, 3):
        sends[i].wait_recv()
    project(1 - c, True)

    block = rows

    def score_of(h, qb, part, buf):
        s = dot(
            q_aug[h, qb * block : (qb + 1) * block, :],
            k_aug[h, part * 2 * rows : (part + 1) * 2 * rows, :],
            NT,
        )
        score[buf] = s
        top[buf] = jnp.broadcast_to(jnp.max(s, axis=1, keepdims=True), (block, 128))

    def weigh(h, qb, part, buf):
        here = slice(qb * block, (qb + 1) * block)
        m = top[buf][:, :1]
        if part:
            before = peak[h, here, :][:, :1]
            m = jnp.maximum(before, m)
        p = jnp.exp(score[buf] - m).astype(BF16)
        pv = dot(p, v_aug[h, part * 2 * rows : (part + 1) * 2 * rows, :])
        if not part:
            acc[h, here, :] = pv
            peak[h, here, :] = jnp.broadcast_to(m, (block, 128))
            return
        pv = pv + acc[h, here, :] * jnp.exp(before - m)
        total = pv[:, 64:65]
        slot_live = column_of(meta[qb, 1:2, :].astype(F32))
        lse = jnp.where(slot_live > 0, m + jnp.log(total), 0.0)
        spot = lanes((block, 128))
        value = pv / total
        a = split3(lse)
        tail = q_aug[h, here, 128:].astype(F32)
        for i in range(3):
            tail = jnp.where(spot == LSE0 - 128 + i, -a[i], tail)
        q_aug[h, here, 128:] = tail.astype(BF16)
        return value

    def sweep(part, t, unused):
        order = [(0, 0), (0, 1), (1, 0), (1, 1)]
        for i, (odd, qb) in enumerate(order):
            if i < 3:
                score_of(2 * t + order[i + 1][0], order[i + 1][1], part, (i + 1) % 2)
            else:
                score_of(jnp.minimum(2 * t + 2, heads - 2), 0, part, 0)
            value = weigh(2 * t + odd, qb, part, i % 2)
            if part:
                here = slice(qb * block, (qb + 1) * block)
                if odd:
                    value = jnp.where(low128, att[t, here, :], pltpu.roll(value, 64, 1))
                att[t, here, :] = value
                if odd:
                    att_low[t, here, :] = value.astype(BF16)
        if not part:

            @pl.when(t == 1)
            def _():
                pieces[0].wait_recv()
                forwards[0].start()

        return unused

    score_of(0, 0, 0, 0)
    lax.fori_loop(0, heads // 2, functools.partial(sweep, 0), 0)
    pieces[1].wait_recv()
    forwards[1].start()
    sends[1].wait_recv()
    sends[2].wait_recv()
    project(2 + c, False)
    for copy in forwards:
        copy.wait_recv()
    project(3 - c, False)
    stores = [
        pltpu.make_async_copy(k_aug, k_hbm, lsem.at[3]),
        pltpu.make_async_copy(v_aug, v_hbm, lsem.at[4]),
        pltpu.make_async_copy(nrm, n_hbm, lsem.at[5]),
    ]
    for store in stores:
        store.start()
    score_of(0, 0, 1, 0)
    lax.fori_loop(0, heads // 2, functools.partial(sweep, 1), 0)
    stores += [
        pltpu.make_async_copy(q_aug, q_hbm, lsem.at[6]),
        pltpu.make_async_copy(att, a_hbm, lsem.at[7]),
    ]
    for store in stores[3:]:
        store.start()
    theirs = pl.ds(pl.multiple_of((1 - c) * rows, rows), rows)
    swap = remote(att_low.at[:, theirs, :], att_in, rsem, 8, sibling)
    swap.start()
    tiles = heads // 2
    for t in range(tiles):
        att_out[:, pl.ds(at128((c * tiles + t) * 128), 128)] = att_low[t, own, :]
    swap.wait_recv()
    for t in range(tiles):
        att_out[:, pl.ds(at128(((1 - c) * tiles + t) * 128), 128)] = att_in[t]
    for copy in sends + pieces + forwards + [swap]:
        copy.wait_send()
    for store in stores:
        store.wait()


def forward_attention(tokens, seg, live, coords, vectors, t_rows, t_cols, w_qkv):
    rows, width = tokens.shape
    heads = t_rows.shape[0] // 2
    group = rows * 4
    any_spec = pl.BlockSpec(memory_space=pl.ANY)
    vmem = pl.BlockSpec(memory_space=pltpu.VMEM)
    return pl.pallas_call(
        forward_kernel,
        out_shape=[
            jax.ShapeDtypeStruct((rows, width), BF16),
            jax.ShapeDtypeStruct((heads, 2 * rows, 256), BF16),
            jax.ShapeDtypeStruct((heads, group, 256), BF16),
            jax.ShapeDtypeStruct((heads, group, 128), BF16),
            jax.ShapeDtypeStruct((heads // 2, 2 * rows, 128), F32),
            jax.ShapeDtypeStruct((group, width), BF16),
        ],
        in_specs=[vmem] * 7 + [any_spec],
        out_specs=[vmem] + [any_spec] * 5,
        scratch_shapes=[
            pltpu.VMEM((group, width), BF16),
            pltpu.VMEM((3, width, heads * 64), BF16),
            pltpu.VMEM((4, 8, rows), jnp.int32),
            pltpu.VMEM((heads, 256, 256), BF16),
            pltpu.VMEM((2, 16, 256), F32),
            pltpu.VMEM((heads, 2 * rows, 256), BF16),
            pltpu.VMEM((heads, group, 256), BF16),
            pltpu.VMEM((heads, group, 128), BF16),
            pltpu.VMEM((heads, 2 * rows, 128), F32),
            pltpu.VMEM((heads, 2 * rows, 128), F32),
            pltpu.VMEM((2, rows, 2 * rows), F32),
            pltpu.VMEM((2, rows, 128), F32),
            pltpu.VMEM((heads // 2, 2 * rows, 128), F32),
            pltpu.VMEM((heads // 2, 2 * rows, 128), BF16),
            pltpu.VMEM((heads // 2, rows, 128), BF16),
            pltpu.SemaphoreType.DMA((9,)),
            pltpu.SemaphoreType.DMA((9,)),
            pltpu.SemaphoreType.DMA((8,)),
        ],
        compiler_params=pltpu.CompilerParams(
            collective_id=0, has_side_effects=True, vmem_limit_bytes=VMEM_LIMIT
        ),
        name="attention_forward",
    )(tokens, seg, live, coords, vectors, t_rows, t_cols, w_qkv)


(LN1_GAIN, LN1_BIAS, B_QUERY, B_VALUE, B_OUT, SCALE_ATTN, LN2_GAIN, LN2_BIAS, B_FC2, SCALE_MLP, B_FC1) = range(11)
GELU_A, GELU_B = 0.7978845608, 0.044715


def norm_stats(values):
    average = jnp.mean(values, axis=-1, keepdims=True)
    centered = values - average
    scale = lax.rsqrt(jnp.mean(centered * centered, axis=-1, keepdims=True) + EPS)
    return centered * scale, scale


def norm_back(grad, hat, scale, gain):
    e = grad * gain
    return scale * (
        e
        - jnp.mean(e, axis=-1, keepdims=True)
        - hat * jnp.mean(e * hat, axis=-1, keepdims=True)
    )


def dense_kernel(
    att, tokens, grad_out, live, vectors, w_out, w_fc1, w_fc2,
    out, g_stream_out, g_att, gw_out, gw_fc1, gw_fc2, sums,
    branch_attn, stream_s, normed_s, g_mlp_s, branch_mlp, g_normed,
):
    j = pl.program_id(0)
    row = lambda i: vectors[i : i + 1, :]
    live_col = column_of(live[...].astype(F32))

    @pl.when(j == 0)
    def _():
        source = tokens[...].astype(F32)
        branch = dot(att[...], w_out[...]) + row(B_OUT)
        branch_attn[...] = branch
        part = live_col * row(SCALE_ATTN) * branch
        stream = source + part
        stream_s[...] = stream
        hat, unused = norm_stats(stream)
        normed_s[...] = (hat * row(LN2_GAIN) + row(LN2_BIAS)).astype(BF16)
        g_mlp = (grad_out[...].astype(F32) * (live_col * row(SCALE_MLP))).astype(BF16)
        g_mlp_s[...] = g_mlp
        sums[...] = jnp.zeros_like(sums)
        sums[4:5, :] = jnp.sum(g_mlp.astype(F32), axis=0, keepdims=True)
        sums[10:11, :] = jnp.sum(live_col * source * source, axis=0, keepdims=True)
        sums[11:12, :] = jnp.sum(part * part, axis=0, keepdims=True)
        sums[13:14, :] = jnp.broadcast_to(jnp.sum(live_col, axis=0, keepdims=True), (1, part.shape[1]))
        branch_mlp[...] = jnp.zeros_like(branch_mlp)
        g_normed[...] = jnp.zeros_like(g_normed)

    u = dot(normed_s[...], w_fc1[...]) + vectors[pl.ds(B_FC1 + j, 1), :]
    square = u * u
    t = jnp.tanh(GELU_A * u * (1.0 + GELU_B * square))
    hidden = (0.5 * u * (1.0 + t)).astype(BF16)
    slope = 0.5 * (1.0 + t) + 0.5 * u * (1.0 - t * t) * (GELU_A + (3.0 * GELU_A * GELU_B) * square)
    branch_mlp[...] += dot(hidden, w_fc2[...])
    g_mlp = g_mlp_s[...]
    g_pre = (dot(g_mlp, w_fc2[...], NT) * slope).astype(BF16)
    sums[pl.ds(6 + j, 1), :] = jnp.sum(g_pre.astype(F32), axis=0, keepdims=True)
    gw_fc2[...] = dot(hidden, g_mlp, TN).astype(BF16)
    gw_fc1[0] = dot(normed_s[...], g_pre, TN).astype(BF16)
    g_normed[...] += dot(g_pre, w_fc1[...], NT)

    @pl.when(j == pl.num_programs(0) - 1)
    def _():
        grad = grad_out[...].astype(F32)
        branch = branch_mlp[...] + row(B_FC2)
        part = live_col * row(SCALE_MLP) * branch
        stream = stream_s[...]
        out[...] = (stream + part).astype(BF16)
        sums[12:13, :] = jnp.sum(part * part, axis=0, keepdims=True)
        sums[5:6, :] = jnp.sum(grad * live_col * branch, axis=0, keepdims=True)
        hat, scale = norm_stats(stream)
        g_n2 = g_normed[...]
        sums[2:3, :] = jnp.sum(g_n2 * hat, axis=0, keepdims=True)
        sums[3:4, :] = jnp.sum(g_n2, axis=0, keepdims=True)
        g_stream = grad + norm_back(g_n2, hat, scale, row(LN2_GAIN))
        g_stream_out[...] = g_stream
        gated = g_stream * live_col
        g_attn = (gated * row(SCALE_ATTN)).astype(BF16)
        sums[1:2, :] = jnp.sum(gated * branch_attn[...], axis=0, keepdims=True)
        sums[0:1, :] = jnp.sum(g_attn.astype(F32), axis=0, keepdims=True)
        gw_out[...] = dot(att[...], g_attn, TN).astype(BF16)
        g_att[...] = dot(g_attn, w_out[...], NT).astype(BF16)


def dense_layer(att, tokens, grad_out, live, vectors, w_out, w_fc1, w_fc2):
    rows, width = tokens.shape
    hidden = w_fc1.shape[1]
    steps = hidden // width
    whole = lambda *shape: pl.BlockSpec(shape, lambda j: (0,) * len(shape))
    return pl.pallas_call(
        dense_kernel,
        grid=(steps,),
        out_shape=[
            jax.ShapeDtypeStruct((rows, width), BF16),
            jax.ShapeDtypeStruct((rows, width), F32),
            jax.ShapeDtypeStruct((rows, width), BF16),
            jax.ShapeDtypeStruct((width, width), BF16),
            jax.ShapeDtypeStruct((steps, width, width), BF16),
            jax.ShapeDtypeStruct((hidden, width), BF16),
            jax.ShapeDtypeStruct((16, width), F32),
        ],
        in_specs=[
            whole(rows, width),
            whole(rows, width),
            whole(rows, width),
            whole(1, rows),
            whole(*vectors.shape),
            whole(width, width),
            pl.BlockSpec((width, width), lambda j: (0, j)),
            pl.BlockSpec((width, width), lambda j: (j, 0)),
        ],
        out_specs=[
            whole(rows, width),
            whole(rows, width),
            whole(rows, width),
            whole(width, width),
            pl.BlockSpec((1, width, width), lambda j: (j, 0, 0)),
            pl.BlockSpec((width, width), lambda j: (j, 0)),
            whole(16, width),
        ],
        scratch_shapes=[
            pltpu.VMEM((rows, width), F32),
            pltpu.VMEM((rows, width), F32),
            pltpu.VMEM((rows, width), BF16),
            pltpu.VMEM((rows, width), BF16),
            pltpu.VMEM((rows, width), F32),
            pltpu.VMEM((rows, width), F32),
        ],
        compiler_params=pltpu.CompilerParams(vmem_limit_bytes=VMEM_LIMIT),
        name="dense_layer",
    )(att, tokens, grad_out, live, vectors, w_out, w_fc1, w_fc2)


def backward_kernel(
    g_att, tokens, g_stream, vectors, q_hbm, k_hbm, v_hbm, a_hbm, n_hbm, w_hbm,
    g_tokens, gw, sums,
    q_aug, k_aug, v_aug, att, nrm, w_own, g_rows, g_aug, q_turn, g_turn, d_query, d_key, d_value,
    dq, dkv, half_out, half_in, across_in, gw_acc,
    rsend, rrecv, lsem,
):
    rows, width = g_att.shape
    heads, head_dim = q_aug.shape[0], 64
    cols = heads * head_dim
    dp, x, c = place()
    sibling = (dp, x * 2 + 1 - c)
    across = (dp, (1 - x) * 2 + c)
    rsem = (rsend, rrecv)
    span = 2 * rows

    loads = {}
    for h in range(heads):
        loads["q", h] = pltpu.make_async_copy(q_hbm.at[h], q_aug.at[h], lsem.at[h])
        loads["k", h] = pltpu.make_async_copy(k_hbm.at[h], k_aug.at[h], lsem.at[heads + h])
        loads["v", h] = pltpu.make_async_copy(v_hbm.at[h], v_aug.at[h], lsem.at[2 * heads + h])
    loads["a"] = pltpu.make_async_copy(a_hbm, att, lsem.at[3 * heads])
    loads["n"] = pltpu.make_async_copy(n_hbm, nrm, lsem.at[3 * heads + 1])
    for part in range(3):
        loads["w", part] = pltpu.make_async_copy(
            w_hbm.at[:, pl.ds(at128(part * width + c * cols), cols)], w_own.at[part],
            lsem.at[3 * heads + 2 + part],
        )
    loads["a"].start()
    for h in range(heads):
        for kind in "qkv":
            loads[kind, h].start()
    for part in range(3):
        loads["w", part].start()
    loads["n"].start()

    own = pl.ds(pl.multiple_of(c * rows, rows), rows)
    other = pl.ds(pl.multiple_of((1 - c) * rows, rows), rows)
    greet([sibling, across])
    swap = remote(
        g_att.at[:, pl.ds(at128((1 - c) * cols), cols)], g_rows.at[own], rsem, 0, sibling
    )
    swap.start()
    g_rows[own] = g_att[:, pl.ds(at128(c * cols), cols)]
    d_query[...] = jnp.zeros_like(d_query)
    loads["a"].wait()
    swap.wait_recv()

    spot = lanes((span, 128))
    low = spot < head_dim
    for t in range(heads // 2):
        g = g_rows[:, t * 128 : (t + 1) * 128].astype(F32)
        product = g * att[t]
        for odd in range(2):
            h = 2 * t + odd
            delta = jnp.sum(jnp.where(low if odd == 0 else ~low, product, 0.0), axis=1, keepdims=True)
            tile = g if odd == 0 else pltpu.roll(g, 64, 1)
            tile = jnp.where(low, tile, 0.0)
            for i, piece in enumerate(split3(delta)):
                tile = jnp.where(spot == 64 + i, -piece, tile)
            tile = tile.astype(BF16)
            g_aug[h] = tile
            g_turn[h] = jnp.transpose(tile)
    for h in range(heads):
        for kind in "qkv":
            loads[kind, h].wait()
        q_turn[h] = jnp.transpose(q_aug[h])

    block = rows
    step = rows

    def pair(it, unused):
        part = 1 - it // (heads // 2)
        t = it % (heads // 2)
        for odd in range(2):
            h = 2 * t + odd
            for qb in range(span // block):
                here = slice(qb * block, (qb + 1) * block)
                total = d_query[h, :, here]
                for kb in range(span // step):
                    there = slice(kb * step, (kb + 1) * step)
                    source = pl.ds(pl.multiple_of(part * span + kb * step, step), step)
                    keys = k_aug[h, source, :]
                    p = jnp.exp(dot(keys, q_turn[h, :, here]))
                    p_low = p.astype(BF16)
                    ds = (p * dot(v_aug[h, source, :], g_turn[h, :, here])).astype(BF16)
                    gain_value = dot(p_low, g_aug[h, here, :])
                    gain_key = dot(ds, q_aug[h, here, :128])
                    if qb == 0:
                        d_value[odd, there, :] = gain_value
                        d_key[odd, there, :] = gain_key
                    else:
                        d_value[odd, there, :] += gain_value
                        d_key[odd, there, :] += gain_key
                    total = total + dot(keys, ds, TN)
                d_query[h, :, here] = total
        place_k = pl.ds(at128(t * 128), 128)
        place_v = pl.ds(at128(cols + t * 128), 128)
        dkv[part, :, place_k] = jnp.where(low, d_key[0], pltpu.roll(d_key[1], 64, 1)).astype(BF16)
        dkv[part, :, place_v] = jnp.where(low, d_value[0], pltpu.roll(d_value[1], 64, 1)).astype(BF16)

        @pl.when(part == 0)
        def _():
            both = jnp.concatenate([d_query[2 * t, :head_dim, :], d_query[2 * t + 1, :head_dim, :]], axis=0)
            dq[:, place_k] = (jnp.transpose(both) * head_dim ** (-0.5)).astype(BF16)

        return unused

    def through_keys(part, where):
        return dot(dkv[part, where, :cols], w_own[1], NT) + dot(dkv[part, where, cols:], w_own[2], NT)

    lax.fori_loop(0, heads // 2, pair, 0)
    for part in range(3):
        loads["w", part].wait()
    loads["n"].wait()
    half_out[0] = through_keys(1, other).astype(BF16)
    give = remote(half_out.at[0], half_in.at[0], rsem, 1, sibling)
    give.start()
    gw_acc[...] = dot(nrm[span:], dkv[1], TN)
    mine = through_keys(1, own)
    give.wait()
    half_out[0] = (mine + half_in[0].astype(F32)).astype(BF16)
    cross = remote(half_out.at[0], across_in, rsem, 2, across)
    cross.start()
    lax.fori_loop(heads // 2, heads, pair, 0)

    def through(where):
        return dot(dq[where, :], w_own[0], NT) + through_keys(0, where)

    half_out[1] = through(other).astype(BF16)
    give_local = remote(half_out.at[1], half_in.at[1], rsem, 3, sibling)
    give_local.start()
    gw[:, cols:] = (gw_acc[...] + dot(nrm[:span], dkv[0], TN)).astype(BF16)
    gw[:, :cols] = dot(nrm[:span], dq[...], TN).astype(BF16)
    sums[...] = jnp.zeros_like(sums)
    own_cols = pl.ds(at128(c * cols), cols)
    sums[2:3, own_cols] = jnp.sum(dq[...].astype(F32), axis=0, keepdims=True)
    sums[3:4, own_cols] = jnp.sum(
        dkv[0, :, cols:].astype(F32) + dkv[1, :, cols:].astype(F32), axis=0, keepdims=True
    )
    lane = lanes((256, 256))
    line = lax.broadcasted_iota(jnp.int32, (256, 256), 0)
    in_rows = (lane >= ROW0) & (lane < COL0) & (line >= ROW0) & (line < COL0)
    in_cols = (lane >= COL0) & (lane < SEG0) & (line >= COL0) & (line < SEG0)
    flip = jnp.where(lane + line == 255, 1.0, 0.0).astype(BF16)
    for h in range(heads):
        square = dot(d_query[h].astype(BF16), k_aug[h, :span, :])
        for table, mask in enumerate((in_rows, in_cols)):
            flipped = sum(dot(flip, piece.astype(BF16)) for piece in split3(jnp.where(mask, square, 0.0)))
            turned = pltpu.roll(flipped, 0, 1, stride=1, stride_axis=0)
            sums[pl.ds(4 + table * 4 + c * 2 + h // 3, 1), h % 3 * 256 : h % 3 * 256 + 256] = jnp.sum(
                turned, axis=0, keepdims=True
            )
    g_n1 = through(own)
    give_local.wait_recv()
    cross.wait_recv()
    g_n1 = g_n1 + half_in[1].astype(F32) + across_in[...].astype(F32)
    hat, scale = norm_stats(tokens[...].astype(F32))
    sums[0:1, :] = jnp.sum(g_n1 * hat, axis=0, keepdims=True)
    sums[1:2, :] = jnp.sum(g_n1, axis=0, keepdims=True)
    g_tokens[...] = g_stream[...] + norm_back(g_n1, hat, scale, vectors[LN1_GAIN : LN1_GAIN + 1, :])
    for copy in (swap, cross, give_local):
        copy.wait_send()


def backward_attention(g_att, tokens, g_stream, vectors, q_aug, k_aug, v_aug, att, nrm, w_qkv):
    rows, width = tokens.shape
    heads = q_aug.shape[0]
    cols = heads * 64
    span, group = 2 * rows, 4 * rows
    any_spec = pl.BlockSpec(memory_space=pl.ANY)
    vmem = pl.BlockSpec(memory_space=pltpu.VMEM)
    return pl.pallas_call(
        backward_kernel,
        out_shape=[
            jax.ShapeDtypeStruct((rows, width), F32),
            jax.ShapeDtypeStruct((width, 3 * cols), BF16),
            jax.ShapeDtypeStruct((16, width), F32),
        ],
        in_specs=[vmem] * 4 + [any_spec] * 6,
        out_specs=[vmem] * 3,
        scratch_shapes=[
            pltpu.VMEM((heads, span, 256), BF16),
            pltpu.VMEM((heads, group, 256), BF16),
            pltpu.VMEM((heads, group, 128), BF16),
            pltpu.VMEM((heads // 2, span, 128), F32),
            pltpu.VMEM((group, width), BF16),
            pltpu.VMEM((3, width, cols), BF16),
            pltpu.VMEM((span, cols), BF16),
            pltpu.VMEM((heads, span, 128), BF16),
            pltpu.VMEM((heads, 256, span), BF16),
            pltpu.VMEM((heads, 128, span), BF16),
            pltpu.VMEM((heads, 256, span), F32),
            pltpu.VMEM((2, span, 128), F32),
            pltpu.VMEM((2, span, 128), F32),
            pltpu.VMEM((span, cols), BF16),
            pltpu.VMEM((2, span, 2 * cols), BF16),
            pltpu.VMEM((2, rows, width), BF16),
            pltpu.VMEM((2, rows, width), BF16),
            pltpu.VMEM((rows, width), BF16),
            pltpu.VMEM((width, 2 * cols), F32),
            pltpu.SemaphoreType.DMA((4,)),
            pltpu.SemaphoreType.DMA((4,)),
            pltpu.SemaphoreType.DMA((3 * heads + 5,)),
        ],
        compiler_params=pltpu.CompilerParams(
            collective_id=1, has_side_effects=True, vmem_limit_bytes=VMEM_LIMIT
        ),
        name="attention_backward",
    )(g_att, tokens, g_stream, vectors, q_aug, k_aug, v_aug, att, nrm, w_qkv)


def body(
    tokens, grad_out, segment, live_rows, coords, ln1_gain, ln1_bias, w_qkv, b_query, b_value, w_out,
    b_out, scale_attn, ln2_gain, ln2_bias, w_fc1, b_fc1, w_fc2, b_fc2, scale_mlp, table_rows, table_cols,
):
    rows, width = tokens.shape
    heads = table_rows.shape[0] // 2
    cols = heads * 64
    line = lambda v: v.reshape(1, -1)
    live = line(live_rows)
    vectors = jnp.concatenate(
        [
            line(v)
            for v in (ln1_gain, ln1_bias, b_query, b_value, b_out, scale_attn, ln2_gain, ln2_bias, b_fc2, scale_mlp)
        ]
        + [b_fc1.reshape(-1, width)],
        axis=0,
    ).astype(F32)
    att_low, q_aug, k_aug, v_aug, att, nrm = forward_attention(
        tokens, line(segment), live, coords, vectors, table_rows, table_cols, w_qkv
    )
    out, g_stream, g_att, gw_out, gw_fc1, gw_fc2, early = dense_layer(
        att_low, tokens, grad_out, live, vectors, w_out, w_fc1, w_fc2
    )
    n_dp = lax.axis_size("dp")
    mlp = jnp.concatenate(
        [
            gw_fc1.reshape(-1, n_dp, width // n_dp, width).transpose(1, 0, 2, 3).reshape(n_dp, -1, width),
            gw_fc2.reshape(n_dp, -1, width),
            gw_out.reshape(n_dp, -1, width),
        ],
        axis=1,
    )
    mlp = lax.psum(lax.psum_scatter(mlp, "dp", scatter_dimension=0, tiled=True), "blk")[0].astype(F32)
    g_tokens, gw, late = backward_attention(
        g_att, tokens, g_stream, vectors, q_aug, k_aug, v_aug, att, nrm, w_qkv
    )
    c = lax.axis_index("blk") % 2
    spread = jnp.zeros((width, 3, 2, cols), BF16)
    spread = lax.dynamic_update_slice(spread, gw.reshape(width, 3, 1, cols), (0, 0, c, 0))
    sum_qkv = lax.psum(
        lax.psum_scatter(spread.reshape(width, -1), "dp", scatter_dimension=0, tiled=True), "blk"
    ).astype(F32)
    early, late = lax.psum((early, late), ("dp", "blk"))
    totals = jnp.sum(early[10:13], axis=1)
    root_means = jnp.sqrt(totals / (early[13, 0] * width))
    spans = table_rows.shape[1]
    limit = (spans - 1) // 2
    offset = jnp.arange(1, 257)
    offset = jnp.where(offset < 128, offset, offset - 256)
    pick = (jnp.clip(offset, -limit, limit)[:, None] + limit == jnp.arange(spans)[None, :]).astype(F32)
    tables = jnp.dot(late[4:12].reshape(-1, 256), pick, precision=lax.Precision.HIGHEST)
    part = width // n_dp
    fc1_rows = gw_fc1.shape[0] * part
    sum_fc1 = mlp[:fc1_rows].reshape(-1, part, width).transpose(1, 0, 2).reshape(part, -1)
    fc2_rows = gw_fc2.shape[0] // n_dp
    sum_fc2 = mlp[fc1_rows : fc1_rows + fc2_rows]
    sum_out = mlp[fc1_rows + fc2_rows :]
    return (
        out, g_tokens, late[0], late[1], sum_qkv, late[2], late[3], sum_out, early[0], early[1], early[2],
        early[3], sum_fc1, early[6:10].reshape(-1), sum_fc2, early[4], early[5],
        tables[: 2 * heads], tables[2 * heads :], root_means,
    )


def solution(mesh):
    rows = P(("dp", "blk"), None)
    flat = P(("dp", "blk"))
    return jax.shard_map(
        body,
        mesh=mesh,
        in_specs=(rows, rows, flat, flat, P(None, ("dp", "blk"))) + (P(),) * 17,
        out_specs=(
            rows, rows, P(), P(), P("dp", None), P(), P(), P("dp", None), P(), P(), P(), P(),
            P("dp", None), P(), P("dp", None), P(), P(), P(), P(), P(),
        ),
        check_vma=False,
    )
```

```python
import functools

import jax
import jax.numpy as jnp
from jax import lax
from jax.experimental import pallas as pl
from jax.experimental.pallas import tpu as pltpu
from jax.sharding import PartitionSpec as P

MESH = pl.DeviceIdType.MESH
BF16 = jnp.bfloat16
F32 = jnp.float32
EPS = 1e-06
MASKED = -1000000000.0
NT = ((1,), (1,))
TN = ((0,), (0,))
ROW0, COL0, SEG0, LIVE0, LSE0 = 64, 150, 236, 240, 241
VMEM_LIMIT = 62 << 20
(LN1_GAIN, LN1_BIAS, B_QUERY, B_VALUE, B_OUT, SCALE_ATTN, LN2_GAIN, LN2_BIAS, B_FC2, SCALE_MLP, B_FC1) = range(11)
GELU_A, GELU_B = 0.7978845608, 0.044715


def dot(left, right, dims=((1,), (0,))):
    return lax.dot_general(left, right, (dims, ((), ())), preferred_element_type=F32)


def split3(value):
    high = value.astype(BF16).astype(F32)
    rest = value - high
    middle = rest.astype(BF16).astype(F32)
    return high, middle, rest - middle


def lanes(shape):
    return lax.broadcasted_iota(jnp.int32, shape, len(shape) - 1)


def column_of(row):
    return jnp.transpose(jnp.broadcast_to(row, (8, row.shape[1])))[:, :1]


def place():
    me = lax.axis_index("blk")
    return lax.axis_index("dp"), me // 2, me % 2


def greet(peers):
    barrier = pltpu.get_barrier_semaphore()
    for peer in peers:
        pl.semaphore_signal(barrier, inc=1, device_id=peer, device_id_type=MESH)
    pl.semaphore_wait(barrier, len(peers))


def remote(src, dst, sems, index, peer):
    return pltpu.make_async_remote_copy(
        src_ref=src,
        dst_ref=dst,
        send_sem=sems[0].at[index],
        recv_sem=sems[1].at[index],
        device_id=peer,
        device_id_type=MESH,
    )


def at128(index):
    return pl.multiple_of(index, 128)


def forward_kernel(
    tokens, seg, live, coords, vectors, table_rows, table_cols, w_hbm,
    att_out, q_hbm, k_hbm, v_hbm, a_hbm, n_hbm,
    nrm, w_own, meta, squares, base, q_aug, k_aug, v_aug, acc, peak, score, top, att, att_low,
    att_in, rsend, rrecv, lsem,
):
    rows, width = tokens.shape
    heads, head_dim = q_aug.shape[0], 64
    cols = heads * head_dim
    dp, x, c = place()
    sibling = (dp, x * 2 + 1 - c)
    across = (dp, (1 - x) * 2 + c)
    diagonal = (dp, (1 - x) * 2 + 1 - c)
    rsem = (rsend, rrecv)
    loads = [
        pltpu.make_async_copy(
            w_hbm.at[:, pl.ds(at128(part * width + c * cols), cols)], w_own.at[part], lsem.at[part]
        )
        for part in range(3)
    ]
    for load in loads:
        load.start()

    source = tokens[...].astype(F32)
    average = jnp.mean(source, axis=-1, keepdims=True)
    centered = source - average
    spread = jnp.mean(centered * centered, axis=-1, keepdims=True)
    normed = centered * lax.rsqrt(spread + EPS) * vectors[LN1_GAIN : LN1_GAIN + 1, :]
    normed = normed + vectors[LN1_BIAS : LN1_BIAS + 1, :]
    own = pl.ds(pl.multiple_of(c * rows, rows), rows)
    nrm[own] = normed.astype(BF16)
    meta[c] = jnp.concatenate(
        [seg[...], live[...], coords[...], jnp.zeros((4, rows), jnp.int32)], axis=0
    )
    greet([sibling, across, diagonal])
    half = rows // 2
    sends = [
        remote(meta.at[c], meta.at[c], rsem, 0, sibling),
        remote(meta.at[c], meta.at[2 + c], rsem, 1, across),
        remote(meta.at[c], meta.at[2 + c], rsem, 2, diagonal),
        remote(nrm.at[own], nrm.at[own], rsem, 3, sibling),
    ]
    pieces, forwards = [], []
    for i in range(2):
        mine = pl.ds(pl.multiple_of(c * rows + i * half, half), half)
        there = pl.ds(pl.multiple_of((2 + c) * rows + i * half, half), half)
        pieces.append(remote(nrm.at[mine], nrm.at[there], rsem, 4 + i, across))
        forwards.append(remote(nrm.at[there], nrm.at[there], rsem, 6 + i, sibling))
    for copy in sends + pieces:
        copy.start()

    spans = table_rows.shape[1]
    limit = (spans - 1) // 2
    offset = lanes((spans, 256))
    offset = jnp.where(offset < 128, offset, offset - 256)
    entry = lax.broadcasted_iota(jnp.int32, (spans, 256), 0)
    pick = jnp.where(jnp.clip(-offset, -limit, limit) + limit == entry, 1.0, 0.0).astype(BF16)
    base[0] = jnp.pad(dot(table_rows[...], pick), ((0, 4), (0, 0)))
    base[1] = jnp.pad(dot(table_cols[...], pick), ((0, 4), (0, 0)))
    lane = lanes((256, 256))
    line = lax.broadcasted_iota(jnp.int32, (256, 256), 0)
    in_rows = (lane >= ROW0) & (lane < COL0) & (line >= ROW0) & (line < COL0)
    in_cols = (lane >= COL0) & (lane < SEG0) & (line >= COL0) & (line < SEG0)
    keep = (lane == line) & (lane >= SEG0) & (lane <= LIVE0)

    def make_square(h, unused):
        shifted = [
            pltpu.roll(
                jnp.broadcast_to(base[i, pl.ds(c * heads + h, 1), :], (256, 256)),
                0, 1, stride=1, stride_axis=0,
            )
            for i in range(2)
        ]
        square = jnp.where(in_rows, shifted[0], jnp.where(in_cols, shifted[1], 0.0))
        squares[h] = jnp.where(keep, 1.0, square).astype(BF16)
        return unused

    lax.fori_loop(0, heads, make_square, 0)
    for load in loads:
        load.wait()
    own_cols = pl.ds(at128(c * cols), cols)
    query_bias = vectors[B_QUERY : B_QUERY + 1, own_cols]
    value_bias = vectors[B_VALUE : B_VALUE + 1, own_cols]

    low128 = lanes((rows, 128)) < head_dim

    def project(slot, queries):
        here = pl.ds(pl.multiple_of(slot * rows, rows), rows)
        info = jnp.transpose(meta[slot].astype(F32)).astype(jnp.int32)
        page, alive, r, col = (info[:, i : i + 1] for i in range(4))
        spot = lanes((rows, 256))
        hot = (spot == r + ROW0) | (spot == col + COL0)
        key_side = jnp.where(hot | ((spot >= LSE0) & (spot < LSE0 + 3)), 1.0, 0.0)
        other = (spot >= SEG0) & (spot < LIVE0) & (spot != page + SEG0)
        dead = (spot == LIVE0) & (alive <= 0)
        key_side = jnp.where(other | dead, MASKED, key_side)
        if queries:
            query_side = jnp.where(hot | (spot == page + SEG0) | (spot == LIVE0), 1.0, 0.0)
            query_side = query_side.astype(BF16)
        inputs = nrm[here]
        ones = jnp.where((spot[:, :128] >= 64) & (spot[:, :128] < 67), 1.0, 0.0)
        keys = dot(inputs, w_own[1])
        values = dot(inputs, w_own[2]) + value_bias
        if queries:
            query = (dot(inputs, w_own[0]) + query_bias) * head_dim ** (-0.5)
        for h in range(heads):
            tile = slice(h // 2 * 128, h // 2 * 128 + 128)
            turn = (lambda v: v) if h % 2 == 0 else (lambda v: pltpu.roll(v, 64, 1))
            k_aug[h, here, :128] = jnp.where(low128, turn(keys[:, tile]), key_side[:, :128]).astype(BF16)
            k_aug[h, here, 128:] = key_side[:, 128:].astype(BF16)
            v_aug[h, here, :] = jnp.where(low128, turn(values[:, tile]), ones).astype(BF16)
            if queries:
                extra = dot(query_side, squares[h])
                q_aug[h, here, :128] = jnp.where(low128, turn(query[:, tile]), extra[:, :128]).astype(BF16)
                q_aug[h, here, 128:] = extra[:, 128:].astype(BF16)

    project(c, True)
    for i in (0, 3):
        sends[i].wait_recv()
    project(1 - c, True)

    block = rows

    def score_of(h, qb, part, buf):
        s = dot(
            q_aug[h, qb * block : (qb + 1) * block, :],
            k_aug[h, part * 2 * rows : (part + 1) * 2 * rows, :],
            NT,
        )
        score[buf] = s
        top[buf] = jnp.broadcast_to(jnp.max(s, axis=1, keepdims=True), (block, 128))

    def weigh(h, qb, part, buf):
        here = slice(qb * block, (qb + 1) * block)
        m = top[buf][:, :1]
        if part:
            before = peak[h, here, :][:, :1]
            m = jnp.maximum(before, m)
        p = jnp.exp(score[buf] - m).astype(BF16)
        pv = dot(p, v_aug[h, part * 2 * rows : (part + 1) * 2 * rows, :])
        if not part:
            acc[h, here, :] = pv
            peak[h, here, :] = jnp.broadcast_to(m, (block, 128))
            return
        pv = pv + acc[h, here, :] * jnp.exp(before - m)
        total = pv[:, 64:65]
        slot_live = column_of(meta[qb, 1:2, :].astype(F32))
        lse = jnp.where(slot_live > 0, m + jnp.log(total), 0.0)
        spot = lanes((block, 128))
        value = pv / total
        a = split3(lse)
        tail = q_aug[h, here, 128:].astype(F32)
        for i in range(3):
            tail = jnp.where(spot == LSE0 - 128 + i, -a[i], tail)
        q_aug[h, here, 128:] = tail.astype(BF16)
        return value

    def sweep(part, t, unused):
        order = [(0, 0), (0, 1), (1, 0), (1, 1)]
        for i, (odd, qb) in enumerate(order):
            if i < 3:
                score_of(2 * t + order[i + 1][0], order[i + 1][1], part, (i + 1) % 2)
            else:
                score_of(jnp.minimum(2 * t + 2, heads - 2), 0, part, 0)
            value = weigh(2 * t + odd, qb, part, i % 2)
            if part:
                here = slice(qb * block, (qb + 1) * block)
                if odd:
                    value = jnp.where(low128, att[t, here, :], pltpu.roll(value, 64, 1))
                att[t, here, :] = value
                if odd:
                    att_low[t, here, :] = value.astype(BF16)
        if not part:

            @pl.when(t == 1)
            def _():
                pieces[0].wait_recv()
                forwards[0].start()

        return unused

    score_of(0, 0, 0, 0)
    lax.fori_loop(0, heads // 2, functools.partial(sweep, 0), 0)
    pieces[1].wait_recv()
    forwards[1].start()
    sends[1].wait_recv()
    sends[2].wait_recv()
    project(2 + c, False)
    for copy in forwards:
        copy.wait_recv()
    project(3 - c, False)
    stores = [
        pltpu.make_async_copy(k_aug, k_hbm, lsem.at[3]),
        pltpu.make_async_copy(v_aug, v_hbm, lsem.at[4]),
        pltpu.make_async_copy(nrm, n_hbm, lsem.at[5]),
    ]
    for store in stores:
        store.start()
    score_of(0, 0, 1, 0)
    lax.fori_loop(0, heads // 2, functools.partial(sweep, 1), 0)
    stores += [
        pltpu.make_async_copy(q_aug, q_hbm, lsem.at[6]),
        pltpu.make_async_copy(att, a_hbm, lsem.at[7]),
    ]
    for store in stores[3:]:
        store.start()
    theirs = pl.ds(pl.multiple_of((1 - c) * rows, rows), rows)
    swap = remote(att_low.at[:, theirs, :], att_in, rsem, 8, sibling)
    swap.start()
    tiles = heads // 2
    for t in range(tiles):
        att_out[:, pl.ds(at128((c * tiles + t) * 128), 128)] = att_low[t, own, :]
    swap.wait_recv()
    for t in range(tiles):
        att_out[:, pl.ds(at128(((1 - c) * tiles + t) * 128), 128)] = att_in[t]
    for copy in sends + pieces + forwards + [swap]:
        copy.wait_send()
    for store in stores:
        store.wait()


def forward_attention(tokens, seg, live, coords, vectors, t_rows, t_cols, w_qkv):
    rows, width = tokens.shape
    heads = t_rows.shape[0] // 2
    group = rows * 4
    any_spec = pl.BlockSpec(memory_space=pl.ANY)
    vmem = pl.BlockSpec(memory_space=pltpu.VMEM)
    return pl.pallas_call(
        forward_kernel,
        out_shape=[
            jax.ShapeDtypeStruct((rows, width), BF16),
            jax.ShapeDtypeStruct((heads, 2 * rows, 256), BF16),
            jax.ShapeDtypeStruct((heads, group, 256), BF16),
            jax.ShapeDtypeStruct((heads, group, 128), BF16),
            jax.ShapeDtypeStruct((heads // 2, 2 * rows, 128), F32),
            jax.ShapeDtypeStruct((group, width), BF16),
        ],
        in_specs=[vmem] * 7 + [any_spec],
        out_specs=[vmem] + [any_spec] * 5,
        scratch_shapes=[
            pltpu.VMEM((group, width), BF16),
            pltpu.VMEM((3, width, heads * 64), BF16),
            pltpu.VMEM((4, 8, rows), jnp.int32),
            pltpu.VMEM((heads, 256, 256), BF16),
            pltpu.VMEM((2, 16, 256), F32),
            pltpu.VMEM((heads, 2 * rows, 256), BF16),
            pltpu.VMEM((heads, group, 256), BF16),
            pltpu.VMEM((heads, group, 128), BF16),
            pltpu.VMEM((heads, 2 * rows, 128), F32),
            pltpu.VMEM((heads, 2 * rows, 128), F32),
            pltpu.VMEM((2, rows, 2 * rows), F32),
            pltpu.VMEM((2, rows, 128), F32),
            pltpu.VMEM((heads // 2, 2 * rows, 128), F32),
            pltpu.VMEM((heads // 2, 2 * rows, 128), BF16),
            pltpu.VMEM((heads // 2, rows, 128), BF16),
            pltpu.SemaphoreType.DMA((9,)),
            pltpu.SemaphoreType.DMA((9,)),
            pltpu.SemaphoreType.DMA((8,)),
        ],
        compiler_params=pltpu.CompilerParams(
            collective_id=0, has_side_effects=True, vmem_limit_bytes=VMEM_LIMIT
        ),
        name="attention_forward",
    )(tokens, seg, live, coords, vectors, t_rows, t_cols, w_qkv)


def norm_stats(values):
    average = jnp.mean(values, axis=-1, keepdims=True)
    centered = values - average
    scale = lax.rsqrt(jnp.mean(centered * centered, axis=-1, keepdims=True) + EPS)
    return centered * scale, scale


def norm_back(grad, hat, scale, gain):
    e = grad * gain
    return scale * (
        e
        - jnp.mean(e, axis=-1, keepdims=True)
        - hat * jnp.mean(e * hat, axis=-1, keepdims=True)
    )


def back_kernel(
    n_dp, att_low, tokens, grad_out, live, vectors, w_out_hbm, w_fc1_hbm, w_fc2_hbm, q_hbm, k_hbm, v_hbm,
    a_hbm, n_hbm, w_hbm,
    out, g_tokens, sum_qkv, sum_out, sum_fc1, sum_fc2, early, late,
    q_aug, k_aug, v_aug, att, nrm, g_att, g_rows, half_in,
    dkv_out, dkv_in,
    c1, c2, c3, y1, y2, y3, yq, z1, z2, z3, zq, xo1, xo2, xo3, xoq, xi1, xi2, xi3, xiq, gi1, gi2, gi3, giq,
    wq, v_out, v_in,
    cs, cr, ys, yr, zs, zr, xs, xr, gs, gr, vs, vr, ss, sr, lsem,
):
    rows, width = tokens.shape
    head_dim = 64
    pairs = dkv_out.shape[0]
    heads = 2 * pairs
    cols = heads * head_dim
    span = 2 * rows
    dp, x, c = place()
    y, m = dp % 2, dp // 2
    peers_z = n_dp // 2
    sibling = (dp, x * 2 + 1 - c)
    across = (dp, (1 - x) * 2 + c)
    beside = (dp + 1 - 2 * y, x * 2 + c)
    mine = pl.ds(at128(c * cols), cols)
    theirs = pl.ds(at128((1 - c) * cols), cols)
    steps = w_fc1_hbm.shape[1] // width

    units = {}
    for j in range(4):
        units["1", j] = (c1.at[j], y1.at[j], z1.at[j], xo1.at[j], xi1.at[j], gi1.at[j], j, j)
    units["2", 0] = (None, y2, z2, xo2, xi2, gi2, None, 4)
    units["3", 0] = (c3, y3, z3, xo3, xi3, gi3, 8, 5)
    for t in range(pairs):
        units["q", t] = (wq.at[t], yq.at[t], zq.at[t], xoq.at[t], xiq.at[t], giq.at[t], 9 + t, 6 + t)

    def y_copy(key):
        if key[0] == "2":
            size = n_dp // 8
            chunk = key[1]
            src = c2.at[chunk, :, pl.ds(1 - y, 1)]
            dst = y2.at[pl.ds(chunk * size, size)]
            return remote(src, dst, (ys, yr), 4 + chunk, beside)
        unit = units[key]
        return remote(unit[0].at[:, pl.ds(1 - y, 1)], unit[1], (ys, yr), unit[6], beside)

    def y_done(key):
        y_copy(key).wait_recv()
        if key[0] == "2":
            size = n_dp // 8
            here = pl.ds(key[1] * size, size)
            y2[here] = y2[here] + c2[key[1], :, pl.ds(y, 1)]
        else:
            unit = units[key]
            unit[1][...] = unit[1][...] + unit[0][:, pl.ds(y, 1)]

    def z_copies(key):
        unit = units[key]
        copies = []
        for i in range(1, peers_z):
            to = (m + i) % peers_z
            copies.append(
                remote(unit[1].at[to], unit[2].at[i - 1], (zs.at[unit[7]], zr.at[unit[7]]), i - 1, (2 * to + y, x * 2 + c))
            )
        return copies

    def z_send(key):
        for copy in z_copies(key):
            copy.start()

    def z_done(key):
        unit = units[key]
        for copy in z_copies(key):
            copy.wait_recv()
        total = unit[1][m, 0].astype(F32)
        for i in range(peers_z - 1):
            total = total + unit[2][i, 0].astype(F32)
        unit[3][...] = total.astype(BF16)
        x_copy(key).start()

    def x_copy(key):
        unit = units[key]
        return remote(unit[3], unit[4], (xs, xr), unit[7], across)

    def g_copy(key):
        unit = units[key]
        return remote(unit[4], unit[5], (gs, gr), unit[7], sibling)

    def x_done(key):
        unit = units[key]
        x_copy(key).wait_recv()
        unit[4][...] = (unit[3][...].astype(F32) + unit[4][...].astype(F32)).astype(BF16)
        g_copy(key).start()

    def g_done(key):
        unit = units[key]
        g_copy(key).wait_recv()
        for value, who in ((unit[4], c), (unit[5], 1 - c)):
            full = value[...]
            if key[0] == "1":
                sum_fc1[:, pl.ds(at128(key[1] * width + who * cols), cols)] = full
            elif key[0] == "2":
                sum_fc2[:, pl.ds(at128(who * cols), cols)] = full
            elif key[0] == "3":
                sum_out[:, pl.ds(at128(who * cols), cols)] = full
            else:
                for i in range(3):
                    where = pl.ds(at128(i * width + who * cols + key[1] * 128), 128)
                    sum_qkv[:, where] = full[:, i * 128 : (i + 1) * 128]

    stages = [sibling, across]
    bit = 1
    while bit < n_dp:
        stages.append((dp + bit - 2 * bit * (dp // bit % 2), x * 2 + c))
        bit *= 2
    half_stages = len(stages)

    def v_copy(kind, stage):
        index = kind * half_stages + stage
        return remote(v_out.at[index], v_in.at[index], (vs, vr), index, stages[stage])

    def v_done(kind, stage, result):
        index = kind * half_stages + stage
        v_copy(kind, stage).wait_recv()
        total = v_out[index] + v_in[index]
        if stage + 1 < half_stages:
            v_out[index + 1] = total
            v_copy(kind, stage + 1).start()
        else:
            result[...] = total

    def load_pair(t, slot):
        copies = []
        for i, (src, dst) in enumerate(((q_hbm, q_aug), (k_hbm, k_aug), (v_hbm, v_aug))):
            copies.append(
                pltpu.make_async_copy(src.at[pl.ds(2 * t, 2)], dst.at[slot], lsem.at[3 * slot + i])
            )
        return copies

    plain = [
        pltpu.make_async_copy(a_hbm, att, lsem.at[6]),
        pltpu.make_async_copy(n_hbm.at[pl.ds(0, span)], nrm, lsem.at[7]),
    ]
    row = lambda i: vectors[i : i + 1, :]
    live_col = column_of(live[...].astype(F32))
    greet([sibling, across, beside] + [(2 * ((m + i) % peers_z) + y, x * 2 + c) for i in range(1, peers_z)])

    def dense(w_out, w_fc1, w_fc2, w1, w2, w3, branch_attn, normed_s, g_mlp_s, branch_mlp, g_normed, dsem):
        def load_chunk(j, slot):
            return [
                pltpu.make_async_copy(w_fc1_hbm.at[:, pl.ds(at128(j * width), width)], w_fc1.at[slot], dsem.at[slot]),
                pltpu.make_async_copy(
                    w_fc2_hbm.at[pl.ds(pl.multiple_of(j * width, width), width)], w_fc2.at[slot], dsem.at[2 + slot]
                ),
            ]

        load_out = pltpu.make_async_copy(w_out_hbm, w_out, dsem.at[4])
        load_out.start()
        for copy in load_chunk(0, 0):
            copy.start()
        for copy in load_pair(0, 0) + plain:
            copy.start()
        source = tokens[...].astype(F32)
        g_mlp = (grad_out[...].astype(F32) * (live_col * row(SCALE_MLP))).astype(BF16)
        g_mlp_s[...] = g_mlp
        sums = v_out.at[0]
        sums[...] = jnp.zeros_like(sums)
        sums[4:5, :] = jnp.sum(g_mlp.astype(F32), axis=0, keepdims=True)
        sums[10:11, :] = jnp.sum(live_col * source * source, axis=0, keepdims=True)
        sums[13:14, :] = jnp.broadcast_to(jnp.sum(live_col, axis=0, keepdims=True), (1, width))
        load_out.wait()
        branch = dot(att_low[...], w_out[...]) + row(B_OUT)
        branch_attn[...] = branch
        part = live_col * row(SCALE_ATTN) * branch
        stream = source + part
        g_tokens[...] = stream
        sums[11:12, :] = jnp.sum(part * part, axis=0, keepdims=True)
        hat, unused = norm_stats(stream)
        normed_s[...] = (hat * row(LN2_GAIN) + row(LN2_BIAS)).astype(BF16)
        branch_mlp[...] = jnp.zeros_like(branch_mlp)
        g_normed[...] = jnp.zeros_like(g_normed)

        def core_copies(j):
            return [
                remote(w1.at[:, :, :, theirs], c1.at[j], (cs, cr), j, sibling),
                remote(w2.at[:, :, :, theirs], c2.at[j], (cs, cr), 4 + j, sibling),
            ]

        def core_done(j):
            for copy in core_copies(j):
                copy.wait()
            c2[j] = c2[j] + w2[:, :, :, mine]
            size = n_dp // 8
            remote(
                c2.at[j, :, pl.ds(1 - y, 1)], y2.at[pl.ds(j * size, size)], (ys, yr), 4 + j, beside
            ).start()
            c1[j] = c1[j] + w1[:, :, :, mine]
            remote(c1.at[j, :, pl.ds(1 - y, 1)], y1.at[j], (ys, yr), j, beside).start()

        def chunk(j, unused):
            slot = j % 2
            for copy in load_chunk(j, slot):
                copy.wait()

            @pl.when(j + 1 < steps)
            def _():
                for copy in load_chunk(j + 1, 1 - slot):
                    copy.start()

            u = dot(normed_s[...], w_fc1[slot]) + vectors[pl.ds(B_FC1 + j, 1), :]
            square = u * u
            t = jnp.tanh(GELU_A * u * (1.0 + GELU_B * square))
            hidden = (0.5 * u * (1.0 + t)).astype(BF16)
            slope = 0.5 * (1.0 + t) + 0.5 * u * (1.0 - t * t) * (GELU_A + (3.0 * GELU_A * GELU_B) * square)

            @pl.when(j > 0)
            def _():
                core_done(j - 1)

            g_mlp = g_mlp_s[...]
            g_pre = (dot(g_mlp, w_fc2[slot], NT) * slope).astype(BF16)
            sums[pl.ds(6 + j, 1), :] = jnp.sum(g_pre.astype(F32), axis=0, keepdims=True)
            spread_rows(w2, None, dot(hidden, g_mlp, TN))
            spread_rows(w1, None, dot(normed_s[...], g_pre, TN))
            for copy in core_copies(j):
                copy.start()
            branch_mlp[...] += dot(hidden, w_fc2[slot])
            g_normed[...] += dot(g_pre, w_fc1[slot], NT)
            return unused

        lax.fori_loop(0, steps, chunk, 0)
        core_done(steps - 1)
        grad = grad_out[...].astype(F32)
        branch = branch_mlp[...] + row(B_FC2)
        part = live_col * row(SCALE_MLP) * branch
        stream = g_tokens[...]
        out[...] = (stream + part).astype(BF16)
        sums[12:13, :] = jnp.sum(part * part, axis=0, keepdims=True)
        sums[5:6, :] = jnp.sum(grad * live_col * branch, axis=0, keepdims=True)
        hat, scale = norm_stats(stream)
        g_n2 = g_normed[...]
        sums[2:3, :] = jnp.sum(g_n2 * hat, axis=0, keepdims=True)
        sums[3:4, :] = jnp.sum(g_n2, axis=0, keepdims=True)
        g_tokens[...] = grad + norm_back(g_n2, hat, scale, row(LN2_GAIN))
        gated = g_tokens[...] * live_col
        g_attn = (gated * row(SCALE_ATTN)).astype(BF16)
        g_att[...] = dot(g_attn, w_out[...], NT).astype(BF16)
        swap.start()
        sums[1:2, :] = jnp.sum(gated * branch_attn[...], axis=0, keepdims=True)
        sums[0:1, :] = jnp.sum(g_attn.astype(F32), axis=0, keepdims=True)
        v_copy(0, 0).start()
        spread_rows(w3, None, dot(att_low[...], g_attn, TN))
        give = remote(w3.at[:, :, :, theirs], c3, (cs, cr), 8, sibling)
        give.start()
        give.wait()
        c3[...] = c3[...] + w3[:, :, :, mine]
        y_copy(("3", 0)).start()

    def spread_rows(ref, slot, value):
        size = ref.shape[-2]
        for i in range(ref.shape[-4]):
            for k in range(2):
                block = value[(2 * i + k) * size : (2 * i + k + 1) * size].astype(BF16)
                if slot is None:
                    ref[i, k] = block
                else:
                    ref[slot, i, k] = block

    own = pl.ds(pl.multiple_of(c * rows, rows), rows)
    other = pl.ds(pl.multiple_of((1 - c) * rows, rows), rows)
    swap = remote(g_att.at[:, theirs], g_rows.at[own], (ss, sr), 0, sibling)
    part_rows = width // n_dp
    wide_rows = w_fc2_hbm.shape[0] // n_dp
    pl.run_scoped(
        dense,
        pltpu.VMEM((width, width), BF16),
        pltpu.VMEM((2, width, width), BF16),
        pltpu.VMEM((2, width, width), BF16),
        pltpu.VMEM((peers_z, 2, part_rows, width), BF16),
        pltpu.VMEM((n_dp // 8, 2, wide_rows, width), BF16),
        pltpu.VMEM((peers_z, 2, part_rows, width), BF16),
        pltpu.VMEM((rows, width), F32),
        pltpu.VMEM((rows, width), BF16),
        pltpu.VMEM((rows, width), BF16),
        pltpu.VMEM((rows, width), F32),
        pltpu.VMEM((rows, width), F32),
        pltpu.SemaphoreType.DMA((5,)),
    )

    def attention(g_aug, q_turn, g_turn, dq, dkv, dkv_own, d_query, d_key, d_value, w_own):
        late_loads = [
            pltpu.make_async_copy(
                w_hbm.at[:, pl.ds(at128(part * width + c * cols), cols)], w_own.at[part], lsem.at[8 + part]
            )
            for part in range(3)
        ]
        for copy in late_loads:
            copy.start()
        g_rows[own] = g_att[:, mine]
        for copy in plain:
            copy.wait()
        swap.wait_recv()
        spot = lanes((span, 128))
        low = spot < head_dim
        lane = lanes((256, 256))
        line = lax.broadcasted_iota(jnp.int32, (256, 256), 0)
        in_rows = (lane >= ROW0) & (lane < COL0) & (line >= ROW0) & (line < COL0)
        in_cols = (lane >= COL0) & (lane < SEG0) & (line >= COL0) & (line < SEG0)
        flip = jnp.where(lane + line == 255, 1.0, 0.0).astype(BF16)
        sums = v_out.at[half_stages]
        sums[...] = jnp.zeros_like(sums)
        block = rows

        def dkv_copy(t):
            return remote(dkv_out.at[t], dkv_in.at[t], (ss, sr), 1 + t, across)

        def finish_pair(t):
            dkv_copy(t).wait_recv()
            both = (dkv_own[...] + dkv_in[t].astype(F32)).astype(BF16)
            place_k = pl.ds(at128(t * 128), 128)
            dkv[0, :, place_k] = both[:, :128]
            dkv[1, :, place_k] = both[:, 128:]
            part = jnp.concatenate([dq[:, place_k], both], axis=1)
            spread_rows(wq, t, dot(nrm[...], part, TN))

        plan = {
            0: [lambda: v_done(0, 0, early), lambda: y_done(("2", 0)), lambda: y_done(("1", 0)), lambda: z_send(("1", 0))],
            1: [lambda: v_done(0, 1, early)],
            2: [lambda: v_done(0, 2, early), lambda: y_done(("2", 1)), lambda: y_done(("1", 1)), lambda: z_send(("1", 1))],
            3: [lambda: z_done(("1", 0))],
            4: [lambda: v_done(0, 3, early), lambda: y_done(("2", 2)), lambda: y_done(("1", 2)), lambda: z_send(("1", 2)), lambda: x_done(("1", 0))],
            5: [lambda: y_done(("2", 3)), lambda: z_send(("2", 0)), lambda: z_done(("1", 1)), lambda: finish_pair(0), lambda: y_copy(("q", 0)).start()],
            6: [lambda: v_done(0, 4, early), lambda: y_done(("1", 3)), lambda: z_send(("1", 3)), lambda: x_done(("1", 1)), lambda: g_done(("1", 0))],
            7: [lambda: y_done(("3", 0)), lambda: z_send(("3", 0)), lambda: z_done(("1", 2))],
            8: [lambda: y_done(("q", 0)), lambda: z_send(("q", 0)), lambda: x_done(("1", 2)), lambda: g_done(("1", 1))],
            9: [lambda: z_done(("2", 0)), lambda: z_done(("1", 3)), lambda: finish_pair(1), lambda: y_copy(("q", 1)).start()],
            10: [lambda: z_done(("3", 0)), lambda: x_done(("1", 3)), lambda: g_done(("1", 2))],
            11: [lambda: z_done(("q", 0)), lambda: x_done(("2", 0)), lambda: x_done(("3", 0))],
        }

        def sweep(it, unused):
            part = 1 - it % 2
            t = it // 2
            slot = t % 2

            @pl.when(part == 1)
            def _():
                for copy in load_pair(t, slot):
                    copy.wait()
                g = g_rows[:, pl.ds(at128(t * 128), 128)].astype(F32)
                product = g * att[t]
                for odd in range(2):
                    q_turn[odd] = jnp.transpose(q_aug[slot, odd])
                    delta = jnp.sum(jnp.where(low if odd == 0 else ~low, product, 0.0), axis=1, keepdims=True)
                    tile = g if odd == 0 else pltpu.roll(g, 64, 1)
                    tile = jnp.where(low, tile, 0.0)
                    for i, piece in enumerate(split3(delta)):
                        tile = jnp.where(spot == 64 + i, -piece, tile)
                    tile = tile.astype(BF16)
                    g_aug[odd] = tile
                    g_turn[odd] = jnp.transpose(tile)
                d_query[...] = jnp.zeros_like(d_query)

            @pl.when((part == 1) & (t + 1 < pairs))
            def _():
                for copy in load_pair(t + 1, 1 - slot):
                    copy.start()

            for odd in range(2):
                for qb in range(span // block):
                    here = slice(qb * block, (qb + 1) * block)
                    total = d_query[odd, :, here]
                    for kb in range(span // block):
                        there = slice(kb * block, (kb + 1) * block)
                        source = pl.ds(pl.multiple_of(part * span + kb * block, block), block)
                        keys = k_aug[slot, odd, source, :]
                        p = jnp.exp(dot(keys, q_turn[odd, :, here]))
                        p_low = p.astype(BF16)
                        ds = (p * dot(v_aug[slot, odd, source, :], g_turn[odd, :, here])).astype(BF16)
                        gain_value = dot(p_low, g_aug[odd, here, :])
                        gain_key = dot(ds, q_aug[slot, odd, here, :128])
                        if qb == 0:
                            d_value[odd, there, :] = gain_value
                            d_key[odd, there, :] = gain_key
                        else:
                            d_value[odd, there, :] += gain_value
                            d_key[odd, there, :] += gain_key
                        total = total + dot(keys, ds, TN)
                    d_query[odd, :, here] = total
                if odd == 1:
                    new_key = jnp.where(low, d_key[0], pltpu.roll(d_key[1], 64, 1))
                    new_value = jnp.where(low, d_value[0], pltpu.roll(d_value[1], 64, 1))

                    @pl.when(part == 1)
                    def _():
                        dkv_out[t, :, :128] = new_key.astype(BF16)
                        dkv_out[t, :, 128:] = new_value.astype(BF16)
                        dkv_copy(t).start()

                    @pl.when(part == 0)
                    def _():
                        dkv_own[:, :128] = new_key
                        dkv_own[:, 128:] = new_value
                        both = jnp.concatenate([d_query[0, :head_dim, :], d_query[1, :head_dim, :]], axis=0)
                        dq[:, pl.ds(at128(t * 128), 128)] = (jnp.transpose(both) * head_dim ** (-0.5)).astype(BF16)
                        for k in range(2):
                            square = dot(d_query[k].astype(BF16), k_aug[slot, k, :span, :])
                            for table, mask in enumerate((in_rows, in_cols)):
                                flipped = sum(
                                    dot(flip, piece.astype(BF16)) for piece in split3(jnp.where(mask, square, 0.0))
                                )
                                turned = pltpu.roll(flipped, 0, 1, stride=1, stride_axis=0)
                                h = 2 * t + k
                                sums[pl.ds(4 + table * 4 + c * 2 + h // 3, 1), pl.ds(at128(h % 3 * 256), 256)] = (
                                    jnp.sum(turned, axis=0, keepdims=True)
                                )

                for i in range(2 * pairs):

                    @pl.when(it == i)
                    def _(i=i):
                        for act in plan.get(2 * i + odd, []):
                            act()

            return unused

        lax.fori_loop(0, 2 * pairs, sweep, 0)
        last = pairs - 1
        finish_pair(last)
        y_copy(("q", last)).start()

        for copy in late_loads:
            copy.wait()

        def through(where):
            total = dot(dq[where, :], w_own[0], NT)
            return total + dot(dkv[0, where, :], w_own[1], NT) + dot(dkv[1, where, :], w_own[2], NT)

        swap.wait_send()
        g_att[...] = through(other).astype(BF16)
        give = remote(g_att, half_in, (ss, sr), 1 + pairs, sibling)
        give.start()
        y_done(("q", 1))
        z_send(("q", 1))
        g_done(("1", 3))
        x_done(("q", 0))
        g_done(("2", 0))
        g_done(("3", 0))
        sums[2:3, mine] = jnp.sum(dq[...].astype(F32), axis=0, keepdims=True)
        sums[3:4, mine] = jnp.sum(dkv[1].astype(F32), axis=0, keepdims=True)
        g_n1 = through(own)
        hat, scale = norm_stats(tokens[...].astype(F32))
        give.wait_recv()
        g_n1 = g_n1 + half_in[...].astype(F32)
        sums[0:1, :] = jnp.sum(g_n1 * hat, axis=0, keepdims=True)
        sums[1:2, :] = jnp.sum(g_n1, axis=0, keepdims=True)
        v_copy(1, 0).start()
        y_done(("q", last))
        z_send(("q", last))
        g_tokens[...] = g_tokens[...] + norm_back(g_n1, hat, scale, row(LN1_GAIN))
        v_done(1, 0, late)
        z_done(("q", 1))
        v_done(1, 1, late)
        g_done(("q", 0))
        v_done(1, 2, late)
        x_done(("q", 1))
        z_done(("q", last))
        v_done(1, 3, late)
        g_done(("q", 1))
        x_done(("q", last))
        for stage in range(4, half_stages):
            v_done(1, stage, late)
        g_done(("q", last))
        for stage in range(5, half_stages):
            v_done(0, stage, early)
        give.wait_send()
        for t in range(pairs):
            dkv_copy(t).wait_send()

    pl.run_scoped(
        attention,
        pltpu.VMEM((2, span, 128), BF16),
        pltpu.VMEM((2, 256, span), BF16),
        pltpu.VMEM((2, 128, span), BF16),
        pltpu.VMEM((span, cols), BF16),
        pltpu.VMEM((2, span, cols), BF16),
        pltpu.VMEM((span, 256), F32),
        pltpu.VMEM((2, 256, span), F32),
        pltpu.VMEM((2, span, 128), F32),
        pltpu.VMEM((2, span, 128), F32),
        pltpu.VMEM((3, width, cols), BF16),
    )
    for key in units:
        if key[0] != "2":
            y_copy(key).wait_send()
        for copy in z_copies(key):
            copy.wait_send()
        x_copy(key).wait_send()
        g_copy(key).wait_send()
    for j in range(4):
        y_copy(("2", j)).wait_send()
    for kind in range(2):
        for stage in range(half_stages):
            v_copy(kind, stage).wait_send()


def backward(n_dp, att_low, tokens, grad_out, live, vectors, w_out, w_fc1, w_fc2, q_aug, k_aug, v_aug, att, nrm, w_qkv):
    rows, width = tokens.shape
    heads = q_aug.shape[0]
    pairs, cols = heads // 2, heads * 64
    span, group = 2 * rows, 4 * rows
    hidden = w_fc1.shape[1]
    steps = hidden // width
    z, part, wide = n_dp // 2, width // n_dp, hidden // n_dp
    stages = 2 + n_dp.bit_length() - 1
    any_spec = pl.BlockSpec(memory_space=pl.ANY)
    vmem = pl.BlockSpec(memory_space=pltpu.VMEM)
    low = lambda *shape: pltpu.VMEM(shape, BF16)
    full = lambda *shape: pltpu.VMEM(shape, F32)
    dma = lambda *shape: pltpu.SemaphoreType.DMA(shape)
    received = lambda: [low(steps, part, cols), low(wide, cols), low(part, cols), low(pairs, part, cols)]
    return pl.pallas_call(
        functools.partial(back_kernel, n_dp),
        out_shape=[
            jax.ShapeDtypeStruct((rows, width), BF16),
            jax.ShapeDtypeStruct((rows, width), F32),
            jax.ShapeDtypeStruct((part, 3 * width), BF16),
            jax.ShapeDtypeStruct((part, width), BF16),
            jax.ShapeDtypeStruct((part, hidden), BF16),
            jax.ShapeDtypeStruct((wide, width), BF16),
            jax.ShapeDtypeStruct((16, width), F32),
            jax.ShapeDtypeStruct((16, width), F32),
        ],
        in_specs=[vmem] * 5 + [any_spec] * 9,
        out_specs=[vmem] * 8,
        scratch_shapes=[
            low(2, 2, span, 256), low(2, 2, group, 256), low(2, 2, group, 128),
            full(pairs, span, 128), low(span, width),
            low(rows, width), low(span, cols), low(rows, width),
            low(pairs, span, 256), low(pairs, span, 256),
            low(steps, z, 2, part, cols), low(steps, n_dp // 8, 2, wide, cols), low(z, 2, part, cols),
            low(steps, z, 1, part, cols), low(z, 1, wide, cols), low(z, 1, part, cols), low(pairs, z, 1, part, cols),
            low(steps, z - 1, 1, part, cols), low(z - 1, 1, wide, cols), low(z - 1, 1, part, cols),
            low(pairs, z - 1, 1, part, cols),
            *received(), *received(), *received(),
            low(pairs, z, 2, part, cols), full(2 * stages, 16, width), full(2 * stages, 16, width),
            dma(9), dma(9), dma(12), dma(12), dma(9, z - 1), dma(9, z - 1), dma(9), dma(9), dma(9), dma(9),
            dma(2 * stages), dma(2 * stages), dma(2 + pairs), dma(2 + pairs), dma(11),
        ],
        compiler_params=pltpu.CompilerParams(
            collective_id=1, has_side_effects=True, vmem_limit_bytes=VMEM_LIMIT
        ),
        name="backward",
    )(att_low, tokens, grad_out, live, vectors, w_out, w_fc1, w_fc2, q_aug, k_aug, v_aug, att, nrm, w_qkv)


def body(
    tokens, grad_out, segment, live_rows, coords, ln1_gain, ln1_bias, w_qkv, b_query, b_value, w_out,
    b_out, scale_attn, ln2_gain, ln2_bias, w_fc1, b_fc1, w_fc2, b_fc2, scale_mlp, table_rows, table_cols,
):
    rows, width = tokens.shape
    heads = table_rows.shape[0] // 2
    line = lambda v: v.reshape(1, -1)
    live = line(live_rows)
    vectors = jnp.concatenate(
        [
            line(v)
            for v in (ln1_gain, ln1_bias, b_query, b_value, b_out, scale_attn, ln2_gain, ln2_bias, b_fc2, scale_mlp)
        ]
        + [b_fc1.reshape(-1, width)],
        axis=0,
    ).astype(F32)
    att_low, q_aug, k_aug, v_aug, att, nrm = forward_attention(
        tokens, line(segment), live, coords, vectors, table_rows, table_cols, w_qkv
    )
    out, g_tokens, sum_qkv, sum_out, sum_fc1, sum_fc2, early, late = backward(
        lax.axis_size("dp"), att_low, tokens, grad_out, live, vectors, w_out, w_fc1, w_fc2,
        q_aug, k_aug, v_aug, att, nrm, w_qkv,
    )
    totals = jnp.sum(early[10:13], axis=1)
    root_means = jnp.sqrt(totals / (early[13, 0] * width))
    spans = table_rows.shape[1]
    limit = (spans - 1) // 2
    offset = jnp.arange(1, 257)
    offset = jnp.where(offset < 128, offset, offset - 256)
    pick = (jnp.clip(offset, -limit, limit)[:, None] + limit == jnp.arange(spans)[None, :]).astype(F32)
    tables = jnp.dot(late[4:12].reshape(-1, 256), pick, precision=lax.Precision.HIGHEST)
    return (
        out, g_tokens, late[0], late[1], sum_qkv.astype(F32), late[2], late[3], sum_out.astype(F32), early[0], early[1], early[2],
        early[3], sum_fc1.astype(F32), early[6:10].reshape(-1), sum_fc2.astype(F32), early[4], early[5],
        tables[: 2 * heads], tables[2 * heads :], root_means,
    )


def solution(mesh):
    rows = P(("dp", "blk"), None)
    flat = P(("dp", "blk"))
    return jax.shard_map(
        body,
        mesh=mesh,
        in_specs=(rows, rows, flat, flat, P(None, ("dp", "blk"))) + (P(),) * 17,
        out_specs=(
            rows, rows, P(), P(), P("dp", None), P(), P(), P("dp", None), P(), P(), P(), P(),
            P("dp", None), P(), P("dp", None), P(), P(), P(), P(), P(),
        ),
        check_vma=False,
    )
```

```python
import functools

import jax
import jax.numpy as jnp
from jax import lax
from jax.experimental import pallas as pl
from jax.experimental.pallas import tpu as pltpu
from jax.sharding import PartitionSpec as P

MESH = pl.DeviceIdType.MESH
BF16 = jnp.bfloat16
F32 = jnp.float32
EPS = 1e-06
MASKED = -1000000000.0
NT = ((1,), (1,))
TN = ((0,), (0,))
ROW0, COL0, SEG0, LIVE0, LSE0 = 64, 150, 236, 240, 241
VMEM_LIMIT = 62 << 20
(LN1_GAIN, LN1_BIAS, B_QUERY, B_VALUE, B_OUT, SCALE_ATTN, LN2_GAIN, LN2_BIAS, B_FC2, SCALE_MLP, B_FC1) = range(11)
GELU_A, GELU_B = 0.7978845608, 0.044715


def dot(left, right, dims=((1,), (0,))):
    return lax.dot_general(left, right, (dims, ((), ())), preferred_element_type=F32)


def split3(value):
    high = value.astype(BF16).astype(F32)
    rest = value - high
    middle = rest.astype(BF16).astype(F32)
    return high, middle, rest - middle


def lanes(shape):
    return lax.broadcasted_iota(jnp.int32, shape, len(shape) - 1)


def column_of(row):
    return jnp.transpose(jnp.broadcast_to(row, (8, row.shape[1])))[:, :1]


def place():
    me = lax.axis_index("blk")
    return lax.axis_index("dp"), me // 2, me % 2


def greet(peers):
    barrier = pltpu.get_barrier_semaphore()
    for peer in peers:
        pl.semaphore_signal(barrier, inc=1, device_id=peer, device_id_type=MESH)
    pl.semaphore_wait(barrier, len(peers))


def remote(src, dst, sems, index, peer):
    return pltpu.make_async_remote_copy(
        src_ref=src,
        dst_ref=dst,
        send_sem=sems[0].at[index],
        recv_sem=sems[1].at[index],
        device_id=peer,
        device_id_type=MESH,
    )


def at128(index):
    return pl.multiple_of(index, 128)


def forward_kernel(
    tokens, seg, live, coords, ln1_gain, ln1_bias, b_query, b_value, table_rows, table_cols, w_hbm,
    att_out, q_hbm, k_hbm, v_hbm, a_hbm, n_hbm,
    nrm, w_own, meta, squares, base, q_aug, k_aug, v_aug, acc, peak, score, top, att, att_low,
    att_in, vectors, rsend, rrecv, lsem,
):
    rows, width = tokens.shape
    heads, head_dim = q_aug.shape[0], 64
    for i, vector in enumerate((ln1_gain, ln1_bias, b_query, b_value)):
        vectors[i : i + 1, :] = vector[...].astype(F32).reshape(1, width)
    cols = heads * head_dim
    dp, x, c = place()
    sibling = (dp, x * 2 + 1 - c)
    across = (dp, (1 - x) * 2 + c)
    diagonal = (dp, (1 - x) * 2 + 1 - c)
    rsem = (rsend, rrecv)
    loads = [
        pltpu.make_async_copy(
            w_hbm.at[:, pl.ds(at128(part * width + c * cols), cols)], w_own.at[part], lsem.at[part]
        )
        for part in range(3)
    ]
    for load in loads:
        load.start()

    source = tokens[...].astype(F32)
    average = jnp.mean(source, axis=-1, keepdims=True)
    centered = source - average
    spread = jnp.mean(centered * centered, axis=-1, keepdims=True)
    normed = centered * lax.rsqrt(spread + EPS) * vectors[LN1_GAIN : LN1_GAIN + 1, :]
    normed = normed + vectors[LN1_BIAS : LN1_BIAS + 1, :]
    own = pl.ds(pl.multiple_of(c * rows, rows), rows)
    nrm[own] = normed.astype(BF16)
    meta[c] = jnp.concatenate(
        [seg[...], live[...], coords[...], jnp.zeros((4, rows), jnp.int32)], axis=0
    )
    greet([sibling, across, diagonal])
    half = rows // 2
    sends = [
        remote(meta.at[c], meta.at[c], rsem, 0, sibling),
        remote(meta.at[c], meta.at[2 + c], rsem, 1, across),
        remote(meta.at[c], meta.at[2 + c], rsem, 2, diagonal),
        remote(nrm.at[own], nrm.at[own], rsem, 3, sibling),
    ]
    pieces, forwards = [], []
    for i in range(2):
        mine = pl.ds(pl.multiple_of(c * rows + i * half, half), half)
        there = pl.ds(pl.multiple_of((2 + c) * rows + i * half, half), half)
        pieces.append(remote(nrm.at[mine], nrm.at[there], rsem, 4 + i, across))
        forwards.append(remote(nrm.at[there], nrm.at[there], rsem, 6 + i, sibling))
    for copy in sends + pieces:
        copy.start()

    spans = table_rows.shape[1]
    limit = (spans - 1) // 2
    offset = lanes((spans, 256))
    offset = jnp.where(offset < 128, offset, offset - 256)
    entry = lax.broadcasted_iota(jnp.int32, (spans, 256), 0)
    pick = jnp.where(jnp.clip(-offset, -limit, limit) + limit == entry, 1.0, 0.0).astype(BF16)
    base[0] = jnp.pad(dot(table_rows[...], pick), ((0, 4), (0, 0)))
    base[1] = jnp.pad(dot(table_cols[...], pick), ((0, 4), (0, 0)))
    lane = lanes((256, 256))
    line = lax.broadcasted_iota(jnp.int32, (256, 256), 0)
    in_rows = (lane >= ROW0) & (lane < COL0) & (line >= ROW0) & (line < COL0)
    in_cols = (lane >= COL0) & (lane < SEG0) & (line >= COL0) & (line < SEG0)
    keep = (lane == line) & (lane >= SEG0) & (lane <= LIVE0)

    def make_square(h, unused):
        shifted = [
            pltpu.roll(
                jnp.broadcast_to(base[i, pl.ds(c * heads + h, 1), :], (256, 256)),
                0, 1, stride=1, stride_axis=0,
            )
            for i in range(2)
        ]
        square = jnp.where(in_rows, shifted[0], jnp.where(in_cols, shifted[1], 0.0))
        squares[h] = jnp.where(keep, 1.0, square).astype(BF16)
        return unused

    lax.fori_loop(0, heads, make_square, 0)
    for load in loads:
        load.wait()
    own_cols = pl.ds(at128(c * cols), cols)
    query_bias = vectors[B_QUERY : B_QUERY + 1, own_cols]
    value_bias = vectors[B_VALUE : B_VALUE + 1, own_cols]

    low128 = lanes((rows, 128)) < head_dim

    def project(slot, queries):
        here = pl.ds(pl.multiple_of(slot * rows, rows), rows)
        info = jnp.transpose(meta[slot].astype(F32)).astype(jnp.int32)
        page, alive, r, col = (info[:, i : i + 1] for i in range(4))
        spot = lanes((rows, 256))
        hot = (spot == r + ROW0) | (spot == col + COL0)
        key_side = jnp.where(hot | ((spot >= LSE0) & (spot < LSE0 + 3)), 1.0, 0.0)
        other = (spot >= SEG0) & (spot < LIVE0) & (spot != page + SEG0)
        dead = (spot == LIVE0) & (alive <= 0)
        key_side = jnp.where(other | dead, MASKED, key_side)
        if queries:
            query_side = jnp.where(hot | (spot == page + SEG0) | (spot == LIVE0), 1.0, 0.0)
            query_side = query_side.astype(BF16)
        inputs = nrm[here]
        ones = jnp.where((spot[:, :128] >= 64) & (spot[:, :128] < 67), 1.0, 0.0)
        keys = dot(inputs, w_own[1])
        values = dot(inputs, w_own[2]) + value_bias
        if queries:
            query = (dot(inputs, w_own[0]) + query_bias) * head_dim ** (-0.5)
        for h in range(heads):
            tile = slice(h // 2 * 128, h // 2 * 128 + 128)
            turn = (lambda v: v) if h % 2 == 0 else (lambda v: pltpu.roll(v, 64, 1))
            k_aug[h, here, :128] = jnp.where(low128, turn(keys[:, tile]), key_side[:, :128]).astype(BF16)
            k_aug[h, here, 128:] = key_side[:, 128:].astype(BF16)
            v_aug[h, here, :] = jnp.where(low128, turn(values[:, tile]), ones).astype(BF16)
            if queries:
                extra = dot(query_side, squares[h])
                q_aug[h, here, :128] = jnp.where(low128, turn(query[:, tile]), extra[:, :128]).astype(BF16)
                q_aug[h, here, 128:] = extra[:, 128:].astype(BF16)

    project(c, True)
    for i in (0, 3):
        sends[i].wait_recv()
    project(1 - c, True)

    block = rows

    def score_of(h, qb, part, buf):
        s = dot(
            q_aug[h, qb * block : (qb + 1) * block, :],
            k_aug[h, part * 2 * rows : (part + 1) * 2 * rows, :],
            NT,
        )
        score[buf] = s
        top[buf] = jnp.broadcast_to(jnp.max(s, axis=1, keepdims=True), (block, 128))

    def weigh(h, qb, part, buf):
        here = slice(qb * block, (qb + 1) * block)
        m = top[buf][:, :1]
        if part:
            before = peak[h, here, :][:, :1]
            m = jnp.maximum(before, m)
        p = jnp.exp(score[buf] - m).astype(BF16)
        pv = dot(p, v_aug[h, part * 2 * rows : (part + 1) * 2 * rows, :])
        if not part:
            acc[h, here, :] = pv
            peak[h, here, :] = jnp.broadcast_to(m, (block, 128))
            return
        pv = pv + acc[h, here, :] * jnp.exp(before - m)
        total = pv[:, 64:65]
        slot_live = column_of(meta[qb, 1:2, :].astype(F32))
        lse = jnp.where(slot_live > 0, m + jnp.log(total), 0.0)
        spot = lanes((block, 128))
        value = pv / total
        a = split3(lse)
        tail = q_aug[h, here, 128:].astype(F32)
        for i in range(3):
            tail = jnp.where(spot == LSE0 - 128 + i, -a[i], tail)
        q_aug[h, here, 128:] = tail.astype(BF16)
        return value

    def sweep(part, t, unused):
        order = [(0, 0), (0, 1), (1, 0), (1, 1)]
        for i, (odd, qb) in enumerate(order):
            if i < 3:
                score_of(2 * t + order[i + 1][0], order[i + 1][1], part, (i + 1) % 2)
            else:
                score_of(jnp.minimum(2 * t + 2, heads - 2), 0, part, 0)
            value = weigh(2 * t + odd, qb, part, i % 2)
            if part:
                here = slice(qb * block, (qb + 1) * block)
                if odd:
                    value = jnp.where(low128, att[t, here, :], pltpu.roll(value, 64, 1))
                att[t, here, :] = value
                if odd:
                    att_low[t, here, :] = value.astype(BF16)
        if not part:

            @pl.when(t == 1)
            def _():
                pieces[0].wait_recv()
                forwards[0].start()

        return unused

    score_of(0, 0, 0, 0)
    lax.fori_loop(0, heads // 2, functools.partial(sweep, 0), 0)
    pieces[1].wait_recv()
    forwards[1].start()
    sends[1].wait_recv()
    sends[2].wait_recv()
    project(2 + c, False)
    for copy in forwards:
        copy.wait_recv()
    project(3 - c, False)
    stores = [
        pltpu.make_async_copy(k_aug, k_hbm, lsem.at[3]),
        pltpu.make_async_copy(v_aug, v_hbm, lsem.at[4]),
        pltpu.make_async_copy(nrm, n_hbm, lsem.at[5]),
    ]
    for store in stores:
        store.start()
    score_of(0, 0, 1, 0)
    lax.fori_loop(0, heads // 2, functools.partial(sweep, 1), 0)
    stores += [
        pltpu.make_async_copy(q_aug, q_hbm, lsem.at[6]),
        pltpu.make_async_copy(att, a_hbm, lsem.at[7]),
    ]
    for store in stores[3:]:
        store.start()
    theirs = pl.ds(pl.multiple_of((1 - c) * rows, rows), rows)
    swap = remote(att_low.at[:, theirs, :], att_in, rsem, 8, sibling)
    swap.start()
    tiles = heads // 2
    for t in range(tiles):
        att_out[:, pl.ds(at128((c * tiles + t) * 128), 128)] = att_low[t, own, :]
    swap.wait_recv()
    for t in range(tiles):
        att_out[:, pl.ds(at128(((1 - c) * tiles + t) * 128), 128)] = att_in[t]
    for copy in sends + pieces + forwards + [swap]:
        copy.wait_send()
    for store in stores:
        store.wait()


def forward_attention(tokens, seg, live, coords, norm_vectors, t_rows, t_cols, w_qkv):
    rows, width = tokens.shape
    heads = t_rows.shape[0] // 2
    group = rows * 4
    any_spec = pl.BlockSpec(memory_space=pl.ANY)
    vmem = pl.BlockSpec(memory_space=pltpu.VMEM)
    return pl.pallas_call(
        forward_kernel,
        out_shape=[
            jax.ShapeDtypeStruct((rows, width), BF16),
            jax.ShapeDtypeStruct((heads, 2 * rows, 256), BF16),
            jax.ShapeDtypeStruct((heads, group, 256), BF16),
            jax.ShapeDtypeStruct((heads, group, 128), BF16),
            jax.ShapeDtypeStruct((heads // 2, 2 * rows, 128), F32),
            jax.ShapeDtypeStruct((group, width), BF16),
        ],
        in_specs=[vmem] * 10 + [any_spec],
        out_specs=[vmem] + [any_spec] * 5,
        scratch_shapes=[
            pltpu.VMEM((group, width), BF16),
            pltpu.VMEM((3, width, heads * 64), BF16),
            pltpu.VMEM((4, 8, rows), jnp.int32),
            pltpu.VMEM((heads, 256, 256), BF16),
            pltpu.VMEM((2, 16, 256), F32),
            pltpu.VMEM((heads, 2 * rows, 256), BF16),
            pltpu.VMEM((heads, group, 256), BF16),
            pltpu.VMEM((heads, group, 128), BF16),
            pltpu.VMEM((heads, 2 * rows, 128), F32),
            pltpu.VMEM((heads, 2 * rows, 128), F32),
            pltpu.VMEM((2, rows, 2 * rows), F32),
            pltpu.VMEM((2, rows, 128), F32),
            pltpu.VMEM((heads // 2, 2 * rows, 128), F32),
            pltpu.VMEM((heads // 2, 2 * rows, 128), BF16),
            pltpu.VMEM((heads // 2, rows, 128), BF16),
            pltpu.VMEM((8, width), F32),
            pltpu.SemaphoreType.DMA((9,)),
            pltpu.SemaphoreType.DMA((9,)),
            pltpu.SemaphoreType.DMA((8,)),
        ],
        compiler_params=pltpu.CompilerParams(
            collective_id=0, has_side_effects=True, vmem_limit_bytes=VMEM_LIMIT
        ),
        name="attention_forward",
    )(tokens, seg, live, coords, *norm_vectors, t_rows, t_cols, w_qkv)


def norm_stats(values):
    average = jnp.mean(values, axis=-1, keepdims=True)
    centered = values - average
    scale = lax.rsqrt(jnp.mean(centered * centered, axis=-1, keepdims=True) + EPS)
    return centered * scale, scale


def norm_back(grad, hat, scale, gain):
    e = grad * gain
    return scale * (
        e
        - jnp.mean(e, axis=-1, keepdims=True)
        - hat * jnp.mean(e * hat, axis=-1, keepdims=True)
    )


def back_kernel(
    n_dp, att_low, tokens, grad_out, live, ln1_gain, b_out, scale_attn, ln2_gain, ln2_bias, b_fc2, scale_mlp, b_fc1,
    w_out_hbm, w_fc1_hbm, w_fc2_hbm, q_hbm, k_hbm, v_hbm,
    a_hbm, n_hbm, w_hbm,
    out, g_tokens, sum_qkv, sum_out, sum_fc1, sum_fc2, early, late,
    q_aug, k_aug, v_aug, att, nrm, g_att, g_rows, half_in,
    dkv_out, dkv_in,
    c1, c2, c3, p1, y1, y2, y3, yq, z1, z2, z3, zq, xo1, xo2, xo3, xoq, xi1, xi2, xi3, xiq, gi1, gi2, gi3, giq,
    wq, v_out, v_in, vectors,
    cs, cr, ps, pr, ys, yr, zs, zr, xs, xr, gs, gr, vs, vr, ss, sr, lsem,
):
    rows, width = tokens.shape
    head_dim = 64
    pairs = dkv_out.shape[0]
    heads = 2 * pairs
    cols = heads * head_dim
    span = 2 * rows
    dp, x, c = place()
    y, m = dp % 2, dp // 2
    peers_z = n_dp // 2
    sibling = (dp, x * 2 + 1 - c)
    across = (dp, (1 - x) * 2 + c)
    beside = (dp + 1 - 2 * y, x * 2 + c)
    mine = pl.ds(at128(c * cols), cols)
    theirs = pl.ds(at128((1 - c) * cols), cols)
    steps = w_fc1_hbm.shape[1] // width

    units = {}
    for j in range(2):
        units["1", j] = (c1.at[2 * j + x], y1.at[j], z1.at[j], xo1.at[j], xi1.at[j], gi1.at[j, 0], j, j)
    units["2", 0] = (None, y2, z2, xo2, xi2, gi2, None, 4)
    units["3", 0] = (c3, y3, z3, xo3, xi3, gi3, 8, 5)
    for t in range(pairs):
        units["q", t] = (wq.at[t], yq.at[t], zq.at[t], xoq.at[t], xiq.at[t], giq.at[t], 9 + t, 6 + t)

    def pair_copy(pair):
        return remote(c1.at[2 * pair + 1 - x], p1.at[pair], (ps, pr), pair, across)

    def pair_done(pair):
        pair_copy(pair).wait()
        c1[2 * pair + x] = c1[2 * pair + x] + p1[pair]
        y_copy(("1", pair)).start()

    def y_copy(key):
        if key[0] == "2":
            size = n_dp // 8
            chunk = key[1]
            src = c2.at[chunk, :, pl.ds(1 - y, 1)]
            dst = y2.at[pl.ds(chunk * size, size)]
            return remote(src, dst, (ys, yr), 4 + chunk, beside)
        unit = units[key]
        return remote(unit[0].at[:, pl.ds(1 - y, 1)], unit[1], (ys, yr), unit[6], beside)

    def y_done(key):
        y_copy(key).wait_recv()
        if key[0] == "2":
            size = n_dp // 8
            here = pl.ds(key[1] * size, size)
            y2[here] = y2[here] + c2[key[1], :, pl.ds(y, 1)]
        else:
            unit = units[key]
            unit[1][...] = unit[1][...] + unit[0][:, pl.ds(y, 1)]

    def z_copy(key, i):
        unit = units[key]
        to = (m + i) % peers_z
        return remote(
            unit[1].at[to], unit[2].at[i - 1], (zs.at[unit[7]], zr.at[unit[7]]), i - 1, (2 * to + y, x * 2 + c)
        )

    def z_copies(key):
        return [z_copy(key, i) for i in range(1, peers_z)]

    def z_send(key):
        for copy in z_copies(key):
            copy.start()

    def z_send_chunk(chunk):
        size = n_dp // 8
        for i in range(size):
            to = chunk * size + i

            @pl.when(m != to)
            def _(to=to):
                z_copy(("2", 0), (to - m + peers_z) % peers_z).start()

    def z_done(key):
        unit = units[key]
        for copy in z_copies(key):
            copy.wait_recv()
        total = unit[1][m, 0].astype(F32)
        for i in range(peers_z - 1):
            total = total + unit[2][i, 0].astype(F32)
        unit[3][...] = total.astype(BF16)
        x_copy(key).start()
        if key[0] == "1":
            g_copy(key).start()

    def x_copy(key):
        unit = units[key]
        return remote(unit[3], unit[4], (xs, xr), unit[7], across)

    def g_copy(key):
        unit = units[key]
        return remote(unit[3] if key[0] == "1" else unit[4], unit[5], (gs, gr), unit[7], sibling)

    def second_copy(pair):
        return remote(xi1.at[pair], gi1.at[pair, 1], (gs, gr), 2 + pair, sibling)

    def x_done(key):
        unit = units[key]
        x_copy(key).wait_recv()
        if key[0] == "1":
            second_copy(key[1]).start()
            return
        unit[4][...] = (unit[3][...].astype(F32) + unit[4][...].astype(F32)).astype(BF16)
        g_copy(key).start()

    def g_done(key):
        unit = units[key]
        g_copy(key).wait_recv()
        if key[0] == "1":
            second_copy(key[1]).wait_recv()
            for chip, who, ref in (
                (x, c, unit[3]), (1 - x, c, unit[4]), (x, 1 - c, unit[5]), (1 - x, 1 - c, gi1.at[key[1], 1])
            ):
                where = pl.ds(at128((2 * key[1] + chip) * width + who * cols), cols)
                sum_fc1[:, where] = ref[...]
            return
        for value, who in ((unit[4], c), (unit[5], 1 - c)):
            full = value[...]
            if key[0] == "2":
                sum_fc2[:, pl.ds(at128(who * cols), cols)] = full
            elif key[0] == "3":
                sum_out[:, pl.ds(at128(who * cols), cols)] = full
            else:
                for i in range(3):
                    where = pl.ds(at128(i * width + who * cols + key[1] * 128), 128)
                    sum_qkv[:, where] = full[:, i * 128 : (i + 1) * 128]

    stages = [sibling, across]
    bit = 1
    while bit < n_dp:
        stages.append((dp + bit - 2 * bit * (dp // bit % 2), x * 2 + c))
        bit *= 2
    half_stages = len(stages)

    def v_copy(kind, stage):
        index = kind * half_stages + stage
        return remote(v_out.at[index], v_in.at[index], (vs, vr), index, stages[stage])

    def v_done(kind, stage, result):
        index = kind * half_stages + stage
        v_copy(kind, stage).wait_recv()
        total = v_out[index] + v_in[index]
        if stage + 1 < half_stages:
            v_out[index + 1] = total
            v_copy(kind, stage + 1).start()
        else:
            result[...] = total

    def load_pair(t, slot):
        copies = []
        for i, (src, dst) in enumerate(((q_hbm, q_aug), (k_hbm, k_aug), (v_hbm, v_aug))):
            copies.append(
                pltpu.make_async_copy(src.at[pl.ds(2 * t, 2)], dst.at[slot], lsem.at[3 * slot + i])
            )
        return copies

    plain = [
        pltpu.make_async_copy(a_hbm, att, lsem.at[6]),
        pltpu.make_async_copy(n_hbm.at[pl.ds(0, span)], nrm, lsem.at[7]),
    ]
    for i, vector in (
        (LN1_GAIN, ln1_gain), (B_OUT, b_out), (SCALE_ATTN, scale_attn), (LN2_GAIN, ln2_gain), (LN2_BIAS, ln2_bias),
        (B_FC2, b_fc2), (SCALE_MLP, scale_mlp),
    ):
        vectors[i : i + 1, :] = vector[...].astype(F32).reshape(1, width)
    for i in range(steps):
        vectors[B_FC1 + i : B_FC1 + i + 1, :] = b_fc1[i * width : (i + 1) * width].astype(F32).reshape(1, width)
    row = lambda i: vectors[i : i + 1, :]
    live_col = column_of(live[...].astype(F32))
    greet([sibling, across, beside] + [(2 * ((m + i) % peers_z) + y, x * 2 + c) for i in range(1, peers_z)])

    def dense(w_out, w_fc1, w_fc2, w1, w2, w3, branch_attn, normed_s, g_mlp_s, branch_mlp, g_normed, dsem):
        def load_chunk(j, slot):
            return [
                pltpu.make_async_copy(w_fc1_hbm.at[:, pl.ds(at128(j * width), width)], w_fc1.at[slot], dsem.at[slot]),
                pltpu.make_async_copy(
                    w_fc2_hbm.at[pl.ds(pl.multiple_of(j * width, width), width)], w_fc2.at[slot], dsem.at[2 + slot]
                ),
            ]

        load_out = pltpu.make_async_copy(w_out_hbm, w_out, dsem.at[4])
        load_out.start()
        for copy in load_chunk(0, 0):
            copy.start()
        for copy in load_pair(0, 0) + plain:
            copy.start()
        source = tokens[...].astype(F32)
        g_mlp = (grad_out[...].astype(F32) * (live_col * row(SCALE_MLP))).astype(BF16)
        g_mlp_s[...] = g_mlp
        sums = v_out.at[0]
        sums[...] = jnp.zeros_like(sums)
        sums[4:5, :] = jnp.sum(g_mlp.astype(F32), axis=0, keepdims=True)
        sums[10:11, :] = jnp.sum(live_col * source * source, axis=0, keepdims=True)
        sums[13:14, :] = jnp.broadcast_to(jnp.sum(live_col, axis=0, keepdims=True), (1, width))
        load_out.wait()
        branch = dot(att_low[...], w_out[...]) + row(B_OUT)
        branch_attn[...] = branch
        part = live_col * row(SCALE_ATTN) * branch
        stream = source + part
        g_tokens[...] = stream
        sums[11:12, :] = jnp.sum(part * part, axis=0, keepdims=True)
        hat, unused = norm_stats(stream)
        normed_s[...] = (hat * row(LN2_GAIN) + row(LN2_BIAS)).astype(BF16)
        branch_mlp[...] = jnp.zeros_like(branch_mlp)
        g_normed[...] = jnp.zeros_like(g_normed)

        def core_copies(j):
            return [
                remote(w1.at[:, :, :, theirs], c1.at[j], (cs, cr), j, sibling),
                remote(w2.at[:, :, :, theirs], c2.at[j], (cs, cr), 4 + j, sibling),
            ]

        def core_done(j):
            for copy in core_copies(j):
                copy.wait()
            c2[j] = c2[j] + w2[:, :, :, mine]
            size = n_dp // 8
            remote(
                c2.at[j, :, pl.ds(1 - y, 1)], y2.at[pl.ds(j * size, size)], (ys, yr), 4 + j, beside
            ).start()
            c1[j] = c1[j] + w1[:, :, :, mine]
            for pair in range(2):

                @pl.when(j == 2 * pair + 1)
                def _(pair=pair):
                    pair_copy(pair).start()

        def chunk(j, unused):
            slot = j % 2
            for copy in load_chunk(j, slot):
                copy.wait()

            @pl.when(j + 1 < steps)
            def _():
                for copy in load_chunk(j + 1, 1 - slot):
                    copy.start()

            u = dot(normed_s[...], w_fc1[slot]) + vectors[pl.ds(B_FC1 + j, 1), :]
            square = u * u
            t = jnp.tanh(GELU_A * u * (1.0 + GELU_B * square))
            hidden = (0.5 * u * (1.0 + t)).astype(BF16)
            slope = 0.5 * (1.0 + t) + 0.5 * u * (1.0 - t * t) * (GELU_A + (3.0 * GELU_A * GELU_B) * square)

            @pl.when(j > 0)
            def _():
                core_done(j - 1)

            for k in (2, 3):

                @pl.when(j == k)
                def _(k=k):
                    y_done(("2", k - 2))
                    z_send_chunk(k - 2)

            g_mlp = g_mlp_s[...]
            g_pre = (dot(g_mlp, w_fc2[slot], NT) * slope).astype(BF16)
            sums[pl.ds(6 + j, 1), :] = jnp.sum(g_pre.astype(F32), axis=0, keepdims=True)
            spread_rows(w2, None, dot(hidden, g_mlp, TN))
            spread_rows(w1, None, dot(normed_s[...], g_pre, TN))
            for copy in core_copies(j):
                copy.start()
            branch_mlp[...] += dot(hidden, w_fc2[slot])
            g_normed[...] += dot(g_pre, w_fc1[slot], NT)
            return unused

        lax.fori_loop(0, steps, chunk, 0)
        core_done(jnp.int32(steps - 1))
        y_done(("2", 2))
        z_send_chunk(2)
        pair_done(0)
        grad = grad_out[...].astype(F32)
        branch = branch_mlp[...] + row(B_FC2)
        part = live_col * row(SCALE_MLP) * branch
        stream = g_tokens[...]
        out[...] = (stream + part).astype(BF16)
        sums[12:13, :] = jnp.sum(part * part, axis=0, keepdims=True)
        sums[5:6, :] = jnp.sum(grad * live_col * branch, axis=0, keepdims=True)
        hat, scale = norm_stats(stream)
        g_n2 = g_normed[...]
        sums[2:3, :] = jnp.sum(g_n2 * hat, axis=0, keepdims=True)
        sums[3:4, :] = jnp.sum(g_n2, axis=0, keepdims=True)
        g_tokens[...] = grad + norm_back(g_n2, hat, scale, row(LN2_GAIN))
        gated = g_tokens[...] * live_col
        g_attn = (gated * row(SCALE_ATTN)).astype(BF16)
        g_att[...] = dot(g_attn, w_out[...], NT).astype(BF16)
        swap.start()
        sums[1:2, :] = jnp.sum(gated * branch_attn[...], axis=0, keepdims=True)
        sums[0:1, :] = jnp.sum(g_attn.astype(F32), axis=0, keepdims=True)
        v_copy(0, 0).start()
        spread_rows(w3, None, dot(att_low[...], g_attn, TN))
        give = remote(w3.at[:, :, :, theirs], c3, (cs, cr), 8, sibling)
        give.start()
        give.wait()
        c3[...] = c3[...] + w3[:, :, :, mine]
        y_copy(("3", 0)).start()
        y_done(("2", 3))
        z_send_chunk(3)

    def spread_rows(ref, slot, value):
        size = ref.shape[-2]
        for i in range(ref.shape[-4]):
            for k in range(2):
                block = value[(2 * i + k) * size : (2 * i + k + 1) * size].astype(BF16)
                if slot is None:
                    ref[i, k] = block
                else:
                    ref[slot, i, k] = block

    own = pl.ds(pl.multiple_of(c * rows, rows), rows)
    other = pl.ds(pl.multiple_of((1 - c) * rows, rows), rows)
    swap = remote(g_att.at[:, theirs], g_rows.at[own], (ss, sr), 0, sibling)
    part_rows = width // n_dp
    wide_rows = w_fc2_hbm.shape[0] // n_dp
    pl.run_scoped(
        dense,
        pltpu.VMEM((width, width), BF16),
        pltpu.VMEM((2, width, width), BF16),
        pltpu.VMEM((2, width, width), BF16),
        pltpu.VMEM((peers_z, 2, part_rows, width), BF16),
        pltpu.VMEM((n_dp // 8, 2, wide_rows, width), BF16),
        pltpu.VMEM((peers_z, 2, part_rows, width), BF16),
        pltpu.VMEM((rows, width), F32),
        pltpu.VMEM((rows, width), BF16),
        pltpu.VMEM((rows, width), BF16),
        pltpu.VMEM((rows, width), F32),
        pltpu.VMEM((rows, width), F32),
        pltpu.SemaphoreType.DMA((5,)),
    )

    def attention(g_aug, q_turn, g_turn, dq, dkv, dkv_own, d_query, d_key, d_value, w_own):
        late_loads = [
            pltpu.make_async_copy(
                w_hbm.at[:, pl.ds(at128(part * width + c * cols), cols)], w_own.at[part], lsem.at[8 + part]
            )
            for part in range(3)
        ]
        for copy in late_loads:
            copy.start()
        g_rows[own] = g_att[:, mine]
        for copy in plain:
            copy.wait()
        swap.wait_recv()
        spot = lanes((span, 128))
        low = spot < head_dim
        lane = lanes((256, 256))
        line = lax.broadcasted_iota(jnp.int32, (256, 256), 0)
        in_rows = (lane >= ROW0) & (lane < COL0) & (line >= ROW0) & (line < COL0)
        in_cols = (lane >= COL0) & (lane < SEG0) & (line >= COL0) & (line < SEG0)
        flip = jnp.where(lane + line == 255, 1.0, 0.0).astype(BF16)
        sums = v_out.at[half_stages]
        sums[...] = jnp.zeros_like(sums)
        block = rows

        def dkv_copy(t, odd):
            return remote(dkv_out.at[t, odd], dkv_in.at[t, odd], (ss, sr), 1 + 2 * t + odd, across)

        def finish_pair(t):
            for odd in range(2):
                dkv_copy(t, odd).wait_recv()
            first, second = (dkv_own[odd] + dkv_in[t, odd].astype(F32) for odd in range(2))
            place_k = pl.ds(at128(t * 128), 128)
            dkv[0, :, place_k] = jnp.where(low, first, pltpu.roll(second, 64, 1)).astype(BF16)
            dkv[1, :, place_k] = jnp.where(low, pltpu.roll(first, 64, 1), second).astype(BF16)
            both = jnp.concatenate([dkv[0, :, place_k], dkv[1, :, place_k]], axis=1)
            part = jnp.concatenate([dq[:, place_k], both], axis=1)
            spread_rows(wq, t, dot(nrm[...], part, TN))

        plan = {
            0: [lambda: v_done(0, 0, early)],
            1: [lambda: v_done(0, 1, early)],
            2: [lambda: y_done(("1", 0)), lambda: z_send(("1", 0)), lambda: pair_done(1), lambda: v_done(0, 2, early)],
            3: [lambda: y_done(("3", 0)), lambda: z_send(("3", 0))],
            4: [lambda: v_done(0, 3, early)],
            5: [lambda: y_done(("1", 1)), lambda: z_send(("1", 1)), lambda: finish_pair(0), lambda: y_copy(("q", 0)).start()],
            6: [lambda: z_done(("1", 0)), lambda: v_done(0, 4, early)],
            7: [lambda: z_done(("3", 0))],
            8: [lambda: z_done(("2", 0)), lambda: y_done(("q", 0)), lambda: z_send(("q", 0))],
            9: [lambda: z_done(("1", 1)), lambda: finish_pair(1), lambda: y_copy(("q", 1)).start(), lambda: x_done(("1", 0)), lambda: x_done(("3", 0))],
            10: [lambda: x_done(("2", 0)), lambda: z_done(("q", 0)), lambda: x_done(("1", 1))],
            11: [lambda: y_done(("q", 1)), lambda: z_send(("q", 1)), lambda: g_done(("1", 0)), lambda: g_done(("3", 0)), lambda: x_done(("q", 0))],
        }

        def sweep(it, unused):
            part = 1 - it % 2
            t = it // 2
            slot = t % 2

            @pl.when(part == 1)
            def _():
                for copy in load_pair(t, slot):
                    copy.wait()
                g = g_rows[:, pl.ds(at128(t * 128), 128)].astype(F32)
                product = g * att[t]
                for odd in range(2):
                    q_turn[odd] = jnp.transpose(q_aug[slot, odd])
                    delta = jnp.sum(jnp.where(low if odd == 0 else ~low, product, 0.0), axis=1, keepdims=True)
                    tile = g if odd == 0 else pltpu.roll(g, 64, 1)
                    tile = jnp.where(low, tile, 0.0)
                    for i, piece in enumerate(split3(delta)):
                        tile = jnp.where(spot == 64 + i, -piece, tile)
                    tile = tile.astype(BF16)
                    g_aug[odd] = tile
                    g_turn[odd] = jnp.transpose(tile)
                d_query[...] = jnp.zeros_like(d_query)

            @pl.when((part == 1) & (t + 1 < pairs))
            def _():
                for copy in load_pair(t + 1, 1 - slot):
                    copy.start()

            for odd in range(2):
                for qb in range(span // block):
                    here = slice(qb * block, (qb + 1) * block)
                    total = d_query[odd, :, here]
                    for kb in range(span // block):
                        there = slice(kb * block, (kb + 1) * block)
                        source = pl.ds(pl.multiple_of(part * span + kb * block, block), block)
                        keys = k_aug[slot, odd, source, :]
                        p = jnp.exp(dot(keys, q_turn[odd, :, here]))
                        p_low = p.astype(BF16)
                        ds = (p * dot(v_aug[slot, odd, source, :], g_turn[odd, :, here])).astype(BF16)
                        gain_value = dot(p_low, g_aug[odd, here, :])
                        gain_key = dot(ds, q_aug[slot, odd, here, :128])
                        if qb == 0:
                            d_value[odd, there, :] = gain_value
                            d_key[odd, there, :] = gain_key
                        else:
                            d_value[odd, there, :] += gain_value
                            d_key[odd, there, :] += gain_key
                        total = total + dot(keys, ds, TN)
                    d_query[odd, :, here] = total
                new = jnp.where(low, d_key[odd], pltpu.roll(d_value[odd], 64, 1))

                @pl.when(part == 1)
                def _(odd=odd):
                    dkv_out[t, odd] = new.astype(BF16)
                    dkv_copy(t, odd).start()

                @pl.when(part == 0)
                def _(odd=odd):
                    dkv_own[odd] = new

                if odd == 1:

                    @pl.when(part == 0)
                    def _():
                        both = jnp.concatenate([d_query[0, :head_dim, :], d_query[1, :head_dim, :]], axis=0)
                        dq[:, pl.ds(at128(t * 128), 128)] = (jnp.transpose(both) * head_dim ** (-0.5)).astype(BF16)
                        for k in range(2):
                            square = dot(d_query[k].astype(BF16), k_aug[slot, k, :span, :])
                            for table, mask in enumerate((in_rows, in_cols)):
                                flipped = sum(
                                    dot(flip, piece.astype(BF16)) for piece in split3(jnp.where(mask, square, 0.0))
                                )
                                turned = pltpu.roll(flipped, 0, 1, stride=1, stride_axis=0)
                                h = 2 * t + k
                                sums[pl.ds(4 + table * 4 + c * 2 + h // 3, 1), pl.ds(at128(h % 3 * 256), 256)] = (
                                    jnp.sum(turned, axis=0, keepdims=True)
                                )

                for i in range(2 * pairs):

                    @pl.when(it == i)
                    def _(i=i):
                        for act in plan.get(2 * i + odd, []):
                            act()

            return unused

        lax.fori_loop(0, 2 * pairs, sweep, 0)
        last = pairs - 1
        finish_pair(last)
        y_copy(("q", last)).start()

        for copy in late_loads:
            copy.wait()

        def through(where):
            total = dot(dq[where, :], w_own[0], NT)
            return total + dot(dkv[0, where, :], w_own[1], NT) + dot(dkv[1, where, :], w_own[2], NT)

        swap.wait_send()
        g_att[...] = through(other).astype(BF16)
        give = remote(g_att, half_in, (ss, sr), 1 + 2 * pairs, sibling)
        give.start()
        g_done(("1", 1))
        g_done(("2", 0))
        sums[2:3, mine] = jnp.sum(dq[...].astype(F32), axis=0, keepdims=True)
        sums[3:4, mine] = jnp.sum(dkv[1].astype(F32), axis=0, keepdims=True)
        g_n1 = through(own)
        hat, scale = norm_stats(tokens[...].astype(F32))
        give.wait_recv()
        g_n1 = g_n1 + half_in[...].astype(F32)
        sums[0:1, :] = jnp.sum(g_n1 * hat, axis=0, keepdims=True)
        sums[1:2, :] = jnp.sum(g_n1, axis=0, keepdims=True)
        v_copy(1, 0).start()
        y_done(("q", last))
        z_send(("q", last))
        g_tokens[...] = g_tokens[...] + norm_back(g_n1, hat, scale, row(LN1_GAIN))
        v_done(1, 0, late)
        z_done(("q", 1))
        v_done(1, 1, late)
        g_done(("q", 0))
        v_done(1, 2, late)
        x_done(("q", 1))
        z_done(("q", last))
        v_done(1, 3, late)
        g_done(("q", 1))
        x_done(("q", last))
        for stage in range(4, half_stages):
            v_done(1, stage, late)
        g_done(("q", last))
        for stage in range(5, half_stages):
            v_done(0, stage, early)
        give.wait_send()
        for t in range(pairs):
            for odd in range(2):
                dkv_copy(t, odd).wait_send()

    pl.run_scoped(
        attention,
        pltpu.VMEM((2, span, 128), BF16),
        pltpu.VMEM((2, 256, span), BF16),
        pltpu.VMEM((2, 128, span), BF16),
        pltpu.VMEM((span, cols), BF16),
        pltpu.VMEM((2, span, cols), BF16),
        pltpu.VMEM((2, span, 128), F32),
        pltpu.VMEM((2, 256, span), F32),
        pltpu.VMEM((2, span, 128), F32),
        pltpu.VMEM((2, span, 128), F32),
        pltpu.VMEM((3, width, cols), BF16),
    )
    for key in units:
        if key[0] != "2":
            y_copy(key).wait_send()
        for copy in z_copies(key):
            copy.wait_send()
        x_copy(key).wait_send()
        g_copy(key).wait_send()
    for j in range(4):
        y_copy(("2", j)).wait_send()
    for pair in range(2):
        second_copy(pair).wait_send()
    for kind in range(2):
        for stage in range(half_stages):
            v_copy(kind, stage).wait_send()


def backward(n_dp, att_low, tokens, grad_out, live, vectors, w_out, w_fc1, w_fc2, q_aug, k_aug, v_aug, att, nrm, w_qkv):
    rows, width = tokens.shape
    heads = q_aug.shape[0]
    pairs, cols = heads // 2, heads * 64
    span, group = 2 * rows, 4 * rows
    hidden = w_fc1.shape[1]
    steps = hidden // width
    z, part, wide = n_dp // 2, width // n_dp, hidden // n_dp
    stages = 2 + n_dp.bit_length() - 1
    any_spec = pl.BlockSpec(memory_space=pl.ANY)
    vmem = pl.BlockSpec(memory_space=pltpu.VMEM)
    low = lambda *shape: pltpu.VMEM(shape, BF16)
    full = lambda *shape: pltpu.VMEM(shape, F32)
    dma = lambda *shape: pltpu.SemaphoreType.DMA(shape)
    received = lambda *lead: [low(2, *lead, part, cols), low(wide, cols), low(part, cols), low(pairs, part, cols)]
    return pl.pallas_call(
        functools.partial(back_kernel, n_dp),
        out_shape=[
            jax.ShapeDtypeStruct((rows, width), BF16),
            jax.ShapeDtypeStruct((rows, width), F32),
            jax.ShapeDtypeStruct((part, 3 * width), BF16),
            jax.ShapeDtypeStruct((part, width), BF16),
            jax.ShapeDtypeStruct((part, hidden), BF16),
            jax.ShapeDtypeStruct((wide, width), BF16),
            jax.ShapeDtypeStruct((16, width), F32),
            jax.ShapeDtypeStruct((16, width), F32),
        ],
        in_specs=[vmem] * 12 + [any_spec] * 9,
        out_specs=[vmem] * 8,
        scratch_shapes=[
            low(2, 2, span, 256), low(2, 2, group, 256), low(2, 2, group, 128),
            full(pairs, span, 128), low(span, width),
            low(rows, width), low(span, cols), low(rows, width),
            low(pairs, 2, span, 128), low(pairs, 2, span, 128),
            low(steps, z, 2, part, cols), low(steps, n_dp // 8, 2, wide, cols), low(z, 2, part, cols),
            low(2, z, 2, part, cols),
            low(2, z, 1, part, cols), low(z, 1, wide, cols), low(z, 1, part, cols), low(pairs, z, 1, part, cols),
            low(2, z - 1, 1, part, cols), low(z - 1, 1, wide, cols), low(z - 1, 1, part, cols),
            low(pairs, z - 1, 1, part, cols),
            *received(), *received(), *received(2),
            low(pairs, z, 2, part, cols), full(2 * stages, 16, width), full(2 * stages, 16, width), full(16, width),
            dma(9), dma(9), dma(2), dma(2), dma(12), dma(12), dma(9, z - 1), dma(9, z - 1), dma(9), dma(9), dma(9), dma(9),
            dma(2 * stages), dma(2 * stages), dma(2 + 2 * pairs), dma(2 + 2 * pairs), dma(11),
        ],
        compiler_params=pltpu.CompilerParams(
            collective_id=1, has_side_effects=True, vmem_limit_bytes=VMEM_LIMIT
        ),
        name="backward",
    )(att_low, tokens, grad_out, live, *vectors, w_out, w_fc1, w_fc2, q_aug, k_aug, v_aug, att, nrm, w_qkv)


def outputs_kernel(out_in, tokens_in, qkv_in, out_w_in, fc1_in, fc2_in, early, late, *refs):
    (
        out, g_tokens, g_ln1, b_ln1, qkv, b_query, b_value, out_w, b_out, s_attn, g_ln2, b_ln2, fc1, b_fc1, fc2,
        b_fc2, s_mlp, t_rows, t_cols, means,
    ) = refs
    width = out.shape[1]
    out[...] = out_in[...]
    g_tokens[...] = tokens_in[...]
    for ref, value in ((qkv, qkv_in), (out_w, out_w_in), (fc1, fc1_in), (fc2, fc2_in)):
        ref[...] = value[...].astype(F32)
    for i, ref in enumerate((b_out, s_attn, g_ln2, b_ln2, b_fc2, s_mlp)):
        ref[...] = early[i, :]
    for i in range(b_fc1.shape[0] // width):
        b_fc1[i * width : (i + 1) * width] = early[6 + i, :]
    for i, ref in enumerate((g_ln1, b_ln1, b_query, b_value)):
        ref[...] = late[i, :]
    count = early[13:14, :1]
    lane = lanes((1, 3))
    squares = jnp.zeros((1, 3), F32)
    for i in range(3):
        squares = jnp.where(lane == i, jnp.sum(early[10 + i : 11 + i, :], axis=1, keepdims=True), squares)
    means[...] = jnp.sqrt(squares / (count * width))[0]
    spans = t_rows.shape[1]
    limit = (spans - 1) // 2
    offset = lax.broadcasted_iota(jnp.int32, (256, spans), 0) + 1
    offset = jnp.where(offset < 128, offset, offset - 256)
    pick = jnp.where(jnp.clip(offset, -limit, limit) + limit == lanes((256, spans)), 1.0, 0.0).astype(BF16)
    for third in range(3):
        part = late[4:12, third * 256 : (third + 1) * 256]
        sums = sum(dot(piece.astype(BF16), pick) for piece in split3(part))
        for i in range(8):
            ref = (t_rows, t_cols)[i // 4]
            ref[i % 4 * 3 + third : i % 4 * 3 + third + 1, :] = sums[i : i + 1, :]


def write_outputs(arrays, shapes):
    vmem = pl.BlockSpec(memory_space=pltpu.VMEM)
    return pl.pallas_call(
        outputs_kernel,
        out_shape=[jax.ShapeDtypeStruct(*shape) for shape in shapes],
        in_specs=[vmem] * len(arrays),
        out_specs=[vmem] * len(shapes),
        compiler_params=pltpu.CompilerParams(vmem_limit_bytes=VMEM_LIMIT),
        name="outputs",
    )(*arrays)


def body(
    tokens, grad_out, segment, live_rows, coords, ln1_gain, ln1_bias, w_qkv, b_query, b_value, w_out,
    b_out, scale_attn, ln2_gain, ln2_bias, w_fc1, b_fc1, w_fc2, b_fc2, scale_mlp, table_rows, table_cols,
):
    rows, width = tokens.shape
    heads = table_rows.shape[0] // 2
    line = lambda v: v.reshape(1, -1)
    live = line(live_rows)
    att_low, q_aug, k_aug, v_aug, att, nrm = forward_attention(
        tokens, line(segment), live, coords, (ln1_gain, ln1_bias, b_query, b_value), table_rows, table_cols, w_qkv
    )
    out, g_tokens, sum_qkv, sum_out, sum_fc1, sum_fc2, early, late = backward(
        lax.axis_size("dp"), att_low, tokens, grad_out, live,
        (ln1_gain, b_out, scale_attn, ln2_gain, ln2_bias, b_fc2, scale_mlp, b_fc1), w_out, w_fc1, w_fc2,
        q_aug, k_aug, v_aug, att, nrm, w_qkv,
    )
    part, hidden = sum_out.shape[0], w_fc1.shape[1]
    vector, table = ((width,), F32), (table_rows.shape, F32)
    return write_outputs(
        (out, g_tokens, sum_qkv, sum_out, sum_fc1, sum_fc2, early, late),
        [
            ((rows, width), BF16), ((rows, width), F32), vector, vector, ((part, 3 * width), F32), vector, vector,
            ((part, width), F32), vector, vector, vector, vector, ((part, hidden), F32), ((hidden,), F32),
            (sum_fc2.shape, F32), vector, vector, table, table, ((3,), F32),
        ],
    )


def solution(mesh):
    rows = P(("dp", "blk"), None)
    flat = P(("dp", "blk"))
    return jax.shard_map(
        body,
        mesh=mesh,
        in_specs=(rows, rows, flat, flat, P(None, ("dp", "blk"))) + (P(),) * 17,
        out_specs=(
            rows, rows, P(), P(), P("dp", None), P(), P(), P("dp", None), P(), P(), P(), P(),
            P("dp", None), P(), P("dp", None), P(), P(), P(), P(), P(),
        ),
        check_vma=False,
    )
```

```python
import functools

import jax
import jax.numpy as jnp
from jax import lax
from jax.experimental import pallas as pl
from jax.experimental.pallas import tpu as pltpu
from jax.sharding import PartitionSpec as P

MESH = pl.DeviceIdType.MESH
BF16 = jnp.bfloat16
F32 = jnp.float32
EPS = 1e-06
MASKED = -1000000000.0
NT = ((1,), (1,))
TN = ((0,), (0,))
ROW0, COL0, SEG0, LIVE0, LSE0 = 64, 150, 236, 240, 241
VMEM_LIMIT = 63 << 20
(LN1_GAIN, LN1_BIAS, B_QUERY, B_VALUE, B_OUT, SCALE_ATTN, LN2_GAIN, LN2_BIAS, B_FC2, SCALE_MLP, B_FC1) = range(11)
GELU_A, GELU_B = 0.7978845608, 0.044715


def dot(left, right, dims=((1,), (0,))):
    return lax.dot_general(left, right, (dims, ((), ())), preferred_element_type=F32)


def split3(value):
    high = value.astype(BF16).astype(F32)
    rest = value - high
    middle = rest.astype(BF16).astype(F32)
    return high, middle, rest - middle


def lanes(shape):
    return lax.broadcasted_iota(jnp.int32, shape, len(shape) - 1)


def column_of(row):
    return jnp.transpose(jnp.broadcast_to(row, (8, row.shape[1])))[:, :1]


def place():
    me = lax.axis_index("blk")
    return lax.axis_index("dp"), me // 2, me % 2


def announce(peers):
    barrier = pltpu.get_barrier_semaphore()
    for peer in peers:
        pl.semaphore_signal(barrier, inc=1, device_id=peer, device_id_type=MESH)


def meet(peers):
    pl.semaphore_wait(pltpu.get_barrier_semaphore(), len(peers))


def remote(src, dst, sems, index, peer):
    return pltpu.make_async_remote_copy(
        src_ref=src,
        dst_ref=dst,
        send_sem=sems[0].at[index],
        recv_sem=sems[1].at[index],
        device_id=peer,
        device_id_type=MESH,
    )


def at128(index):
    return pl.multiple_of(index, 128)


def forward_kernel(
    tokens, seg, live, coords, ln1_gain, ln1_bias, b_query, b_value, table_rows, table_cols, w_hbm,
    att_out, q_hbm, k_hbm, v_hbm, a_hbm, n_hbm,
    nrm, w_own, meta, squares, base, q_aug, k_aug, v_aug, acc, peak, score, top, att, att_low,
    att_in, vectors, alive_rows, rsend, rrecv, lsem,
):
    rows, width = tokens.shape
    heads, head_dim = q_aug.shape[0], 64
    cols = heads * head_dim
    dp, x, c = place()
    sibling = (dp, x * 2 + 1 - c)
    across = (dp, (1 - x) * 2 + c)
    diagonal = (dp, (1 - x) * 2 + 1 - c)
    rsem = (rsend, rrecv)
    announce([sibling, across, diagonal])
    loads = [
        pltpu.make_async_copy(
            w_hbm.at[:, pl.ds(at128(part * width + c * cols), cols)], w_own.at[part], lsem.at[part]
        )
        for part in range(3)
    ]
    for load in loads:
        load.start()

    for i, vector in enumerate((ln1_gain, ln1_bias, b_query, b_value)):
        vectors[i : i + 1, :] = vector[...].astype(F32).reshape(1, width)

    source = tokens[...].astype(F32)
    average = jnp.mean(source, axis=-1, keepdims=True)
    centered = source - average
    spread = jnp.mean(centered * centered, axis=-1, keepdims=True)
    normed = centered * lax.rsqrt(spread + EPS) * vectors[LN1_GAIN : LN1_GAIN + 1, :]
    normed = normed + vectors[LN1_BIAS : LN1_BIAS + 1, :]
    own = pl.ds(pl.multiple_of(c * rows, rows), rows)
    nrm[own] = normed.astype(BF16)
    meta[c] = jnp.concatenate(
        [seg[...], live[...], coords[...], jnp.zeros((4, rows), jnp.int32)], axis=0
    )
    meet([sibling, across, diagonal])
    half = rows // 2
    sends = [
        remote(meta.at[c], meta.at[c], rsem, 0, sibling),
        remote(meta.at[c], meta.at[2 + c], rsem, 1, across),
        remote(meta.at[c], meta.at[2 + c], rsem, 2, diagonal),
        remote(nrm.at[own], nrm.at[own], rsem, 3, sibling),
    ]
    pieces, forwards = [], []
    for i in range(2):
        mine = pl.ds(pl.multiple_of(c * rows + i * half, half), half)
        there = pl.ds(pl.multiple_of((2 + c) * rows + i * half, half), half)
        pieces.append(remote(nrm.at[mine], nrm.at[there], rsem, 4 + i, across))
        forwards.append(remote(nrm.at[there], nrm.at[there], rsem, 6 + i, sibling))
    for copy in sends + pieces:
        copy.start()

    spans = table_rows.shape[1]
    limit = (spans - 1) // 2
    offset = lanes((spans, 256))
    offset = jnp.where(offset < 128, offset, offset - 256)
    entry = lax.broadcasted_iota(jnp.int32, (spans, 256), 0)
    pick = jnp.where(jnp.clip(-offset, -limit, limit) + limit == entry, 1.0, 0.0).astype(BF16)
    base[0] = jnp.pad(dot(table_rows[...], pick), ((0, 4), (0, 0)))
    base[1] = jnp.pad(dot(table_cols[...], pick), ((0, 4), (0, 0)))
    lane = lanes((256, 256))
    line = lax.broadcasted_iota(jnp.int32, (256, 256), 0)
    in_rows = (lane >= ROW0) & (lane < COL0) & (line >= ROW0) & (line < COL0)
    in_cols = (lane >= COL0) & (lane < SEG0) & (line >= COL0) & (line < SEG0)
    keep = (lane == line) & (lane >= SEG0) & (lane <= LIVE0)

    def make_square(h, unused):
        shifted = [
            pltpu.roll(
                jnp.broadcast_to(base[i, pl.ds(c * heads + h, 1), :], (256, 256)),
                0, 1, stride=1, stride_axis=0,
            )
            for i in range(2)
        ]
        square = jnp.where(in_rows, shifted[0], jnp.where(in_cols, shifted[1], 0.0))
        squares[h] = jnp.where(keep, 1.0, square).astype(BF16)
        return unused

    lax.fori_loop(0, heads, make_square, 0)
    for load in loads:
        load.wait()
    own_cols = pl.ds(at128(c * cols), cols)
    query_bias = vectors[B_QUERY : B_QUERY + 1, own_cols]
    value_bias = vectors[B_VALUE : B_VALUE + 1, own_cols]

    low128 = lanes((rows, 128)) < head_dim

    def project(slot, queries):
        here = pl.ds(pl.multiple_of(slot * rows, rows), rows)
        info = jnp.transpose(meta[slot].astype(F32)).astype(jnp.int32)
        page, alive, r, col = (info[:, i : i + 1] for i in range(4))
        spot = lanes((rows, 256))
        hot = (spot == r + ROW0) | (spot == col + COL0)
        key_side = jnp.where(hot | ((spot >= LSE0) & (spot < LSE0 + 3)), 1.0, 0.0)
        other = (spot >= SEG0) & (spot < LIVE0) & (spot != page + SEG0)
        dead = (spot == LIVE0) & (alive <= 0)
        key_side = jnp.where(other | dead, MASKED, key_side)
        if queries:
            query_side = jnp.where(hot | (spot == page + SEG0) | (spot == LIVE0), 1.0, 0.0)
            query_side = query_side.astype(BF16)
        inputs = nrm[here]
        ones = jnp.where((spot[:, :128] >= 64) & (spot[:, :128] < 67), 1.0, 0.0)
        keys = dot(inputs, w_own[1])
        values = dot(inputs, w_own[2]) + value_bias
        if queries:
            query = (dot(inputs, w_own[0]) + query_bias) * head_dim ** (-0.5)
        for h in range(heads):
            tile = slice(h // 2 * 128, h // 2 * 128 + 128)
            turn = (lambda v: v) if h % 2 == 0 else (lambda v: pltpu.roll(v, 64, 1))
            k_aug[h, here, :128] = jnp.where(low128, turn(keys[:, tile]), key_side[:, :128]).astype(BF16)
            k_aug[h, here, 128:] = key_side[:, 128:].astype(BF16)
            v_aug[h, here, :] = jnp.where(low128, turn(values[:, tile]), ones).astype(BF16)
            if queries:
                extra = dot(query_side, squares[h])
                q_aug[h, here, :128] = jnp.where(low128, turn(query[:, tile]), extra[:, :128]).astype(BF16)
                q_aug[h, here, 128:] = extra[:, 128:].astype(BF16)

    project(c, True)
    for i in (0, 3):
        sends[i].wait_recv()
    project(1 - c, True)

    block = rows

    def score_of(h, qb, part, buf):
        s = dot(
            q_aug[h, qb * block : (qb + 1) * block, :],
            k_aug[h, part * 2 * rows : (part + 1) * 2 * rows, :],
            NT,
        )
        score[buf] = s
        top[buf] = jnp.broadcast_to(jnp.max(s, axis=1, keepdims=True), (block, 128))

    def weigh(h, qb, part, buf):
        here = slice(qb * block, (qb + 1) * block)
        m = top[buf]
        if part:
            before = peak[h, here, :]
            m = jnp.maximum(before, m)
        p = jnp.concatenate(
            [jnp.exp(score[buf, :, i : i + 128] - m).astype(BF16) for i in range(0, 2 * rows, 128)], axis=1
        )
        pv = dot(p, v_aug[h, part * 2 * rows : (part + 1) * 2 * rows, :])
        if not part:
            acc[h, here, :] = pv
            peak[h, here, :] = m
            return
        pv = pv + acc[h, here, :] * jnp.exp(before - m)
        total = jnp.broadcast_to(pv[:, 64:65], (block, 128))
        lse = jnp.where(alive_rows[qb] > 0, m + jnp.log(total), 0.0)
        value = pv / total
        tail = q_aug[h, here, 128:].astype(F32)
        for i, piece in enumerate(split3(lse)):
            tail = jnp.where(low_lane == LSE0 - 128 + i, -piece, tail)
        q_aug[h, here, 128:] = tail.astype(BF16)
        return value

    low_lane = lanes((block, 128))
    for qb in range(2):
        alive_rows[qb] = jnp.broadcast_to(column_of(meta[qb, 1:2, :].astype(F32)), (block, 128))

    def sweep(part, t, unused):
        order = [(0, 0), (0, 1), (1, 0), (1, 1)]
        for i, (odd, qb) in enumerate(order):
            if i < 3:
                score_of(2 * t + order[i + 1][0], order[i + 1][1], part, (i + 1) % 2)
            else:
                score_of(jnp.minimum(2 * t + 2, heads - 2), 0, part, 0)
            value = weigh(2 * t + odd, qb, part, i % 2)
            if part:
                here = slice(qb * block, (qb + 1) * block)
                if odd:
                    value = jnp.where(low128, att[t, here, :], pltpu.roll(value, 64, 1))
                att[t, here, :] = value
                if odd:
                    att_low[t, here, :] = value.astype(BF16)
        if not part:

            @pl.when(t == 1)
            def _():
                pieces[0].wait_recv()
                forwards[0].start()

        return unused

    score_of(0, 0, 0, 0)
    lax.fori_loop(0, heads // 2, functools.partial(sweep, 0), 0)
    pieces[1].wait_recv()
    forwards[1].start()
    sends[1].wait_recv()
    sends[2].wait_recv()
    project(2 + c, False)
    for copy in forwards:
        copy.wait_recv()
    project(3 - c, False)
    stores = [
        pltpu.make_async_copy(k_aug, k_hbm, lsem.at[3]),
        pltpu.make_async_copy(v_aug, v_hbm, lsem.at[4]),
        pltpu.make_async_copy(nrm, n_hbm, lsem.at[5]),
    ]
    for store in stores:
        store.start()
    score_of(0, 0, 1, 0)
    lax.fori_loop(0, heads // 2, functools.partial(sweep, 1), 0)
    stores += [
        pltpu.make_async_copy(q_aug, q_hbm, lsem.at[6]),
        pltpu.make_async_copy(att, a_hbm, lsem.at[7]),
    ]
    for store in stores[3:]:
        store.start()
    theirs = pl.ds(pl.multiple_of((1 - c) * rows, rows), rows)
    swap = remote(att_low.at[:, theirs, :], att_in, rsem, 8, sibling)
    swap.start()
    tiles = heads // 2
    for t in range(tiles):
        att_out[:, pl.ds(at128((c * tiles + t) * 128), 128)] = att_low[t, own, :]
    swap.wait_recv()
    for t in range(tiles):
        att_out[:, pl.ds(at128(((1 - c) * tiles + t) * 128), 128)] = att_in[t]
    for copy in sends + pieces + forwards + [swap]:
        copy.wait_send()
    for store in stores:
        store.wait()


def forward_attention(tokens, seg, live, coords, norm_vectors, t_rows, t_cols, w_qkv):
    rows, width = tokens.shape
    heads = t_rows.shape[0] // 2
    group = rows * 4
    any_spec = pl.BlockSpec(memory_space=pl.ANY)
    vmem = pl.BlockSpec(memory_space=pltpu.VMEM)
    return pl.pallas_call(
        forward_kernel,
        out_shape=[
            jax.ShapeDtypeStruct((rows, width), BF16),
            jax.ShapeDtypeStruct((heads, 2 * rows, 256), BF16),
            jax.ShapeDtypeStruct((heads, group, 256), BF16),
            jax.ShapeDtypeStruct((heads, group, 128), BF16),
            jax.ShapeDtypeStruct((heads // 2, 2 * rows, 128), F32),
            jax.ShapeDtypeStruct((group, width), BF16),
        ],
        in_specs=[vmem] * 10 + [any_spec],
        out_specs=[vmem] + [any_spec] * 5,
        scratch_shapes=[
            pltpu.VMEM((group, width), BF16),
            pltpu.VMEM((3, width, heads * 64), BF16),
            pltpu.VMEM((4, 8, rows), jnp.int32),
            pltpu.VMEM((heads, 256, 256), BF16),
            pltpu.VMEM((2, 16, 256), F32),
            pltpu.VMEM((heads, 2 * rows, 256), BF16),
            pltpu.VMEM((heads, group, 256), BF16),
            pltpu.VMEM((heads, group, 128), BF16),
            pltpu.VMEM((heads, 2 * rows, 128), F32),
            pltpu.VMEM((heads, 2 * rows, 128), F32),
            pltpu.VMEM((2, rows, 2 * rows), F32),
            pltpu.VMEM((2, rows, 128), F32),
            pltpu.VMEM((heads // 2, 2 * rows, 128), F32),
            pltpu.VMEM((heads // 2, 2 * rows, 128), BF16),
            pltpu.VMEM((heads // 2, rows, 128), BF16),
            pltpu.VMEM((8, width), F32),
            pltpu.VMEM((2, rows, 128), F32),
            pltpu.SemaphoreType.DMA((9,)),
            pltpu.SemaphoreType.DMA((9,)),
            pltpu.SemaphoreType.DMA((8,)),
        ],
        compiler_params=pltpu.CompilerParams(
            collective_id=0, has_side_effects=True, vmem_limit_bytes=VMEM_LIMIT
        ),
        name="attention_forward",
    )(tokens, seg, live, coords, *norm_vectors, t_rows, t_cols, w_qkv)


def norm_stats(values):
    average = jnp.mean(values, axis=-1, keepdims=True)
    centered = values - average
    scale = lax.rsqrt(jnp.mean(centered * centered, axis=-1, keepdims=True) + EPS)
    return centered * scale, scale


def norm_back(grad, hat, scale, gain):
    e = grad * gain
    return scale * (
        e
        - jnp.mean(e, axis=-1, keepdims=True)
        - hat * jnp.mean(e * hat, axis=-1, keepdims=True)
    )


def back_kernel(
    n_dp, att_low, tokens, grad_out, live, ln1_gain, b_out, scale_attn, ln2_gain, ln2_bias, b_fc2, scale_mlp, b_fc1,
    w_out_hbm, w_fc1_hbm, w_fc2_hbm, q_hbm, k_hbm, v_hbm,
    a_hbm, n_hbm, w_hbm,
    out, g_tokens, sum_qkv, sum_out, sum_fc1, sum_fc2, early, late,
    q_aug, k_aug, v_aug, att, nrm, g_att, g_rows, half_in,
    dkv_out, dkv_in,
    c1, c2, c3, p1, y1, y2, y3, yq, z1, z2, z3, zq, xo1, xo2, xo3, xoq, xi1, xi2, xi3, xiq, gi1, gi2, gi3, giq,
    wq, va, vb, vc, vectors,
    cs, cr, ps, pr, ys, yr, zs, zr, xs, xr, gs, gr, vas, var, vbs, vbr, vcs, vcr, ss, sr, lsem,
):
    rows, width = tokens.shape
    head_dim = 64
    pairs = dkv_out.shape[0]
    heads = 2 * pairs
    cols = heads * head_dim
    span = 2 * rows
    dp, x, c = place()
    y, m = dp % 2, dp // 2
    peers_z = n_dp // 2
    sibling = (dp, x * 2 + 1 - c)
    across = (dp, (1 - x) * 2 + c)
    beside = (dp + 1 - 2 * y, x * 2 + c)
    mine = pl.ds(at128(c * cols), cols)
    theirs = pl.ds(at128((1 - c) * cols), cols)
    steps = w_fc1_hbm.shape[1] // width

    units = {}
    for j in range(2):
        units["1", j] = (c1.at[2 * j + x], y1.at[j], z1.at[j], xo1.at[j], xi1.at[j], gi1.at[j, 0], j, j)
    units["2", 0] = (None, y2, z2, xo2, xi2, gi2, None, 4)
    units["3", 0] = (c3, y3, z3, xo3, xi3, gi3, 8, 5)
    for t in range(pairs):
        units["q", t] = (wq.at[t], yq.at[t], zq.at[t], xoq.at[t], xiq.at[t], giq.at[t], 9 + t, 6 + t)

    def pair_copy(pair):
        return remote(c1.at[2 * pair + 1 - x], p1.at[pair], (ps, pr), pair, across)

    def pair_done(pair):
        pair_copy(pair).wait()
        c1[2 * pair + x] = c1[2 * pair + x] + p1[pair]
        y_copy(("1", pair)).start()

    def y_copy(key):
        if key[0] == "2":
            size = n_dp // 8
            chunk = key[1]
            src = c2.at[chunk, :, pl.ds(1 - y, 1)]
            dst = y2.at[pl.ds(chunk * size, size)]
            return remote(src, dst, (ys, yr), 4 + chunk, beside)
        unit = units[key]
        return remote(unit[0].at[:, pl.ds(1 - y, 1)], unit[1], (ys, yr), unit[6], beside)

    def y_done(key):
        y_copy(key).wait_recv()
        if key[0] == "2":
            size = n_dp // 8
            here = pl.ds(key[1] * size, size)
            y2[here] = y2[here] + c2[key[1], :, pl.ds(y, 1)]
        else:
            unit = units[key]
            unit[1][...] = unit[1][...] + unit[0][:, pl.ds(y, 1)]

    def z_copy(key, i):
        unit = units[key]
        to = (m + i) % peers_z
        return remote(
            unit[1].at[to], unit[2].at[i - 1], (zs.at[unit[7]], zr.at[unit[7]]), i - 1, (2 * to + y, x * 2 + c)
        )

    def z_copies(key):
        return [z_copy(key, i) for i in range(1, peers_z)]

    def z_send(key):
        for copy in z_copies(key):
            copy.start()

    def z_send_chunk(chunk):
        size = n_dp // 8
        for i in range(size):
            to = chunk * size + i

            @pl.when(m != to)
            def _(to=to):
                z_copy(("2", 0), (to - m + peers_z) % peers_z).start()

    def z_done(key):
        unit = units[key]
        for copy in z_copies(key):
            copy.wait_recv()
        total = unit[1][m, 0].astype(F32)
        for i in range(peers_z - 1):
            total = total + unit[2][i, 0].astype(F32)
        unit[3][...] = total.astype(BF16)
        if key[0] == "1":
            g_copy(key).start()

    def x_copy(key):
        unit = units[key]
        return remote(unit[3], unit[4], (xs, xr), unit[7], across)

    def g_copy(key):
        unit = units[key]
        return remote(unit[3] if key[0] == "1" else unit[4], unit[5], (gs, gr), unit[7], sibling)

    def second_copy(pair):
        return remote(xi1.at[pair], gi1.at[pair, 1], (gs, gr), 2 + pair, sibling)

    def x_done(key):
        unit = units[key]
        x_copy(key).wait_recv()
        if key[0] == "1":
            second_copy(key[1]).start()
            return
        unit[4][...] = (unit[3][...].astype(F32) + unit[4][...].astype(F32)).astype(BF16)
        g_copy(key).start()

    def g_done(key):
        unit = units[key]
        g_copy(key).wait_recv()
        if key[0] == "1":
            second_copy(key[1]).wait_recv()
            for chip, who, ref in (
                (x, c, unit[3]), (1 - x, c, unit[4]), (x, 1 - c, unit[5]), (1 - x, 1 - c, gi1.at[key[1], 1])
            ):
                where = pl.ds(at128((2 * key[1] + chip) * width + who * cols), cols)
                sum_fc1[:, where] = ref[...]
            return
        for value, who in ((unit[4], c), (unit[5], 1 - c)):
            full = value[...]
            if key[0] == "2":
                sum_fc2[:, pl.ds(at128(who * cols), cols)] = full
            elif key[0] == "3":
                sum_out[:, pl.ds(at128(who * cols), cols)] = full
            else:
                for i in range(3):
                    where = pl.ds(at128(i * width + who * cols + key[1] * 128), 128)
                    sum_qkv[:, where] = full[:, i * 128 : (i + 1) * 128]

    quad = x * 2 + y

    def quad_copies(kind, size):
        copies = []
        for i in range(1, 4):
            to_x = x if i < 2 else 1 - x
            to_y = y if i % 2 == 0 else 1 - y
            here = va.at[kind, quad, pl.ds(0, size)]
            copies.append(remote(here, here, (vas.at[kind], var.at[kind]), i - 1, (2 * m + to_y, to_x * 2 + c)))
        return copies

    def line_copies(kind, size):
        copies = []
        for i in range(1, peers_z):
            here = vb.at[kind, m, pl.ds(0, size)]
            to = (m + i) % peers_z
            copies.append(remote(here, here, (vbs.at[kind], vbr.at[kind]), i - 1, (2 * to + y, x * 2 + c)))
        return copies

    def last_copy(kind, size):
        return remote(
            vc.at[kind, 0, pl.ds(0, size)], vc.at[kind, 1, pl.ds(0, size)], (vcs, vcr), kind, sibling
        )

    def quad_send(kind, size):
        for copy in quad_copies(kind, size):
            copy.start()

    def quad_done(kind, size):
        for copy in quad_copies(kind, size):
            copy.wait_recv()
        total = va[kind, 0, :size]
        for i in range(1, 4):
            total = total + va[kind, i, :size]
        vb[kind, m, :size] = total
        for copy in line_copies(kind, size):
            copy.start()

    def line_done(kind, size):
        for copy in line_copies(kind, size):
            copy.wait_recv()
        total = vb[kind, 0, :size]
        for i in range(1, peers_z):
            total = total + vb[kind, i, :size]
        vc[kind, 0, :size] = total
        last_copy(kind, size).start()

    def early_done():
        last_copy(0, 16).wait_recv()
        early[...] = vc[0, 0] + vc[0, 1]

    def late_done():
        last_copy(1, 8).wait_recv()
        ours, other_core = vc[1, 0, :8], vc[1, 1, :8]
        late[:8] = jnp.where(c == 0, ours, other_core)
        late[8:] = jnp.where(c == 0, other_core, ours)
        late[:2] = ours[:2] + other_core[:2]

    def load_pair(t, slot):
        copies = []
        for i, (src, dst) in enumerate(((q_hbm, q_aug), (k_hbm, k_aug), (v_hbm, v_aug))):
            copies.append(
                pltpu.make_async_copy(src.at[pl.ds(2 * t, 2)], dst.at[slot], lsem.at[3 * slot + i])
            )
        return copies

    plain = [
        pltpu.make_async_copy(a_hbm, att, lsem.at[6]),
        pltpu.make_async_copy(n_hbm.at[pl.ds(0, span)], nrm, lsem.at[7]),
    ]
    peers = [sibling, across, beside, (dp + 1 - 2 * y, (1 - x) * 2 + c)] + [(2 * ((m + i) % peers_z) + y, x * 2 + c) for i in range(1, peers_z)]
    announce(peers)

    row = lambda i: vectors[i : i + 1, :]
    live_col = column_of(live[...].astype(F32))
    def dense(w_out, w_fc1, w_fc2, w1, w2, w3, branch_attn, normed_s, g_mlp_s, branch_mlp, g_normed, hidden_s, g_pre_s, dsem):
        def load_chunk(j, slot):
            return [
                pltpu.make_async_copy(w_fc1_hbm.at[:, pl.ds(at128(j * width), width)], w_fc1.at[slot], dsem.at[slot]),
                pltpu.make_async_copy(
                    w_fc2_hbm.at[pl.ds(pl.multiple_of(j * width, width), width)], w_fc2.at[slot], dsem.at[2 + slot]
                ),
            ]

        load_out = pltpu.make_async_copy(w_out_hbm, w_out, dsem.at[4])
        load_out.start()
        for copy in load_chunk(0, 0):
            copy.start()
        for copy in load_pair(0, 0) + plain:
            copy.start()
        for i, vector in (
            (LN1_GAIN, ln1_gain), (B_OUT, b_out), (SCALE_ATTN, scale_attn), (LN2_GAIN, ln2_gain), (LN2_BIAS, ln2_bias),
            (B_FC2, b_fc2), (SCALE_MLP, scale_mlp),
        ):
            vectors[i : i + 1, :] = vector[...].astype(F32).reshape(1, width)
        for i in range(steps):
            vectors[B_FC1 + i : B_FC1 + i + 1, :] = b_fc1[i * width : (i + 1) * width].astype(F32).reshape(1, width)
        source = tokens[...].astype(F32)
        g_mlp = (grad_out[...].astype(F32) * (live_col * row(SCALE_MLP))).astype(BF16)
        g_mlp_s[...] = g_mlp
        sums = va.at[0, quad]
        sums[...] = jnp.zeros_like(sums)
        sums[4:5, :] = jnp.sum(g_mlp.astype(F32), axis=0, keepdims=True)
        sums[10:11, :] = jnp.sum(live_col * source * source, axis=0, keepdims=True)
        sums[13:14, :] = jnp.broadcast_to(jnp.sum(live_col, axis=0, keepdims=True), (1, width))
        load_out.wait()
        branch = dot(att_low[...], w_out[...]) + row(B_OUT)
        branch_attn[...] = branch
        part = live_col * row(SCALE_ATTN) * branch
        stream = source + part
        g_tokens[...] = stream
        sums[11:12, :] = jnp.sum(part * part, axis=0, keepdims=True)
        hat, unused = norm_stats(stream)
        normed_s[...] = (hat * row(LN2_GAIN) + row(LN2_BIAS)).astype(BF16)
        branch_mlp[...] = jnp.zeros_like(branch_mlp)
        g_normed[...] = jnp.zeros_like(g_normed)

        def core_copies(j):
            return [
                remote(w1.at[1 - c], c1.at[j], (cs, cr), j, sibling),
                remote(w2.at[1 - c], c2.at[j], (cs, cr), 4 + j, sibling),
            ]

        def core_done(j):
            for copy in core_copies(j):
                copy.wait()
            c2[j] = c2[j] + w2[c]
            size = n_dp // 8
            remote(
                c2.at[j, :, pl.ds(1 - y, 1)], y2.at[pl.ds(j * size, size)], (ys, yr), 4 + j, beside
            ).start()
            c1[j] = c1[j] + w1[c]
            for pair in range(2):

                @pl.when(j == 2 * pair + 1)
                def _(pair=pair):
                    pair_copy(pair).start()

        def chunk(j, unused):
            slot = j % 2
            for copy in load_chunk(j, slot):
                copy.wait()

            @pl.when(j + 1 < steps)
            def _():
                for copy in load_chunk(j + 1, 1 - slot):
                    copy.start()

            bias = vectors[pl.ds(B_FC1 + j, 1), :]
            third = width // 3
            slopes = []
            for i in range(3):
                here = slice(i * third, (i + 1) * third)
                u = dot(normed_s[...], w_fc1[slot, :, here]) + bias[:, here]
                square = u * u
                t = jnp.tanh(u * (GELU_A + GELU_A * GELU_B * square))
                hidden_s[:, here] = (0.5 * u * (1.0 + t)).astype(BF16)
                slope = 0.5 * (1.0 + t) + (0.5 * u) * (1.0 - t * t) * (GELU_A + (3.0 * GELU_A * GELU_B) * square)
                g_pre = (dot(g_mlp_s[...], w_fc2[slot, here, :], NT) * slope).astype(BF16)
                g_pre_s[:, here] = g_pre
                slopes.append(jnp.sum(g_pre.astype(F32), axis=0, keepdims=True))
            sums[pl.ds(6 + j, 1), :] = jnp.concatenate(slopes, axis=1)

            @pl.when(j > 0)
            def _():
                core_done(j - 1)

            @pl.when(j == steps - 1)
            def _():
                y_done(("2", 0))
                z_send_chunk(0)

            spread_halves(w2, dot(hidden_s[...], g_mlp_s[...], TN))
            spread_halves(w1, dot(normed_s[...], g_pre_s[...], TN))
            for copy in core_copies(j):
                copy.start()
            branch_mlp[...] += dot(hidden_s[...], w_fc2[slot])
            g_normed[...] += dot(g_pre_s[...], w_fc1[slot], NT)
            return unused

        meet(peers)
        lax.fori_loop(0, steps, chunk, 0)
        y_done(("2", 1))
        z_send_chunk(1)
        grad = grad_out[...].astype(F32)
        branch = branch_mlp[...] + row(B_FC2)
        part = live_col * row(SCALE_MLP) * branch
        stream = g_tokens[...]
        out[...] = (stream + part).astype(BF16)
        sums[12:13, :] = jnp.sum(part * part, axis=0, keepdims=True)
        sums[5:6, :] = jnp.sum(grad * live_col * branch, axis=0, keepdims=True)
        hat, scale = norm_stats(stream)
        g_n2 = g_normed[...]
        sums[2:3, :] = jnp.sum(g_n2 * hat, axis=0, keepdims=True)
        sums[3:4, :] = jnp.sum(g_n2, axis=0, keepdims=True)
        g_tokens[...] = grad + norm_back(g_n2, hat, scale, row(LN2_GAIN))
        gated = g_tokens[...] * live_col
        g_attn = (gated * row(SCALE_ATTN)).astype(BF16)
        g_att[...] = dot(g_attn, w_out[...], NT).astype(BF16)
        swap.start()
        core_done(jnp.int32(steps - 1))
        sums[1:2, :] = jnp.sum(gated * branch_attn[...], axis=0, keepdims=True)
        sums[0:1, :] = jnp.sum(g_attn.astype(F32), axis=0, keepdims=True)
        quad_send(0, 16)
        spread_halves(w3, dot(att_low[...], g_attn, TN))
        give = remote(w3.at[1 - c], c3, (cs, cr), 8, sibling)
        give.start()
        pair_done(0)
        give.wait()
        c3[...] = c3[...] + w3[c]
        y_copy(("3", 0)).start()

    def spread_rows(ref, value):
        size = ref.shape[-2]
        for i in range(ref.shape[0]):
            for k in range(2):
                ref[i, k] = value[(2 * i + k) * size : (2 * i + k + 1) * size].astype(BF16)

    def spread_halves(ref, value):
        for half in range(2):
            spread_rows(ref.at[half], value[:, half * cols : (half + 1) * cols])

    own = pl.ds(pl.multiple_of(c * rows, rows), rows)
    other = pl.ds(pl.multiple_of((1 - c) * rows, rows), rows)
    swap = remote(g_att.at[:, theirs], g_rows.at[own], (ss, sr), 0, sibling)
    part_rows = width // n_dp
    wide_rows = w_fc2_hbm.shape[0] // n_dp
    pl.run_scoped(
        dense,
        pltpu.VMEM((width, width), BF16),
        pltpu.VMEM((2, width, width), BF16),
        pltpu.VMEM((2, width, width), BF16),
        pltpu.VMEM((2, peers_z, 2, part_rows, cols), BF16),
        pltpu.VMEM((2, n_dp // 8, 2, wide_rows, cols), BF16),
        pltpu.VMEM((2, peers_z, 2, part_rows, cols), BF16),
        pltpu.VMEM((rows, width), F32),
        pltpu.VMEM((rows, width), BF16),
        pltpu.VMEM((rows, width), BF16),
        pltpu.VMEM((rows, width), F32),
        pltpu.VMEM((rows, width), F32),
        pltpu.VMEM((rows, width), BF16),
        pltpu.VMEM((rows, width), BF16),
        pltpu.SemaphoreType.DMA((5,)),
    )

    def attention(g_aug, dq, dkv, dkv_own, d_query, d_key, d_value, w_own):
        late_loads = [
            pltpu.make_async_copy(
                w_hbm.at[:, pl.ds(at128(part * width + c * cols), cols)], w_own.at[part], lsem.at[8 + part]
            )
            for part in range(3)
        ]
        for copy in late_loads:
            copy.start()
        g_rows[own] = g_att[:, mine]
        for copy in plain:
            copy.wait()
        swap.wait_recv()
        spot = lanes((span, 128))
        low = spot < head_dim
        for t in range(pairs):
            g = g_rows[:, t * 128 : (t + 1) * 128].astype(F32)
            product = g * att[t]
            for odd in range(2):
                delta = jnp.sum(jnp.where(low if odd == 0 else ~low, product, 0.0), axis=1, keepdims=True)
                tile = g if odd == 0 else pltpu.roll(g, 64, 1)
                tile = jnp.where(low, tile, 0.0)
                for i, piece in enumerate(split3(delta)):
                    tile = jnp.where(spot == 64 + i, -piece, tile)
                g_aug[2 * t + odd] = tile.astype(BF16)
        lane = lanes((256, 256))
        line = lax.broadcasted_iota(jnp.int32, (256, 256), 0)
        in_rows = (lane >= ROW0) & (lane < COL0) & (line >= ROW0) & (line < COL0)
        in_cols = (lane >= COL0) & (lane < SEG0) & (line >= COL0) & (line < SEG0)
        flip = jnp.where(lane + line == 255, 1.0, 0.0).astype(BF16)
        sums = va.at[1, quad]
        sums[...] = jnp.zeros_like(sums)
        block = rows

        def dkv_copy(t, odd):
            return remote(dkv_out.at[t, odd], dkv_in.at[t, odd], (ss, sr), 1 + 2 * t + odd, across)

        def finish_pair(t):
            for odd in range(2):
                dkv_copy(t, odd).wait_recv()
            first, second = (dkv_own[t % 2, odd] + dkv_in[t, odd].astype(F32) for odd in range(2))
            place_k = pl.ds(at128(t * 128), 128)
            dkv[0, :, place_k] = jnp.where(low, first, pltpu.roll(second, 64, 1)).astype(BF16)
            dkv[1, :, place_k] = jnp.where(low, pltpu.roll(first, 64, 1), second).astype(BF16)
            both = jnp.concatenate([dkv[0, :, place_k], dkv[1, :, place_k]], axis=1)
            part = jnp.concatenate([dq[:, place_k], both], axis=1)
            spread_rows(wq.at[t], dot(nrm[...], part, TN))
            y_copy(("q", t)).start()

        plan = {
            0: [lambda: y_done(("2", 2)), lambda: z_send_chunk(2)],
            2: [lambda: y_done(("2", 3)), lambda: z_send_chunk(3)],
            4: [lambda: pair_done(1)],
            5: [
                lambda: y_done(("1", 0)), lambda: z_send(("1", 0)), lambda: y_done(("3", 0)), lambda: z_send(("3", 0)),
            ],
            6: [lambda: finish_pair(0), lambda: quad_done(0, 16)],
            7: [lambda: y_done(("1", 1)), lambda: z_send(("1", 1))],
            9: [lambda: finish_pair(1), lambda: y_done(("q", 0)), lambda: z_send(("q", 0))],
            10: [
                lambda: z_done(("1", 0)),
                lambda: x_copy(("1", 0)).start(), lambda: z_done(("3", 0)), lambda: x_copy(("3", 0)).start(),
            ],
            11: [
                lambda: y_done(("q", 1)), lambda: z_send(("q", 1)), lambda: line_done(0, 16), lambda: z_done(("2", 0)),
            ],
        }

        def sweep(point, unused):
            it, odd = point // 2, point % 2
            part = 1 - it % 2
            t = it // 2
            slot = t % 2

            @pl.when((part == 1) & (odd == 0))
            def _():
                for copy in load_pair(t, slot):
                    copy.wait()

            @pl.when((part == 1) & (odd == 0) & (t + 1 < pairs))
            def _():
                for copy in load_pair(t + 1, 1 - slot):
                    copy.start()

            @pl.when(part == 1)
            def _():
                d_query[odd] = jnp.zeros(d_query.shape[1:], F32)

            for qb in range(span // block):
                here = slice(qb * block, (qb + 1) * block)
                queries, grads = q_aug[slot, odd, here, :], g_aug[2 * t + odd, here, :]
                total = d_query[odd, :, here]
                for kb in range(span // block):
                    there = slice(kb * block, (kb + 1) * block)
                    source = pl.ds(pl.multiple_of(part * span + kb * block, block), block)
                    keys = k_aug[slot, odd, source, :]
                    p = jnp.exp(dot(keys, queries, NT))
                    p_low = p.astype(BF16)
                    ds = (p * dot(v_aug[slot, odd, source, :], grads, NT)).astype(BF16)
                    gain_value = dot(p_low, grads)
                    gain_key = dot(ds, queries[:, :128])
                    if qb == 0:
                        d_value[odd, there, :] = gain_value
                        d_key[odd, there, :] = gain_key
                    else:
                        d_value[odd, there, :] += gain_value
                        d_key[odd, there, :] += gain_key
                    total = total + dot(keys, ds, TN)
                d_query[odd, :, here] = total
            new = jnp.where(low, d_key[odd], pltpu.roll(d_value[odd], 64, 1))

            @pl.when(part == 1)
            def _():
                dkv_out[t, odd] = new.astype(BF16)
                dkv_copy(t, odd).start()

            @pl.when(part == 0)
            def _():
                dkv_own[t % 2, odd] = new
                square = dot(d_query[odd].astype(BF16), k_aug[slot, odd, :span, :])
                h = 2 * t + odd
                for table, mask in enumerate((in_rows, in_cols)):
                    flipped = sum(dot(flip, piece.astype(BF16)) for piece in split3(jnp.where(mask, square, 0.0)))
                    turned = pltpu.roll(flipped, 0, 1, stride=1, stride_axis=0)
                    sums[pl.ds(3 + table * 2 + h // 3, 1), pl.ds(at128(h % 3 * 256), 256)] = jnp.sum(
                        turned, axis=0, keepdims=True
                    )

            @pl.when((part == 0) & (odd == 1))
            def _():
                both = jnp.concatenate([d_query[0, :head_dim, :], d_query[1, :head_dim, :]], axis=0)
                dq[:, pl.ds(at128(t * 128), 128)] = (jnp.transpose(both) * head_dim ** (-0.5)).astype(BF16)

            for i, acts in plan.items():

                @pl.when(point == i)
                def _(acts=acts):
                    for act in acts:
                        act()

            return unused

        lax.fori_loop(0, 4 * pairs, sweep, 0)
        last = pairs - 1
        finish_pair(last)
        for copy in late_loads:
            copy.wait()

        def through(where):
            total = dot(dq[where, :], w_own[0], NT)
            return total + dot(dkv[0, where, :], w_own[1], NT) + dot(dkv[1, where, :], w_own[2], NT)

        swap.wait_send()
        g_att[...] = through(other).astype(BF16)
        give = remote(g_att, half_in, (ss, sr), 1 + 2 * pairs, sibling)
        give.start()
        z_done(("q", 0))
        x_copy(("q", 0)).start()
        sums[2:3, :cols] = jnp.sum(dq[...].astype(F32), axis=0, keepdims=True)
        sums[2:3, cols:] = jnp.sum(dkv[1].astype(F32), axis=0, keepdims=True)
        g_n1 = through(own)
        hat, scale = norm_stats(tokens[...].astype(F32))
        give.wait_recv()
        g_n1 = g_n1 + half_in[...].astype(F32)
        sums[0:1, :] = jnp.sum(g_n1 * hat, axis=0, keepdims=True)
        sums[1:2, :] = jnp.sum(g_n1, axis=0, keepdims=True)
        quad_send(1, 8)
        y_done(("q", last))
        z_send(("q", last))
        x_copy(("2", 0)).start()
        z_done(("1", 1))
        x_copy(("1", 1)).start()
        g_tokens[...] = g_tokens[...] + norm_back(g_n1, hat, scale, row(LN1_GAIN))
        x_done(("3", 0))
        x_done(("1", 0))
        quad_done(1, 8)
        z_done(("q", 1))
        x_copy(("q", 1)).start()
        x_done(("2", 0))
        x_done(("1", 1))
        x_done(("q", 0))
        early_done()
        g_done(("3", 0))
        g_done(("1", 0))
        z_done(("q", last))
        x_copy(("q", last)).start()
        line_done(1, 8)
        g_done(("2", 0))
        g_done(("1", 1))
        g_done(("q", 0))
        x_done(("q", 1))
        x_done(("q", last))
        late_done()
        g_done(("q", 1))
        g_done(("q", last))
        give.wait_send()
        for t in range(pairs):
            for odd in range(2):
                dkv_copy(t, odd).wait_send()

    pl.run_scoped(
        attention,
        pltpu.VMEM((heads, span, 128), BF16),
        pltpu.VMEM((span, cols), BF16),
        pltpu.VMEM((2, span, cols), BF16),
        pltpu.VMEM((2, 2, span, 128), F32),
        pltpu.VMEM((2, 256, span), F32),
        pltpu.VMEM((2, span, 128), F32),
        pltpu.VMEM((2, span, 128), F32),
        pltpu.VMEM((3, width, cols), BF16),
    )
    for key in units:
        if key[0] != "2":
            y_copy(key).wait_send()
        for copy in z_copies(key):
            copy.wait_send()
        x_copy(key).wait_send()
        g_copy(key).wait_send()
    for j in range(4):
        y_copy(("2", j)).wait_send()
    for pair in range(2):
        second_copy(pair).wait_send()
    for kind, size in enumerate((16, 8)):
        for copy in quad_copies(kind, size) + line_copies(kind, size) + [last_copy(kind, size)]:
            copy.wait_send()


def backward(n_dp, att_low, tokens, grad_out, live, vectors, w_out, w_fc1, w_fc2, q_aug, k_aug, v_aug, att, nrm, w_qkv):
    rows, width = tokens.shape
    heads = q_aug.shape[0]
    pairs, cols = heads // 2, heads * 64
    span, group = 2 * rows, 4 * rows
    hidden = w_fc1.shape[1]
    steps = hidden // width
    z, part, wide = n_dp // 2, width // n_dp, hidden // n_dp
    any_spec = pl.BlockSpec(memory_space=pl.ANY)
    vmem = pl.BlockSpec(memory_space=pltpu.VMEM)
    low = lambda *shape: pltpu.VMEM(shape, BF16)
    full = lambda *shape: pltpu.VMEM(shape, F32)
    dma = lambda *shape: pltpu.SemaphoreType.DMA(shape)
    received = lambda *lead: [low(2, *lead, part, cols), low(wide, cols), low(part, cols), low(pairs, part, cols)]
    return pl.pallas_call(
        functools.partial(back_kernel, n_dp),
        out_shape=[
            jax.ShapeDtypeStruct((rows, width), BF16),
            jax.ShapeDtypeStruct((rows, width), F32),
            jax.ShapeDtypeStruct((part, 3 * width), BF16),
            jax.ShapeDtypeStruct((part, width), BF16),
            jax.ShapeDtypeStruct((part, hidden), BF16),
            jax.ShapeDtypeStruct((wide, width), BF16),
            jax.ShapeDtypeStruct((16, width), F32),
            jax.ShapeDtypeStruct((16, width), F32),
        ],
        in_specs=[vmem] * 12 + [any_spec] * 9,
        out_specs=[vmem] * 8,
        scratch_shapes=[
            low(2, 2, span, 256), low(2, 2, group, 256), low(2, 2, group, 128),
            full(pairs, span, 128), low(span, width),
            low(rows, width), low(span, cols), low(rows, width),
            low(pairs, 2, span, 128), low(pairs, 2, span, 128),
            low(steps, z, 2, part, cols), low(steps, n_dp // 8, 2, wide, cols), low(z, 2, part, cols),
            low(2, z, 2, part, cols),
            low(2, z, 1, part, cols), low(z, 1, wide, cols), low(z, 1, part, cols), low(pairs, z, 1, part, cols),
            low(2, z - 1, 1, part, cols), low(z - 1, 1, wide, cols), low(z - 1, 1, part, cols),
            low(pairs, z - 1, 1, part, cols),
            *received(), *received(), *received(2),
            low(pairs, z, 2, part, cols), full(2, 4, 16, width), full(2, z, 16, width), full(2, 2, 16, width), full(16, width),
            dma(9), dma(9), dma(2), dma(2), dma(12), dma(12), dma(9, z - 1), dma(9, z - 1), dma(9), dma(9), dma(9), dma(9),
            dma(2, 3), dma(2, 3), dma(2, z - 1), dma(2, z - 1), dma(2), dma(2), dma(2 + 2 * pairs), dma(2 + 2 * pairs),
            dma(11),
        ],
        compiler_params=pltpu.CompilerParams(
            collective_id=1, has_side_effects=True, vmem_limit_bytes=VMEM_LIMIT
        ),
        name="backward",
    )(att_low, tokens, grad_out, live, *vectors, w_out, w_fc1, w_fc2, q_aug, k_aug, v_aug, att, nrm, w_qkv)


def outputs_kernel(out_in, tokens_in, qkv_in, out_w_in, fc1_in, fc2_in, early, late, *refs):
    (
        out, g_tokens, g_ln1, b_ln1, qkv, b_query, b_value, out_w, b_out, s_attn, g_ln2, b_ln2, fc1, b_fc1, fc2,
        b_fc2, s_mlp, t_rows, t_cols, means,
    ) = refs
    width = out.shape[1]
    out[...] = out_in[...]
    g_tokens[...] = tokens_in[...]
    for ref, value in ((qkv, qkv_in), (out_w, out_w_in), (fc1, fc1_in), (fc2, fc2_in)):
        ref[...] = value[...].astype(F32)
    for i, ref in enumerate((b_out, s_attn, g_ln2, b_ln2, b_fc2, s_mlp)):
        ref[...] = early[i, :]
    for i in range(b_fc1.shape[0] // width):
        b_fc1[i * width : (i + 1) * width] = early[6 + i, :]
    g_ln1[...] = late[0, :]
    b_ln1[...] = late[1, :]
    half = width // 2
    b_query[...] = jnp.concatenate([late[2:3, :half], late[10:11, :half]], axis=1)[0]
    b_value[...] = jnp.concatenate([late[2:3, half:], late[10:11, half:]], axis=1)[0]
    count = early[13:14, :1]
    lane = lanes((1, 3))
    squares = jnp.zeros((1, 3), F32)
    for i in range(3):
        squares = jnp.where(lane == i, jnp.sum(early[10 + i : 11 + i, :], axis=1, keepdims=True), squares)
    means[...] = jnp.sqrt(squares / (count * width))[0]
    spans = t_rows.shape[1]
    limit = (spans - 1) // 2
    offset = lax.broadcasted_iota(jnp.int32, (256, spans), 0) + 1
    offset = jnp.where(offset < 128, offset, offset - 256)
    pick = jnp.where(jnp.clip(offset, -limit, limit) + limit == lanes((256, spans)), 1.0, 0.0).astype(BF16)
    for third in range(3):
        part = late[:, third * 256 : (third + 1) * 256]
        sums = sum(dot(piece.astype(BF16), pick) for piece in split3(part))
        for i in range(8):
            core, table, group = i // 4, i // 2 % 2, i % 2
            head, source = core * 6 + group * 3 + third, core * 8 + 3 + table * 2 + group
            (t_rows, t_cols)[table][head : head + 1, :] = sums[source : source + 1, :]


def write_outputs(arrays, shapes):
    vmem = pl.BlockSpec(memory_space=pltpu.VMEM)
    return pl.pallas_call(
        outputs_kernel,
        out_shape=[jax.ShapeDtypeStruct(*shape) for shape in shapes],
        in_specs=[vmem] * len(arrays),
        out_specs=[vmem] * len(shapes),
        compiler_params=pltpu.CompilerParams(vmem_limit_bytes=VMEM_LIMIT),
        name="outputs",
    )(*arrays)


def body(
    tokens, grad_out, segment, live_rows, coords, ln1_gain, ln1_bias, w_qkv, b_query, b_value, w_out,
    b_out, scale_attn, ln2_gain, ln2_bias, w_fc1, b_fc1, w_fc2, b_fc2, scale_mlp, table_rows, table_cols,
):
    rows, width = tokens.shape
    heads = table_rows.shape[0] // 2
    line = lambda v: v.reshape(1, -1)
    live = line(live_rows)
    att_low, q_aug, k_aug, v_aug, att, nrm = forward_attention(
        tokens, line(segment), live, coords, (ln1_gain, ln1_bias, b_query, b_value), table_rows, table_cols, w_qkv
    )
    out, g_tokens, sum_qkv, sum_out, sum_fc1, sum_fc2, early, late = backward(
        lax.axis_size("dp"), att_low, tokens, grad_out, live,
        (ln1_gain, b_out, scale_attn, ln2_gain, ln2_bias, b_fc2, scale_mlp, b_fc1), w_out, w_fc1, w_fc2,
        q_aug, k_aug, v_aug, att, nrm, w_qkv,
    )
    part, hidden = sum_out.shape[0], w_fc1.shape[1]
    vector, table = ((width,), F32), (table_rows.shape, F32)
    return write_outputs(
        (out, g_tokens, sum_qkv, sum_out, sum_fc1, sum_fc2, early, late),
        [
            ((rows, width), BF16), ((rows, width), F32), vector, vector, ((part, 3 * width), F32), vector, vector,
            ((part, width), F32), vector, vector, vector, vector, ((part, hidden), F32), ((hidden,), F32),
            (sum_fc2.shape, F32), vector, vector, table, table, ((3,), F32),
        ],
    )


def solution(mesh):
    rows = P(("dp", "blk"), None)
    flat = P(("dp", "blk"))
    return jax.shard_map(
        body,
        mesh=mesh,
        in_specs=(rows, rows, flat, flat, P(None, ("dp", "blk"))) + (P(),) * 17,
        out_specs=(
            rows, rows, P(), P(), P("dp", None), P(), P(), P("dp", None), P(), P(), P(), P(),
            P("dp", None), P(), P("dp", None), P(), P(), P(), P(), P(),
        ),
        check_vma=False,
    )
```

```python
import functools

import jax
import jax.numpy as jnp
from jax import lax
from jax.experimental import pallas as pl
from jax.experimental.pallas import tpu as pltpu
from jax.sharding import PartitionSpec as P

MESH = pl.DeviceIdType.MESH
BF16 = jnp.bfloat16
F32 = jnp.float32
EPS = 1e-06
MASKED = -1000000000.0
NT = ((1,), (1,))
TN = ((0,), (0,))
ROW0, COL0, SEG0, LIVE0, LSE0 = 64, 150, 236, 240, 241
VMEM_LIMIT = 63 << 20
(LN1_GAIN, LN1_BIAS, B_QUERY, B_VALUE, B_OUT, SCALE_ATTN, LN2_GAIN, LN2_BIAS, B_FC2, SCALE_MLP, B_FC1) = range(11)
GELU_A, GELU_B = 0.7978845608, 0.044715


def dot(left, right, dims=((1,), (0,))):
    return lax.dot_general(left, right, (dims, ((), ())), preferred_element_type=F32)


def split3(value):
    high = value.astype(BF16).astype(F32)
    rest = value - high
    middle = rest.astype(BF16).astype(F32)
    return high, middle, rest - middle


def lanes(shape):
    return lax.broadcasted_iota(jnp.int32, shape, len(shape) - 1)


def column_of(row):
    return jnp.transpose(jnp.broadcast_to(row, (8, row.shape[1])))[:, :1]


def place():
    me = lax.axis_index("blk")
    return lax.axis_index("dp"), me // 2, me % 2


def announce(peers):
    barrier = pltpu.get_barrier_semaphore()
    for peer in peers:
        pl.semaphore_signal(barrier, inc=1, device_id=peer, device_id_type=MESH)


def meet(peers):
    pl.semaphore_wait(pltpu.get_barrier_semaphore(), len(peers))


def remote(src, dst, sems, index, peer):
    return pltpu.make_async_remote_copy(
        src_ref=src,
        dst_ref=dst,
        send_sem=sems[0].at[index],
        recv_sem=sems[1].at[index],
        device_id=peer,
        device_id_type=MESH,
    )


def at128(index):
    return pl.multiple_of(index, 128)


def forward_kernel(
    tokens, seg, live, coords, ln1_gain, ln1_bias, b_query, b_value, table_rows, table_cols, w_hbm,
    att_out, q_hbm, k_hbm, v_hbm, a_hbm, n_hbm,
    nrm, w_own, meta, squares, base, q_aug, k_aug, v_aug, acc, peak, score, top, att, att_low,
    att_in, vectors, alive_rows, rsend, rrecv, lsem,
):
    rows, width = tokens.shape
    heads, head_dim = q_aug.shape[0], 64
    cols = heads * head_dim
    dp, x, c = place()
    sibling = (dp, x * 2 + 1 - c)
    across = (dp, (1 - x) * 2 + c)
    diagonal = (dp, (1 - x) * 2 + 1 - c)
    rsem = (rsend, rrecv)
    announce([sibling, across, diagonal])
    loads = [
        pltpu.make_async_copy(
            w_hbm.at[:, pl.ds(at128(part * width + c * cols), cols)], w_own.at[part], lsem.at[part]
        )
        for part in range(3)
    ]
    for load in loads:
        load.start()

    for i, vector in enumerate((ln1_gain, ln1_bias, b_query, b_value)):
        vectors[i : i + 1, :] = vector[...].astype(F32).reshape(1, width)

    source = tokens[...].astype(F32)
    average = jnp.mean(source, axis=-1, keepdims=True)
    centered = source - average
    spread = jnp.mean(centered * centered, axis=-1, keepdims=True)
    normed = centered * lax.rsqrt(spread + EPS) * vectors[LN1_GAIN : LN1_GAIN + 1, :]
    normed = normed + vectors[LN1_BIAS : LN1_BIAS + 1, :]
    own = pl.ds(pl.multiple_of(c * rows, rows), rows)
    nrm[own] = normed.astype(BF16)
    meta[c] = jnp.concatenate(
        [seg[...], live[...], coords[...], jnp.zeros((4, rows), jnp.int32)], axis=0
    )
    meet([sibling, across, diagonal])
    half = rows // 2
    sends = [
        remote(meta.at[c], meta.at[c], rsem, 0, sibling),
        remote(meta.at[c], meta.at[2 + c], rsem, 1, across),
        remote(meta.at[c], meta.at[2 + c], rsem, 2, diagonal),
        remote(nrm.at[own], nrm.at[own], rsem, 3, sibling),
    ]
    pieces, forwards = [], []
    for i in range(2):
        mine = pl.ds(pl.multiple_of(c * rows + i * half, half), half)
        there = pl.ds(pl.multiple_of((2 + c) * rows + i * half, half), half)
        pieces.append(remote(nrm.at[mine], nrm.at[there], rsem, 4 + i, across))
        forwards.append(remote(nrm.at[there], nrm.at[there], rsem, 6 + i, sibling))
    for copy in sends + pieces:
        copy.start()

    spans = table_rows.shape[1]
    limit = (spans - 1) // 2
    offset = lanes((spans, 256))
    offset = jnp.where(offset < 128, offset, offset - 256)
    entry = lax.broadcasted_iota(jnp.int32, (spans, 256), 0)
    pick = jnp.where(jnp.clip(-offset, -limit, limit) + limit == entry, 1.0, 0.0).astype(BF16)
    base[0] = jnp.pad(dot(table_rows[...], pick), ((0, 4), (0, 0)))
    base[1] = jnp.pad(dot(table_cols[...], pick), ((0, 4), (0, 0)))
    lane = lanes((256, 256))
    line = lax.broadcasted_iota(jnp.int32, (256, 256), 0)
    in_rows = (lane >= ROW0) & (lane < COL0) & (line >= ROW0) & (line < COL0)
    in_cols = (lane >= COL0) & (lane < SEG0) & (line >= COL0) & (line < SEG0)
    keep = (lane == line) & (lane >= SEG0) & (lane <= LIVE0)

    def make_square(h, unused):
        shifted = [
            pltpu.roll(
                jnp.broadcast_to(base[i, pl.ds(c * heads + h, 1), :], (256, 256)),
                0, 1, stride=1, stride_axis=0,
            )
            for i in range(2)
        ]
        square = jnp.where(in_rows, shifted[0], jnp.where(in_cols, shifted[1], 0.0))
        squares[h] = jnp.where(keep, 1.0, square).astype(BF16)
        return unused

    lax.fori_loop(0, heads, make_square, 0)
    for load in loads:
        load.wait()
    own_cols = pl.ds(at128(c * cols), cols)
    query_bias = vectors[B_QUERY : B_QUERY + 1, own_cols]
    value_bias = vectors[B_VALUE : B_VALUE + 1, own_cols]

    low128 = lanes((rows, 128)) < head_dim

    def project(slot, queries):
        here = pl.ds(pl.multiple_of(slot * rows, rows), rows)
        info = jnp.transpose(meta[slot].astype(F32)).astype(jnp.int32)
        page, alive, r, col = (info[:, i : i + 1] for i in range(4))
        spot = lanes((rows, 256))
        hot = (spot == r + ROW0) | (spot == col + COL0)
        key_side = jnp.where(hot | ((spot >= LSE0) & (spot < LSE0 + 3)), 1.0, 0.0)
        other = (spot >= SEG0) & (spot < LIVE0) & (spot != page + SEG0)
        dead = (spot == LIVE0) & (alive <= 0)
        key_side = jnp.where(other | dead, MASKED, key_side)
        if queries:
            query_side = jnp.where(hot | (spot == page + SEG0) | (spot == LIVE0), 1.0, 0.0)
            query_side = query_side.astype(BF16)
        inputs = nrm[here]
        ones = jnp.where((spot[:, :128] >= 64) & (spot[:, :128] < 67), 1.0, 0.0)
        keys = dot(inputs, w_own[1])
        values = dot(inputs, w_own[2]) + value_bias
        if queries:
            query = (dot(inputs, w_own[0]) + query_bias) * head_dim ** (-0.5)
        for h in range(heads):
            tile = slice(h // 2 * 128, h // 2 * 128 + 128)
            turn = (lambda v: v) if h % 2 == 0 else (lambda v: pltpu.roll(v, 64, 1))
            k_aug[h, here, :128] = jnp.where(low128, turn(keys[:, tile]), key_side[:, :128]).astype(BF16)
            k_aug[h, here, 128:] = key_side[:, 128:].astype(BF16)
            v_aug[h, here, :] = jnp.where(low128, turn(values[:, tile]), ones).astype(BF16)
            if queries:
                extra = dot(query_side, squares[h])
                q_aug[h, here, :128] = jnp.where(low128, turn(query[:, tile]), extra[:, :128]).astype(BF16)
                q_aug[h, here, 128:] = extra[:, 128:].astype(BF16)

    project(c, True)
    for i in (0, 3):
        sends[i].wait_recv()
    project(1 - c, True)

    block = rows

    def score_of(h, qb, part, buf):
        s = dot(
            q_aug[h, qb * block : (qb + 1) * block, :],
            k_aug[h, part * 2 * rows : (part + 1) * 2 * rows, :],
            NT,
        )
        score[buf] = s
        top[buf] = jnp.broadcast_to(jnp.max(s, axis=1, keepdims=True), (block, 128))

    def weigh(h, qb, part, buf):
        here = slice(qb * block, (qb + 1) * block)
        m = top[buf]
        if part:
            before = peak[h, here, :]
            m = jnp.maximum(before, m)
        p = jnp.concatenate(
            [jnp.exp(score[buf, :, i : i + 128] - m).astype(BF16) for i in range(0, 2 * rows, 128)], axis=1
        )
        pv = dot(p, v_aug[h, part * 2 * rows : (part + 1) * 2 * rows, :])
        if not part:
            acc[h, here, :] = pv
            peak[h, here, :] = m
            return
        pv = pv + acc[h, here, :] * jnp.exp(before - m)
        total = jnp.broadcast_to(pv[:, 64:65], (block, 128))
        lse = jnp.where(alive_rows[qb] > 0, m + jnp.log(total), 0.0)
        value = pv / total
        tail = q_aug[h, here, 128:].astype(F32)
        for i, piece in enumerate(split3(lse)):
            tail = jnp.where(low_lane == LSE0 - 128 + i, -piece, tail)
        q_aug[h, here, 128:] = tail.astype(BF16)
        return value

    low_lane = lanes((block, 128))
    for qb in range(2):
        alive_rows[qb] = jnp.broadcast_to(column_of(meta[qb, 1:2, :].astype(F32)), (block, 128))

    def sweep(part, t, unused):
        order = [(0, 0), (0, 1), (1, 0), (1, 1)]
        for i, (odd, qb) in enumerate(order):
            if i < 3:
                score_of(2 * t + order[i + 1][0], order[i + 1][1], part, (i + 1) % 2)
            else:
                score_of(jnp.minimum(2 * t + 2, heads - 2), 0, part, 0)
            value = weigh(2 * t + odd, qb, part, i % 2)
            if part:
                here = slice(qb * block, (qb + 1) * block)
                if odd:
                    value = jnp.where(low128, att[t, here, :], pltpu.roll(value, 64, 1))
                att[t, here, :] = value
                if odd:
                    att_low[t, here, :] = value.astype(BF16)
        if not part:

            @pl.when(t == 1)
            def _():
                pieces[0].wait_recv()
                forwards[0].start()

        return unused

    score_of(0, 0, 0, 0)
    lax.fori_loop(0, heads // 2, functools.partial(sweep, 0), 0)
    pieces[1].wait_recv()
    forwards[1].start()
    sends[1].wait_recv()
    sends[2].wait_recv()
    project(2 + c, False)
    for copy in forwards:
        copy.wait_recv()
    project(3 - c, False)
    stores = [
        pltpu.make_async_copy(k_aug, k_hbm, lsem.at[3]),
        pltpu.make_async_copy(v_aug, v_hbm, lsem.at[4]),
        pltpu.make_async_copy(nrm, n_hbm, lsem.at[5]),
    ]
    for store in stores:
        store.start()
    score_of(0, 0, 1, 0)
    lax.fori_loop(0, heads // 2, functools.partial(sweep, 1), 0)
    stores += [
        pltpu.make_async_copy(q_aug, q_hbm, lsem.at[6]),
        pltpu.make_async_copy(att, a_hbm, lsem.at[7]),
    ]
    for store in stores[3:]:
        store.start()
    theirs = pl.ds(pl.multiple_of((1 - c) * rows, rows), rows)
    swap = remote(att_low.at[:, theirs, :], att_in, rsem, 8, sibling)
    swap.start()
    tiles = heads // 2
    for t in range(tiles):
        att_out[:, pl.ds(at128((c * tiles + t) * 128), 128)] = att_low[t, own, :]
    swap.wait_recv()
    for t in range(tiles):
        att_out[:, pl.ds(at128(((1 - c) * tiles + t) * 128), 128)] = att_in[t]
    for copy in sends + pieces + forwards + [swap]:
        copy.wait_send()
    for store in stores:
        store.wait()


def forward_attention(tokens, seg, live, coords, norm_vectors, t_rows, t_cols, w_qkv):
    rows, width = tokens.shape
    heads = t_rows.shape[0] // 2
    group = rows * 4
    any_spec = pl.BlockSpec(memory_space=pl.ANY)
    vmem = pl.BlockSpec(memory_space=pltpu.VMEM)
    return pl.pallas_call(
        forward_kernel,
        out_shape=[
            jax.ShapeDtypeStruct((rows, width), BF16),
            jax.ShapeDtypeStruct((heads, 2 * rows, 256), BF16),
            jax.ShapeDtypeStruct((heads, group, 256), BF16),
            jax.ShapeDtypeStruct((heads, group, 128), BF16),
            jax.ShapeDtypeStruct((heads // 2, 2 * rows, 128), F32),
            jax.ShapeDtypeStruct((group, width), BF16),
        ],
        in_specs=[vmem] * 10 + [any_spec],
        out_specs=[vmem] + [any_spec] * 5,
        scratch_shapes=[
            pltpu.VMEM((group, width), BF16),
            pltpu.VMEM((3, width, heads * 64), BF16),
            pltpu.VMEM((4, 8, rows), jnp.int32),
            pltpu.VMEM((heads, 256, 256), BF16),
            pltpu.VMEM((2, 16, 256), F32),
            pltpu.VMEM((heads, 2 * rows, 256), BF16),
            pltpu.VMEM((heads, group, 256), BF16),
            pltpu.VMEM((heads, group, 128), BF16),
            pltpu.VMEM((heads, 2 * rows, 128), F32),
            pltpu.VMEM((heads, 2 * rows, 128), F32),
            pltpu.VMEM((2, rows, 2 * rows), F32),
            pltpu.VMEM((2, rows, 128), F32),
            pltpu.VMEM((heads // 2, 2 * rows, 128), F32),
            pltpu.VMEM((heads // 2, 2 * rows, 128), BF16),
            pltpu.VMEM((heads // 2, rows, 128), BF16),
            pltpu.VMEM((8, width), F32),
            pltpu.VMEM((2, rows, 128), F32),
            pltpu.SemaphoreType.DMA((9,)),
            pltpu.SemaphoreType.DMA((9,)),
            pltpu.SemaphoreType.DMA((8,)),
        ],
        compiler_params=pltpu.CompilerParams(
            collective_id=0, has_side_effects=True, vmem_limit_bytes=VMEM_LIMIT
        ),
        name="attention_forward",
    )(tokens, seg, live, coords, *norm_vectors, t_rows, t_cols, w_qkv)


def norm_stats(values):
    average = jnp.mean(values, axis=-1, keepdims=True)
    centered = values - average
    scale = lax.rsqrt(jnp.mean(centered * centered, axis=-1, keepdims=True) + EPS)
    return centered * scale, scale


def norm_back(grad, hat, scale, gain):
    e = grad * gain
    return scale * (
        e
        - jnp.mean(e, axis=-1, keepdims=True)
        - hat * jnp.mean(e * hat, axis=-1, keepdims=True)
    )


def back_kernel(
    n_dp, att_low, tokens, grad_out, live, ln1_gain, b_out, scale_attn, ln2_gain, ln2_bias, b_fc2, scale_mlp, b_fc1,
    w_out_hbm, w_fc1_hbm, w_fc2_hbm, q_hbm, k_hbm, v_hbm,
    a_hbm, n_hbm, w_hbm,
    out, g_tokens, sum_qkv, sum_out, sum_fc1, sum_fc2, early, late,
    q_aug, k_aug, v_aug, att, nrm, g_att, g_rows, half_in,
    dkv_out, dkv_in,
    c1, c2, c3, p1, y1, y2, y3, yq, z1, z2, z3, zq, xo1, xo2, xo3, xoq, xi1, xi2, xi3, xiq, gi1, gi2, gi3, giq,
    wq, va, vb, vc, vectors,
    cs, cr, ps, pr, ys, yr, zs, zr, xs, xr, gs, gr, vas, var, vbs, vbr, vcs, vcr, ss, sr, lsem,
):
    rows, width = tokens.shape
    head_dim = 64
    pairs = dkv_out.shape[0]
    heads = 2 * pairs
    cols = heads * head_dim
    span = 2 * rows
    dp, x, c = place()
    y, m = dp % 2, dp // 2
    peers_z = n_dp // 2
    sibling = (dp, x * 2 + 1 - c)
    across = (dp, (1 - x) * 2 + c)
    beside = (dp + 1 - 2 * y, x * 2 + c)
    mine = pl.ds(at128(c * cols), cols)
    theirs = pl.ds(at128((1 - c) * cols), cols)
    steps = w_fc1_hbm.shape[1] // width

    units = {}
    for j in range(2):
        units["1", j] = (c1.at[2 * j + x], y1.at[j], z1.at[j], xo1.at[j], xi1.at[j], gi1.at[j, 0], j, j)
    units["2", 0] = (None, y2, z2, xo2, xi2, gi2, None, 4)
    units["3", 0] = (c3, y3, z3, xo3, xi3, gi3, 8, 5)
    for t in range(pairs):
        units["q", t] = (wq.at[t], yq.at[t], zq.at[t], xoq.at[t], xiq.at[t], giq.at[t], 9 + t, 6 + t)

    def pair_copy(pair):
        return remote(c1.at[2 * pair + 1 - x], p1.at[pair], (ps, pr), pair, across)

    def pair_done(pair):
        pair_copy(pair).wait()
        c1[2 * pair + x] = c1[2 * pair + x] + p1[pair]
        y_copy(("1", pair)).start()

    def y_copy(key):
        if key[0] == "2":
            size = n_dp // 8
            chunk = key[1]
            src = c2.at[chunk, :, pl.ds(1 - y, 1)]
            dst = y2.at[pl.ds(chunk * size, size)]
            return remote(src, dst, (ys, yr), 4 + chunk, beside)
        unit = units[key]
        return remote(unit[0].at[:, pl.ds(1 - y, 1)], unit[1], (ys, yr), unit[6], beside)

    def y_done(key):
        y_copy(key).wait_recv()
        if key[0] == "2":
            size = n_dp // 8
            here = pl.ds(key[1] * size, size)
            y2[here] = y2[here] + c2[key[1], :, pl.ds(y, 1)]
        else:
            unit = units[key]
            unit[1][...] = unit[1][...] + unit[0][:, pl.ds(y, 1)]

    def z_copy(key, i):
        unit = units[key]
        to = (m + i) % peers_z
        return remote(
            unit[1].at[to], unit[2].at[i - 1], (zs.at[unit[7]], zr.at[unit[7]]), i - 1, (2 * to + y, x * 2 + c)
        )

    def z_copies(key):
        return [z_copy(key, i) for i in range(1, peers_z)]

    def z_send(key):
        for copy in z_copies(key):
            copy.start()

    def z_send_chunk(chunk):
        size = n_dp // 8
        for i in range(size):
            to = chunk * size + i

            @pl.when(m != to)
            def _(to=to):
                z_copy(("2", 0), (to - m + peers_z) % peers_z).start()

    def z_done(key):
        unit = units[key]
        for copy in z_copies(key):
            copy.wait_recv()
        total = unit[1][m, 0].astype(F32)
        for i in range(peers_z - 1):
            total = total + unit[2][i, 0].astype(F32)
        unit[3][...] = total.astype(BF16)
        if key[0] == "1":
            g_copy(key).start()

    def x_copy(key):
        unit = units[key]
        return remote(unit[3], unit[4], (xs, xr), unit[7], across)

    def g_copy(key):
        unit = units[key]
        return remote(unit[3] if key[0] == "1" else unit[4], unit[5], (gs, gr), unit[7], sibling)

    def second_copy(pair):
        return remote(xi1.at[pair], gi1.at[pair, 1], (gs, gr), 2 + pair, sibling)

    def x_done(key):
        unit = units[key]
        x_copy(key).wait_recv()
        if key[0] == "1":
            second_copy(key[1]).start()
            return
        unit[4][...] = (unit[3][...].astype(F32) + unit[4][...].astype(F32)).astype(BF16)
        g_copy(key).start()

    def g_done(key):
        unit = units[key]
        g_copy(key).wait_recv()
        if key[0] == "1":
            second_copy(key[1]).wait_recv()
            for chip, who, ref in (
                (x, c, unit[3]), (1 - x, c, unit[4]), (x, 1 - c, unit[5]), (1 - x, 1 - c, gi1.at[key[1], 1])
            ):
                where = pl.ds(at128((2 * key[1] + chip) * width + who * cols), cols)
                sum_fc1[:, where] = ref[...]
            return
        for value, who in ((unit[4], c), (unit[5], 1 - c)):
            full = value[...]
            if key[0] == "2":
                sum_fc2[:, pl.ds(at128(who * cols), cols)] = full
            elif key[0] == "3":
                sum_out[:, pl.ds(at128(who * cols), cols)] = full
            else:
                for i in range(3):
                    where = pl.ds(at128(i * width + who * cols + key[1] * 128), 128)
                    sum_qkv[:, where] = full[:, i * 128 : (i + 1) * 128]

    quad = x * 2 + y

    def quad_copies(kind, size):
        copies = []
        for i in range(1, 4):
            to_x = x if i < 2 else 1 - x
            to_y = y if i % 2 == 0 else 1 - y
            here = va.at[kind, quad, pl.ds(0, size)]
            copies.append(remote(here, here, (vas.at[kind], var.at[kind]), i - 1, (2 * m + to_y, to_x * 2 + c)))
        return copies

    def line_copies(kind, size):
        copies = []
        for i in range(1, peers_z):
            here = vb.at[kind, m, pl.ds(0, size)]
            to = (m + i) % peers_z
            copies.append(remote(here, here, (vbs.at[kind], vbr.at[kind]), i - 1, (2 * to + y, x * 2 + c)))
        return copies

    def last_copy(kind, size):
        return remote(
            vc.at[kind, 0, pl.ds(0, size)], vc.at[kind, 1, pl.ds(0, size)], (vcs, vcr), kind, sibling
        )

    def quad_send(kind, size):
        for copy in quad_copies(kind, size):
            copy.start()

    def quad_done(kind, size):
        for copy in quad_copies(kind, size):
            copy.wait_recv()
        total = va[kind, 0, :size]
        for i in range(1, 4):
            total = total + va[kind, i, :size]
        vb[kind, m, :size] = total
        for copy in line_copies(kind, size):
            copy.start()

    def line_done(kind, size):
        for copy in line_copies(kind, size):
            copy.wait_recv()
        total = vb[kind, 0, :size]
        for i in range(1, peers_z):
            total = total + vb[kind, i, :size]
        vc[kind, 0, :size] = total
        last_copy(kind, size).start()

    def early_done():
        last_copy(0, 16).wait_recv()
        early[...] = vc[0, 0] + vc[0, 1]

    def late_done():
        last_copy(1, 8).wait_recv()
        ours, other_core = vc[1, 0, :8], vc[1, 1, :8]
        late[:8] = jnp.where(c == 0, ours, other_core)
        late[8:] = jnp.where(c == 0, other_core, ours)
        late[:2] = ours[:2] + other_core[:2]

    def load_pair(t, slot):
        copies = []
        for i, (src, dst) in enumerate(((q_hbm, q_aug), (k_hbm, k_aug), (v_hbm, v_aug))):
            copies.append(
                pltpu.make_async_copy(src.at[pl.ds(2 * t, 2)], dst.at[slot], lsem.at[3 * slot + i])
            )
        return copies

    plain = [
        pltpu.make_async_copy(a_hbm, att, lsem.at[6]),
        pltpu.make_async_copy(n_hbm.at[pl.ds(0, span)], nrm, lsem.at[7]),
    ]
    peers = [sibling, across, beside, (dp + 1 - 2 * y, (1 - x) * 2 + c)] + [(2 * ((m + i) % peers_z) + y, x * 2 + c) for i in range(1, peers_z)]
    announce(peers)

    row = lambda i: vectors[i : i + 1, :]
    live_col = column_of(live[...].astype(F32))
    def dense(w_out, w_fc1, w_fc2, w1, w2, w3, branch_attn, normed_s, g_mlp_s, branch_mlp, g_normed, hidden_s, g_pre_s, dsem):
        def load_chunk(j, slot):
            return [
                pltpu.make_async_copy(w_fc1_hbm.at[:, pl.ds(at128(j * width), width)], w_fc1.at[slot], dsem.at[slot]),
                pltpu.make_async_copy(
                    w_fc2_hbm.at[pl.ds(pl.multiple_of(j * width, width), width)], w_fc2.at[slot], dsem.at[2 + slot]
                ),
            ]

        load_out = pltpu.make_async_copy(w_out_hbm, w_out, dsem.at[4])
        load_out.start()
        for copy in load_chunk(0, 0):
            copy.start()
        for copy in load_pair(0, 0) + plain:
            copy.start()
        for i, vector in (
            (LN1_GAIN, ln1_gain), (B_OUT, b_out), (SCALE_ATTN, scale_attn), (LN2_GAIN, ln2_gain), (LN2_BIAS, ln2_bias),
            (B_FC2, b_fc2), (SCALE_MLP, scale_mlp),
        ):
            vectors[i : i + 1, :] = vector[...].astype(F32).reshape(1, width)
        for i in range(steps):
            vectors[B_FC1 + i : B_FC1 + i + 1, :] = b_fc1[i * width : (i + 1) * width].astype(F32).reshape(1, width)
        source = tokens[...].astype(F32)
        g_mlp = (grad_out[...].astype(F32) * (live_col * row(SCALE_MLP))).astype(BF16)
        g_mlp_s[...] = g_mlp
        sums = va.at[0, quad]
        sums[...] = jnp.zeros_like(sums)
        sums[4:5, :] = jnp.sum(g_mlp.astype(F32), axis=0, keepdims=True)
        sums[10:11, :] = jnp.sum(live_col * source * source, axis=0, keepdims=True)
        sums[13:14, :] = jnp.broadcast_to(jnp.sum(live_col, axis=0, keepdims=True), (1, width))
        load_out.wait()
        branch = dot(att_low[...], w_out[...]) + row(B_OUT)
        branch_attn[...] = branch
        part = live_col * row(SCALE_ATTN) * branch
        stream = source + part
        g_tokens[...] = stream
        sums[11:12, :] = jnp.sum(part * part, axis=0, keepdims=True)
        hat, unused = norm_stats(stream)
        normed_s[...] = (hat * row(LN2_GAIN) + row(LN2_BIAS)).astype(BF16)
        branch_mlp[...] = jnp.zeros_like(branch_mlp)
        g_normed[...] = jnp.zeros_like(g_normed)

        def core_copies(j):
            return [
                remote(w1.at[1 - c], c1.at[j], (cs, cr), j, sibling),
                remote(w2.at[1 - c], c2.at[j], (cs, cr), 4 + j, sibling),
            ]

        def core_done(j):
            for copy in core_copies(j):
                copy.wait()
            c2[j] = c2[j] + w2[c]
            size = n_dp // 8
            remote(
                c2.at[j, :, pl.ds(1 - y, 1)], y2.at[pl.ds(j * size, size)], (ys, yr), 4 + j, beside
            ).start()
            c1[j] = c1[j] + w1[c]
            for pair in range(2):

                @pl.when(j == 2 * pair + 1)
                def _(pair=pair):
                    pair_copy(pair).start()

        def chunk(j, unused):
            slot = j % 2
            for copy in load_chunk(j, slot):
                copy.wait()

            @pl.when(j + 1 < steps)
            def _():
                for copy in load_chunk(j + 1, 1 - slot):
                    copy.start()

            bias = vectors[pl.ds(B_FC1 + j, 1), :]
            third = width // 3
            slopes = []
            for i in range(3):
                here = slice(i * third, (i + 1) * third)
                u = dot(normed_s[...], w_fc1[slot, :, here]) + bias[:, here]
                square = u * u
                t = jnp.tanh(u * (GELU_A + GELU_A * GELU_B * square))
                hidden_s[:, here] = (0.5 * u * (1.0 + t)).astype(BF16)
                slope = 0.5 * (1.0 + t) + (0.5 * u) * (1.0 - t * t) * (GELU_A + (3.0 * GELU_A * GELU_B) * square)
                g_pre = (dot(g_mlp_s[...], w_fc2[slot, here, :], NT) * slope).astype(BF16)
                g_pre_s[:, here] = g_pre
                slopes.append(jnp.sum(g_pre.astype(F32), axis=0, keepdims=True))
            sums[pl.ds(6 + j, 1), :] = jnp.concatenate(slopes, axis=1)

            @pl.when(j > 0)
            def _():
                core_done(j - 1)

            @pl.when(j == steps - 1)
            def _():
                y_done(("2", 0))
                z_send_chunk(0)

            spread_halves(w2, dot(hidden_s[...], g_mlp_s[...], TN))
            spread_halves(w1, dot(normed_s[...], g_pre_s[...], TN))
            for copy in core_copies(j):
                copy.start()
            branch_mlp[...] += dot(hidden_s[...], w_fc2[slot])
            g_normed[...] += dot(g_pre_s[...], w_fc1[slot], NT)
            return unused

        meet(peers)
        lax.fori_loop(0, steps, chunk, 0)
        y_done(("2", 1))
        z_send_chunk(1)
        grad = grad_out[...].astype(F32)
        branch = branch_mlp[...] + row(B_FC2)
        part = live_col * row(SCALE_MLP) * branch
        stream = g_tokens[...]
        out[...] = (stream + part).astype(BF16)
        sums[12:13, :] = jnp.sum(part * part, axis=0, keepdims=True)
        sums[5:6, :] = jnp.sum(grad * live_col * branch, axis=0, keepdims=True)
        hat, scale = norm_stats(stream)
        g_n2 = g_normed[...]
        sums[2:3, :] = jnp.sum(g_n2 * hat, axis=0, keepdims=True)
        sums[3:4, :] = jnp.sum(g_n2, axis=0, keepdims=True)
        g_tokens[...] = grad + norm_back(g_n2, hat, scale, row(LN2_GAIN))
        gated = g_tokens[...] * live_col
        g_attn = (gated * row(SCALE_ATTN)).astype(BF16)
        g_att[...] = dot(g_attn, w_out[...], NT).astype(BF16)
        swap.start()
        core_done(jnp.int32(steps - 1))
        sums[1:2, :] = jnp.sum(gated * branch_attn[...], axis=0, keepdims=True)
        sums[0:1, :] = jnp.sum(g_attn.astype(F32), axis=0, keepdims=True)
        quad_send(0, 16)
        spread_halves(w3, dot(att_low[...], g_attn, TN))
        give = remote(w3.at[1 - c], c3, (cs, cr), 8, sibling)
        give.start()
        pair_done(0)
        y_done(("2", 2))
        z_send_chunk(2)
        give.wait()
        c3[...] = c3[...] + w3[c]
        y_copy(("3", 0)).start()

    def spread_rows(ref, value):
        size = ref.shape[-2]
        for i in range(ref.shape[0]):
            for k in range(2):
                ref[i, k] = value[(2 * i + k) * size : (2 * i + k + 1) * size].astype(BF16)

    def spread_halves(ref, value):
        for half in range(2):
            spread_rows(ref.at[half], value[:, half * cols : (half + 1) * cols])

    own = pl.ds(pl.multiple_of(c * rows, rows), rows)
    other = pl.ds(pl.multiple_of((1 - c) * rows, rows), rows)
    swap = remote(g_att.at[:, theirs], g_rows.at[own], (ss, sr), 0, sibling)
    part_rows = width // n_dp
    wide_rows = w_fc2_hbm.shape[0] // n_dp
    pl.run_scoped(
        dense,
        pltpu.VMEM((width, width), BF16),
        pltpu.VMEM((2, width, width), BF16),
        pltpu.VMEM((2, width, width), BF16),
        pltpu.VMEM((2, peers_z, 2, part_rows, cols), BF16),
        pltpu.VMEM((2, n_dp // 8, 2, wide_rows, cols), BF16),
        pltpu.VMEM((2, peers_z, 2, part_rows, cols), BF16),
        pltpu.VMEM((rows, width), F32),
        pltpu.VMEM((rows, width), BF16),
        pltpu.VMEM((rows, width), BF16),
        pltpu.VMEM((rows, width), F32),
        pltpu.VMEM((rows, width), F32),
        pltpu.VMEM((rows, width), BF16),
        pltpu.VMEM((rows, width), BF16),
        pltpu.SemaphoreType.DMA((5,)),
    )

    def attention(g_aug, dq, dkv, dkv_own, d_query, d_key, d_value, w_own):
        late_loads = [
            pltpu.make_async_copy(
                w_hbm.at[:, pl.ds(at128(part * width + c * cols), cols)], w_own.at[part], lsem.at[8 + part]
            )
            for part in range(3)
        ]
        for copy in late_loads:
            copy.start()
        g_rows[own] = g_att[:, mine]
        for copy in plain:
            copy.wait()
        swap.wait_recv()
        spot = lanes((span, 128))
        low = spot < head_dim
        for t in range(pairs):
            g = g_rows[:, t * 128 : (t + 1) * 128].astype(F32)
            product = g * att[t]
            for odd in range(2):
                delta = jnp.sum(jnp.where(low if odd == 0 else ~low, product, 0.0), axis=1, keepdims=True)
                tile = g if odd == 0 else pltpu.roll(g, 64, 1)
                tile = jnp.where(low, tile, 0.0)
                for i, piece in enumerate(split3(delta)):
                    tile = jnp.where(spot == 64 + i, -piece, tile)
                g_aug[2 * t + odd] = tile.astype(BF16)
        lane = lanes((256, 256))
        line = lax.broadcasted_iota(jnp.int32, (256, 256), 0)
        in_rows = (lane >= ROW0) & (lane < COL0) & (line >= ROW0) & (line < COL0)
        in_cols = (lane >= COL0) & (lane < SEG0) & (line >= COL0) & (line < SEG0)
        flip = jnp.where(lane + line == 255, 1.0, 0.0).astype(BF16)
        sums = va.at[1, quad]
        sums[...] = jnp.zeros_like(sums)
        block = rows

        def dkv_copy(t, odd):
            return remote(dkv_out.at[t, odd], dkv_in.at[t, odd], (ss, sr), 1 + 2 * t + odd, across)

        def finish_pair(t):
            for odd in range(2):
                dkv_copy(t, odd).wait_recv()
            first, second = (dkv_own[t % 2, odd] + dkv_in[t, odd].astype(F32) for odd in range(2))
            place_k = pl.ds(at128(t * 128), 128)
            dkv[0, :, place_k] = jnp.where(low, first, pltpu.roll(second, 64, 1)).astype(BF16)
            dkv[1, :, place_k] = jnp.where(low, pltpu.roll(first, 64, 1), second).astype(BF16)
            both = jnp.concatenate([dkv[0, :, place_k], dkv[1, :, place_k]], axis=1)
            part = jnp.concatenate([dq[:, place_k], both], axis=1)
            spread_rows(wq.at[t], dot(nrm[...], part, TN))
            y_copy(("q", t)).start()

        plan = {
            0: [lambda: y_done(("2", 3)), lambda: z_send_chunk(3)],
            2: [lambda: y_done(("1", 0)), lambda: z_send(("1", 0)), lambda: pair_done(1)],
            4: [lambda: y_done(("3", 0)), lambda: z_send(("3", 0))],
            5: [lambda: finish_pair(0), lambda: y_done(("1", 1)), lambda: z_send(("1", 1))],
            6: [lambda: quad_done(0, 16)],
            8: [lambda: finish_pair(1), lambda: y_done(("q", 0)), lambda: z_send(("q", 0))],
            10: [
                lambda: y_done(("q", 1)), lambda: z_send(("q", 1)), lambda: z_done(("1", 0)),
                lambda: x_copy(("1", 0)).start(), lambda: z_done(("3", 0)), lambda: x_copy(("3", 0)).start(),
            ],
            11: [lambda: line_done(0, 16), lambda: z_done(("2", 0)), lambda: x_copy(("2", 0)).start()],
        }

        def sweep(point, unused):
            it, odd = point // 2, point % 2
            part = 1 - it % 2
            t = it // 2
            slot = t % 2

            @pl.when((part == 1) & (odd == 0))
            def _():
                for copy in load_pair(t, slot):
                    copy.wait()

            @pl.when((part == 1) & (odd == 0) & (t + 1 < pairs))
            def _():
                for copy in load_pair(t + 1, 1 - slot):
                    copy.start()

            @pl.when(part == 1)
            def _():
                d_query[odd] = jnp.zeros(d_query.shape[1:], F32)

            for qb in range(span // block):
                here = slice(qb * block, (qb + 1) * block)
                queries, grads = q_aug[slot, odd, here, :], g_aug[2 * t + odd, here, :]
                total = d_query[odd, :, here]
                for kb in range(span // block):
                    there = slice(kb * block, (kb + 1) * block)
                    source = pl.ds(pl.multiple_of(part * span + kb * block, block), block)
                    keys = k_aug[slot, odd, source, :]
                    p = jnp.exp(dot(keys, queries, NT))
                    p_low = p.astype(BF16)
                    ds = (p * dot(v_aug[slot, odd, source, :], grads, NT)).astype(BF16)
                    gain_value = dot(p_low, grads)
                    gain_key = dot(ds, queries[:, :128])
                    if qb == 0:
                        d_value[odd, there, :] = gain_value
                        d_key[odd, there, :] = gain_key
                    else:
                        d_value[odd, there, :] += gain_value
                        d_key[odd, there, :] += gain_key
                    total = total + dot(keys, ds, TN)
                d_query[odd, :, here] = total
            new = jnp.where(low, d_key[odd], pltpu.roll(d_value[odd], 64, 1))

            @pl.when(part == 1)
            def _():
                dkv_out[t, odd] = new.astype(BF16)
                dkv_copy(t, odd).start()

            @pl.when(part == 0)
            def _():
                dkv_own[t % 2, odd] = new
                square = dot(d_query[odd].astype(BF16), k_aug[slot, odd, :span, :])
                h = 2 * t + odd
                for table, mask in enumerate((in_rows, in_cols)):
                    flipped = sum(dot(flip, piece.astype(BF16)) for piece in split3(jnp.where(mask, square, 0.0)))
                    turned = pltpu.roll(flipped, 0, 1, stride=1, stride_axis=0)
                    sums[pl.ds(3 + table * 2 + h // 3, 1), pl.ds(at128(h % 3 * 256), 256)] = jnp.sum(
                        turned, axis=0, keepdims=True
                    )

            @pl.when((part == 0) & (odd == 1))
            def _():
                both = jnp.concatenate([d_query[0, :head_dim, :], d_query[1, :head_dim, :]], axis=0)
                dq[:, pl.ds(at128(t * 128), 128)] = (jnp.transpose(both) * head_dim ** (-0.5)).astype(BF16)

            for i, acts in plan.items():

                @pl.when(point == i)
                def _(acts=acts):
                    for act in acts:
                        act()

            return unused

        lax.fori_loop(0, 4 * pairs, sweep, 0)
        last = pairs - 1
        finish_pair(last)
        for copy in late_loads:
            copy.wait()

        def through(where):
            total = dot(dq[where, :], w_own[0], NT)
            return total + dot(dkv[0, where, :], w_own[1], NT) + dot(dkv[1, where, :], w_own[2], NT)

        swap.wait_send()
        g_att[...] = through(other).astype(BF16)
        give = remote(g_att, half_in, (ss, sr), 1 + 2 * pairs, sibling)
        give.start()
        z_done(("q", 0))
        x_copy(("q", 0)).start()
        sums[2:3, :cols] = jnp.sum(dq[...].astype(F32), axis=0, keepdims=True)
        sums[2:3, cols:] = jnp.sum(dkv[1].astype(F32), axis=0, keepdims=True)
        g_n1 = through(own)
        hat, scale = norm_stats(tokens[...].astype(F32))
        give.wait_recv()
        g_n1 = g_n1 + half_in[...].astype(F32)
        sums[0:1, :] = jnp.sum(g_n1 * hat, axis=0, keepdims=True)
        sums[1:2, :] = jnp.sum(g_n1, axis=0, keepdims=True)
        quad_send(1, 8)
        y_done(("q", last))
        z_send(("q", last))
        z_done(("1", 1))
        x_copy(("1", 1)).start()
        g_tokens[...] = g_tokens[...] + norm_back(g_n1, hat, scale, row(LN1_GAIN))
        x_done(("3", 0))
        x_done(("1", 0))
        quad_done(1, 8)
        z_done(("q", 1))
        x_copy(("q", 1)).start()
        x_done(("q", 0))
        early_done()
        g_done(("3", 0))
        g_done(("1", 0))
        z_done(("q", last))
        x_copy(("q", last)).start()
        line_done(1, 8)
        x_done(("2", 0))
        x_done(("1", 1))
        x_done(("q", 1))
        g_done(("q", 0))
        g_done(("2", 0))
        g_done(("1", 1))
        x_done(("q", last))
        late_done()
        g_done(("q", 1))
        g_done(("q", last))
        give.wait_send()
        for t in range(pairs):
            for odd in range(2):
                dkv_copy(t, odd).wait_send()

    pl.run_scoped(
        attention,
        pltpu.VMEM((heads, span, 128), BF16),
        pltpu.VMEM((span, cols), BF16),
        pltpu.VMEM((2, span, cols), BF16),
        pltpu.VMEM((2, 2, span, 128), F32),
        pltpu.VMEM((2, 256, span), F32),
        pltpu.VMEM((2, span, 128), F32),
        pltpu.VMEM((2, span, 128), F32),
        pltpu.VMEM((3, width, cols), BF16),
    )
    for key in units:
        if key[0] != "2":
            y_copy(key).wait_send()
        for copy in z_copies(key):
            copy.wait_send()
        x_copy(key).wait_send()
        g_copy(key).wait_send()
    for j in range(4):
        y_copy(("2", j)).wait_send()
    for pair in range(2):
        second_copy(pair).wait_send()
    for kind, size in enumerate((16, 8)):
        for copy in quad_copies(kind, size) + line_copies(kind, size) + [last_copy(kind, size)]:
            copy.wait_send()


def backward(n_dp, att_low, tokens, grad_out, live, vectors, w_out, w_fc1, w_fc2, q_aug, k_aug, v_aug, att, nrm, w_qkv):
    rows, width = tokens.shape
    heads = q_aug.shape[0]
    pairs, cols = heads // 2, heads * 64
    span, group = 2 * rows, 4 * rows
    hidden = w_fc1.shape[1]
    steps = hidden // width
    z, part, wide = n_dp // 2, width // n_dp, hidden // n_dp
    any_spec = pl.BlockSpec(memory_space=pl.ANY)
    vmem = pl.BlockSpec(memory_space=pltpu.VMEM)
    low = lambda *shape: pltpu.VMEM(shape, BF16)
    full = lambda *shape: pltpu.VMEM(shape, F32)
    dma = lambda *shape: pltpu.SemaphoreType.DMA(shape)
    received = lambda *lead: [low(2, *lead, part, cols), low(wide, cols), low(part, cols), low(pairs, part, cols)]
    return pl.pallas_call(
        functools.partial(back_kernel, n_dp),
        out_shape=[
            jax.ShapeDtypeStruct((rows, width), BF16),
            jax.ShapeDtypeStruct((rows, width), F32),
            jax.ShapeDtypeStruct((part, 3 * width), BF16),
            jax.ShapeDtypeStruct((part, width), BF16),
            jax.ShapeDtypeStruct((part, hidden), BF16),
            jax.ShapeDtypeStruct((wide, width), BF16),
            jax.ShapeDtypeStruct((16, width), F32),
            jax.ShapeDtypeStruct((16, width), F32),
        ],
        in_specs=[vmem] * 12 + [any_spec] * 9,
        out_specs=[vmem] * 8,
        scratch_shapes=[
            low(2, 2, span, 256), low(2, 2, group, 256), low(2, 2, group, 128),
            full(pairs, span, 128), low(span, width),
            low(rows, width), low(span, cols), low(rows, width),
            low(pairs, 2, span, 128), low(pairs, 2, span, 128),
            low(steps, z, 2, part, cols), low(steps, n_dp // 8, 2, wide, cols), low(z, 2, part, cols),
            low(2, z, 2, part, cols),
            low(2, z, 1, part, cols), low(z, 1, wide, cols), low(z, 1, part, cols), low(pairs, z, 1, part, cols),
            low(2, z - 1, 1, part, cols), low(z - 1, 1, wide, cols), low(z - 1, 1, part, cols),
            low(pairs, z - 1, 1, part, cols),
            *received(), *received(), *received(2),
            low(pairs, z, 2, part, cols), full(2, 4, 16, width), full(2, z, 16, width), full(2, 2, 16, width), full(16, width),
            dma(9), dma(9), dma(2), dma(2), dma(12), dma(12), dma(9, z - 1), dma(9, z - 1), dma(9), dma(9), dma(9), dma(9),
            dma(2, 3), dma(2, 3), dma(2, z - 1), dma(2, z - 1), dma(2), dma(2), dma(2 + 2 * pairs), dma(2 + 2 * pairs),
            dma(11),
        ],
        compiler_params=pltpu.CompilerParams(
            collective_id=1, has_side_effects=True, vmem_limit_bytes=VMEM_LIMIT
        ),
        name="backward",
    )(att_low, tokens, grad_out, live, *vectors, w_out, w_fc1, w_fc2, q_aug, k_aug, v_aug, att, nrm, w_qkv)


def outputs_kernel(out_in, tokens_in, qkv_in, out_w_in, fc1_in, fc2_in, early, late, *refs):
    (
        out, g_tokens, g_ln1, b_ln1, qkv, b_query, b_value, out_w, b_out, s_attn, g_ln2, b_ln2, fc1, b_fc1, fc2,
        b_fc2, s_mlp, t_rows, t_cols, means,
    ) = refs
    width = out.shape[1]
    out[...] = out_in[...]
    g_tokens[...] = tokens_in[...]
    for ref, value in ((qkv, qkv_in), (out_w, out_w_in), (fc1, fc1_in), (fc2, fc2_in)):
        ref[...] = value[...].astype(F32)
    for i, ref in enumerate((b_out, s_attn, g_ln2, b_ln2, b_fc2, s_mlp)):
        ref[...] = early[i, :]
    for i in range(b_fc1.shape[0] // width):
        b_fc1[i * width : (i + 1) * width] = early[6 + i, :]
    g_ln1[...] = late[0, :]
    b_ln1[...] = late[1, :]
    half = width // 2
    b_query[...] = jnp.concatenate([late[2:3, :half], late[10:11, :half]], axis=1)[0]
    b_value[...] = jnp.concatenate([late[2:3, half:], late[10:11, half:]], axis=1)[0]
    count = early[13:14, :1]
    lane = lanes((1, 3))
    squares = jnp.zeros((1, 3), F32)
    for i in range(3):
        squares = jnp.where(lane == i, jnp.sum(early[10 + i : 11 + i, :], axis=1, keepdims=True), squares)
    means[...] = jnp.sqrt(squares / (count * width))[0]
    spans = t_rows.shape[1]
    limit = (spans - 1) // 2
    offset = lax.broadcasted_iota(jnp.int32, (256, spans), 0) + 1
    offset = jnp.where(offset < 128, offset, offset - 256)
    pick = jnp.where(jnp.clip(offset, -limit, limit) + limit == lanes((256, spans)), 1.0, 0.0).astype(BF16)
    for third in range(3):
        part = late[:, third * 256 : (third + 1) * 256]
        sums = sum(dot(piece.astype(BF16), pick) for piece in split3(part))
        for i in range(8):
            core, table, group = i // 4, i // 2 % 2, i % 2
            head, source = core * 6 + group * 3 + third, core * 8 + 3 + table * 2 + group
            (t_rows, t_cols)[table][head : head + 1, :] = sums[source : source + 1, :]


def write_outputs(arrays, shapes):
    vmem = pl.BlockSpec(memory_space=pltpu.VMEM)
    return pl.pallas_call(
        outputs_kernel,
        out_shape=[jax.ShapeDtypeStruct(*shape) for shape in shapes],
        in_specs=[vmem] * len(arrays),
        out_specs=[vmem] * len(shapes),
        compiler_params=pltpu.CompilerParams(vmem_limit_bytes=VMEM_LIMIT),
        name="outputs",
    )(*arrays)


def body(
    tokens, grad_out, segment, live_rows, coords, ln1_gain, ln1_bias, w_qkv, b_query, b_value, w_out,
    b_out, scale_attn, ln2_gain, ln2_bias, w_fc1, b_fc1, w_fc2, b_fc2, scale_mlp, table_rows, table_cols,
):
    rows, width = tokens.shape
    heads = table_rows.shape[0] // 2
    line = lambda v: v.reshape(1, -1)
    live = line(live_rows)
    att_low, q_aug, k_aug, v_aug, att, nrm = forward_attention(
        tokens, line(segment), live, coords, (ln1_gain, ln1_bias, b_query, b_value), table_rows, table_cols, w_qkv
    )
    out, g_tokens, sum_qkv, sum_out, sum_fc1, sum_fc2, early, late = backward(
        lax.axis_size("dp"), att_low, tokens, grad_out, live,
        (ln1_gain, b_out, scale_attn, ln2_gain, ln2_bias, b_fc2, scale_mlp, b_fc1), w_out, w_fc1, w_fc2,
        q_aug, k_aug, v_aug, att, nrm, w_qkv,
    )
    part, hidden = sum_out.shape[0], w_fc1.shape[1]
    vector, table = ((width,), F32), (table_rows.shape, F32)
    return write_outputs(
        (out, g_tokens, sum_qkv, sum_out, sum_fc1, sum_fc2, early, late),
        [
            ((rows, width), BF16), ((rows, width), F32), vector, vector, ((part, 3 * width), F32), vector, vector,
            ((part, width), F32), vector, vector, vector, vector, ((part, hidden), F32), ((hidden,), F32),
            (sum_fc2.shape, F32), vector, vector, table, table, ((3,), F32),
        ],
    )


def solution(mesh):
    rows = P(("dp", "blk"), None)
    flat = P(("dp", "blk"))
    return jax.shard_map(
        body,
        mesh=mesh,
        in_specs=(rows, rows, flat, flat, P(None, ("dp", "blk"))) + (P(),) * 17,
        out_specs=(
            rows, rows, P(), P(), P("dp", None), P(), P(), P("dp", None), P(), P(), P(), P(),
            P("dp", None), P(), P("dp", None), P(), P(), P(), P(), P(),
        ),
        check_vma=False,
    )
```

```python
import functools

import jax
import jax.numpy as jnp
from jax import lax
from jax.experimental import pallas as pl
from jax.experimental.pallas import tpu as pltpu
from jax.sharding import PartitionSpec as P

MESH = pl.DeviceIdType.MESH
BF16 = jnp.bfloat16
F32 = jnp.float32
EPS = 1e-06
MASKED = -1000000000.0
NT = ((1,), (1,))
TN = ((0,), (0,))
ROW0, COL0, SEG0, LIVE0, LSE0 = 64, 150, 236, 240, 241
VMEM_LIMIT = 63 << 20
(LN1_GAIN, LN1_BIAS, B_QUERY, B_VALUE, B_OUT, SCALE_ATTN, LN2_GAIN, LN2_BIAS, B_FC2, SCALE_MLP, B_FC1) = range(11)
GELU_A, GELU_B = 0.7978845608, 0.044715


def dot(left, right, dims=((1,), (0,))):
    return lax.dot_general(left, right, (dims, ((), ())), preferred_element_type=F32)


def split3(value):
    high = value.astype(BF16).astype(F32)
    rest = value - high
    middle = rest.astype(BF16).astype(F32)
    return high, middle, rest - middle


def lanes(shape):
    return lax.broadcasted_iota(jnp.int32, shape, len(shape) - 1)


def column_of(row):
    return jnp.transpose(jnp.broadcast_to(row, (8, row.shape[1])))[:, :1]


def place():
    me = lax.axis_index("blk")
    return lax.axis_index("dp"), me // 2, me % 2


def announce(peers):
    barrier = pltpu.get_barrier_semaphore()
    for peer in peers:
        pl.semaphore_signal(barrier, inc=1, device_id=peer, device_id_type=MESH)


def meet(peers):
    pl.semaphore_wait(pltpu.get_barrier_semaphore(), len(peers))


def remote(src, dst, sems, index, peer):
    return pltpu.make_async_remote_copy(
        src_ref=src,
        dst_ref=dst,
        send_sem=sems[0].at[index],
        recv_sem=sems[1].at[index],
        device_id=peer,
        device_id_type=MESH,
    )


def at128(index):
    return pl.multiple_of(index, 128)


def forward_kernel(
    tokens, seg, live, coords, ln1_gain, ln1_bias, b_query, b_value, table_rows, table_cols, w_hbm,
    att_out, q_hbm, k_hbm, v_hbm, a_hbm, n_hbm,
    nrm, w_own, meta, squares, base, q_aug, k_aug, v_aug, acc, peak, score, top, att, att_low,
    att_in, vectors, alive_rows, rsend, rrecv, lsem,
):
    rows, width = tokens.shape
    heads, head_dim = q_aug.shape[0], 64
    cols = heads * head_dim
    dp, x, c = place()
    sibling = (dp, x * 2 + 1 - c)
    across = (dp, (1 - x) * 2 + c)
    diagonal = (dp, (1 - x) * 2 + 1 - c)
    rsem = (rsend, rrecv)
    announce([sibling, across, diagonal])
    loads = [
        pltpu.make_async_copy(
            w_hbm.at[:, pl.ds(at128(part * width + c * cols), cols)], w_own.at[part], lsem.at[part]
        )
        for part in range(3)
    ]
    for load in loads:
        load.start()

    for i, vector in enumerate((ln1_gain, ln1_bias, b_query, b_value)):
        vectors[i : i + 1, :] = vector[...].astype(F32).reshape(1, width)

    source = tokens[...].astype(F32)
    average = jnp.mean(source, axis=-1, keepdims=True)
    centered = source - average
    spread = jnp.mean(centered * centered, axis=-1, keepdims=True)
    normed = centered * lax.rsqrt(spread + EPS) * vectors[LN1_GAIN : LN1_GAIN + 1, :]
    normed = normed + vectors[LN1_BIAS : LN1_BIAS + 1, :]
    own = pl.ds(pl.multiple_of(c * rows, rows), rows)
    nrm[own] = normed.astype(BF16)
    meta[c] = jnp.concatenate(
        [seg[...], live[...], coords[...], jnp.zeros((4, rows), jnp.int32)], axis=0
    )
    meet([sibling, across, diagonal])
    half = rows // 2
    sends = [
        remote(meta.at[c], meta.at[c], rsem, 0, sibling),
        remote(meta.at[c], meta.at[2 + c], rsem, 1, across),
        remote(meta.at[c], meta.at[2 + c], rsem, 2, diagonal),
        remote(nrm.at[own], nrm.at[own], rsem, 3, sibling),
    ]
    pieces, forwards = [], []
    for i in range(2):
        mine = pl.ds(pl.multiple_of(c * rows + i * half, half), half)
        there = pl.ds(pl.multiple_of((2 + c) * rows + i * half, half), half)
        pieces.append(remote(nrm.at[mine], nrm.at[there], rsem, 4 + i, across))
        forwards.append(remote(nrm.at[there], nrm.at[there], rsem, 6 + i, sibling))
    for copy in sends + pieces:
        copy.start()

    spans = table_rows.shape[1]
    limit = (spans - 1) // 2
    offset = lanes((spans, 256))
    offset = jnp.where(offset < 128, offset, offset - 256)
    entry = lax.broadcasted_iota(jnp.int32, (spans, 256), 0)
    pick = jnp.where(jnp.clip(-offset, -limit, limit) + limit == entry, 1.0, 0.0).astype(BF16)
    base[0] = jnp.pad(dot(table_rows[...], pick), ((0, 4), (0, 0)))
    base[1] = jnp.pad(dot(table_cols[...], pick), ((0, 4), (0, 0)))
    lane = lanes((256, 256))
    line = lax.broadcasted_iota(jnp.int32, (256, 256), 0)
    in_rows = (lane >= ROW0) & (lane < COL0) & (line >= ROW0) & (line < COL0)
    in_cols = (lane >= COL0) & (lane < SEG0) & (line >= COL0) & (line < SEG0)
    keep = (lane == line) & (lane >= SEG0) & (lane <= LIVE0)

    def make_square(h, unused):
        shifted = [
            pltpu.roll(
                jnp.broadcast_to(base[i, pl.ds(c * heads + h, 1), :], (256, 256)),
                0, 1, stride=1, stride_axis=0,
            )
            for i in range(2)
        ]
        square = jnp.where(in_rows, shifted[0], jnp.where(in_cols, shifted[1], 0.0))
        squares[h] = jnp.where(keep, 1.0, square).astype(BF16)
        return unused

    lax.fori_loop(0, heads, make_square, 0)
    for load in loads:
        load.wait()
    own_cols = pl.ds(at128(c * cols), cols)
    query_bias = vectors[B_QUERY : B_QUERY + 1, own_cols]
    value_bias = vectors[B_VALUE : B_VALUE + 1, own_cols]

    low128 = lanes((rows, 128)) < head_dim

    def project(slot, queries):
        here = pl.ds(pl.multiple_of(slot * rows, rows), rows)
        info = jnp.transpose(meta[slot].astype(F32)).astype(jnp.int32)
        page, alive, r, col = (info[:, i : i + 1] for i in range(4))
        spot = lanes((rows, 256))
        hot = (spot == r + ROW0) | (spot == col + COL0)
        key_side = jnp.where(hot | ((spot >= LSE0) & (spot < LSE0 + 3)), 1.0, 0.0)
        other = (spot >= SEG0) & (spot < LIVE0) & (spot != page + SEG0)
        dead = (spot == LIVE0) & (alive <= 0)
        key_side = jnp.where(other | dead, MASKED, key_side)
        if queries:
            query_side = jnp.where(hot | (spot == page + SEG0) | (spot == LIVE0), 1.0, 0.0)
            query_side = query_side.astype(BF16)
        inputs = nrm[here]
        ones = jnp.where((spot[:, :128] >= 64) & (spot[:, :128] < 67), 1.0, 0.0)
        keys = dot(inputs, w_own[1])
        values = dot(inputs, w_own[2]) + value_bias
        if queries:
            query = (dot(inputs, w_own[0]) + query_bias) * head_dim ** (-0.5)
        for h in range(heads):
            tile = slice(h // 2 * 128, h // 2 * 128 + 128)
            turn = (lambda v: v) if h % 2 == 0 else (lambda v: pltpu.roll(v, 64, 1))
            k_aug[h, here, :128] = jnp.where(low128, turn(keys[:, tile]), key_side[:, :128]).astype(BF16)
            k_aug[h, here, 128:] = key_side[:, 128:].astype(BF16)
            v_aug[h, here, :] = jnp.where(low128, turn(values[:, tile]), ones).astype(BF16)
            if queries:
                extra = dot(query_side, squares[h])
                q_aug[h, here, :128] = jnp.where(low128, turn(query[:, tile]), extra[:, :128]).astype(BF16)
                q_aug[h, here, 128:] = extra[:, 128:].astype(BF16)

    project(c, True)
    for i in (0, 3):
        sends[i].wait_recv()
    project(1 - c, True)

    block = rows

    def score_of(h, qb, part, buf):
        s = dot(
            q_aug[h, qb * block : (qb + 1) * block, :],
            k_aug[h, part * 2 * rows : (part + 1) * 2 * rows, :],
            NT,
        )
        score[buf] = s
        top[buf] = jnp.broadcast_to(jnp.max(s, axis=1, keepdims=True), (block, 128))

    def weigh(h, qb, part, buf):
        here = slice(qb * block, (qb + 1) * block)
        m = top[buf]
        if part:
            before = peak[h, here, :]
            m = jnp.maximum(before, m)
        p = jnp.concatenate(
            [jnp.exp(score[buf, :, i : i + 128] - m).astype(BF16) for i in range(0, 2 * rows, 128)], axis=1
        )
        pv = dot(p, v_aug[h, part * 2 * rows : (part + 1) * 2 * rows, :])
        if not part:
            acc[h, here, :] = pv
            peak[h, here, :] = m
            return
        pv = pv + acc[h, here, :] * jnp.exp(before - m)
        total = jnp.broadcast_to(pv[:, 64:65], (block, 128))
        lse = jnp.where(alive_rows[qb] > 0, m + jnp.log(total), 0.0)
        value = pv / total
        tail = q_aug[h, here, 128:].astype(F32)
        for i, piece in enumerate(split3(lse)):
            tail = jnp.where(low_lane == LSE0 - 128 + i, -piece, tail)
        q_aug[h, here, 128:] = tail.astype(BF16)
        return value

    low_lane = lanes((block, 128))
    for qb in range(2):
        alive_rows[qb] = jnp.broadcast_to(column_of(meta[qb, 1:2, :].astype(F32)), (block, 128))

    def sweep(part, t, unused):
        order = [(0, 0), (0, 1), (1, 0), (1, 1)]
        for i, (odd, qb) in enumerate(order):
            if i < 3:
                score_of(2 * t + order[i + 1][0], order[i + 1][1], part, (i + 1) % 2)
            else:
                score_of(jnp.minimum(2 * t + 2, heads - 2), 0, part, 0)
            value = weigh(2 * t + odd, qb, part, i % 2)
            if part:
                here = slice(qb * block, (qb + 1) * block)
                if odd:
                    value = jnp.where(low128, att[t, here, :], pltpu.roll(value, 64, 1))
                att[t, here, :] = value
                if odd:
                    att_low[t, here, :] = value.astype(BF16)
        if not part:

            @pl.when(t == 1)
            def _():
                pieces[0].wait_recv()
                forwards[0].start()

        return unused

    score_of(0, 0, 0, 0)
    lax.fori_loop(0, heads // 2, functools.partial(sweep, 0), 0)
    pieces[1].wait_recv()
    forwards[1].start()
    sends[1].wait_recv()
    sends[2].wait_recv()
    project(2 + c, False)
    for copy in forwards:
        copy.wait_recv()
    project(3 - c, False)
    stores = [
        pltpu.make_async_copy(k_aug, k_hbm, lsem.at[3]),
        pltpu.make_async_copy(v_aug, v_hbm, lsem.at[4]),
        pltpu.make_async_copy(nrm, n_hbm, lsem.at[5]),
    ]
    for store in stores:
        store.start()
    score_of(0, 0, 1, 0)
    lax.fori_loop(0, heads // 2, functools.partial(sweep, 1), 0)
    stores += [
        pltpu.make_async_copy(q_aug, q_hbm, lsem.at[6]),
        pltpu.make_async_copy(att, a_hbm, lsem.at[7]),
    ]
    theirs = pl.ds(pl.multiple_of((1 - c) * rows, rows), rows)
    swap = remote(att_low.at[:, theirs, :], att_in, rsem, 8, sibling)
    swap.start()
    for store in stores[3:]:
        store.start()
    tiles = heads // 2
    for t in range(tiles):
        att_out[:, pl.ds(at128((c * tiles + t) * 128), 128)] = att_low[t, own, :]
    swap.wait_recv()
    for t in range(tiles):
        att_out[:, pl.ds(at128(((1 - c) * tiles + t) * 128), 128)] = att_in[t]
    for copy in sends + pieces + forwards + [swap]:
        copy.wait_send()
    for store in stores:
        store.wait()


def forward_attention(tokens, seg, live, coords, norm_vectors, t_rows, t_cols, w_qkv):
    rows, width = tokens.shape
    heads = t_rows.shape[0] // 2
    group = rows * 4
    any_spec = pl.BlockSpec(memory_space=pl.ANY)
    vmem = pl.BlockSpec(memory_space=pltpu.VMEM)
    return pl.pallas_call(
        forward_kernel,
        out_shape=[
            jax.ShapeDtypeStruct((rows, width), BF16),
            jax.ShapeDtypeStruct((heads, 2 * rows, 256), BF16),
            jax.ShapeDtypeStruct((heads, group, 256), BF16),
            jax.ShapeDtypeStruct((heads, group, 128), BF16),
            jax.ShapeDtypeStruct((heads // 2, 2 * rows, 128), F32),
            jax.ShapeDtypeStruct((group, width), BF16),
        ],
        in_specs=[vmem] * 10 + [any_spec],
        out_specs=[vmem] + [any_spec] * 5,
        scratch_shapes=[
            pltpu.VMEM((group, width), BF16),
            pltpu.VMEM((3, width, heads * 64), BF16),
            pltpu.VMEM((4, 8, rows), jnp.int32),
            pltpu.VMEM((heads, 256, 256), BF16),
            pltpu.VMEM((2, 16, 256), F32),
            pltpu.VMEM((heads, 2 * rows, 256), BF16),
            pltpu.VMEM((heads, group, 256), BF16),
            pltpu.VMEM((heads, group, 128), BF16),
            pltpu.VMEM((heads, 2 * rows, 128), F32),
            pltpu.VMEM((heads, 2 * rows, 128), F32),
            pltpu.VMEM((2, rows, 2 * rows), F32),
            pltpu.VMEM((2, rows, 128), F32),
            pltpu.VMEM((heads // 2, 2 * rows, 128), F32),
            pltpu.VMEM((heads // 2, 2 * rows, 128), BF16),
            pltpu.VMEM((heads // 2, rows, 128), BF16),
            pltpu.VMEM((8, width), F32),
            pltpu.VMEM((2, rows, 128), F32),
            pltpu.SemaphoreType.DMA((9,)),
            pltpu.SemaphoreType.DMA((9,)),
            pltpu.SemaphoreType.DMA((8,)),
        ],
        compiler_params=pltpu.CompilerParams(
            collective_id=0, has_side_effects=True, vmem_limit_bytes=VMEM_LIMIT
        ),
        name="attention_forward",
    )(tokens, seg, live, coords, *norm_vectors, t_rows, t_cols, w_qkv)


def norm_stats(values):
    average = jnp.mean(values, axis=-1, keepdims=True)
    centered = values - average
    scale = lax.rsqrt(jnp.mean(centered * centered, axis=-1, keepdims=True) + EPS)
    return centered * scale, scale


def norm_back(grad, hat, scale, gain):
    e = grad * gain
    return scale * (
        e
        - jnp.mean(e, axis=-1, keepdims=True)
        - hat * jnp.mean(e * hat, axis=-1, keepdims=True)
    )


def back_kernel(
    n_dp, att_low, tokens, grad_out, live, ln1_gain, b_out, scale_attn, ln2_gain, ln2_bias, b_fc2, scale_mlp, b_fc1,
    w_out_hbm, w_fc1_hbm, w_fc2_hbm, q_hbm, k_hbm, v_hbm,
    a_hbm, n_hbm, w_hbm,
    out, g_tokens, sum_qkv, sum_out, sum_fc1, sum_fc2, early, late,
    q_aug, k_aug, v_aug, att, nrm, g_att, g_rows, half_in,
    dkv_out, dkv_in,
    c1, c2, c3, p1, y1, y2, y3, yq, z1, z2, z3, zq, xo1, xo2, xo3, xoq, xi1, xi2, xi3, xiq, gi1, gi2, gi3, giq,
    wq, va, vb, vc, vectors,
    cs, cr, ps, pr, ys, yr, zs, zr, xs, xr, gs, gr, vas, var, vbs, vbr, vcs, vcr, ss, sr, lsem,
):
    rows, width = tokens.shape
    head_dim = 64
    pairs = dkv_out.shape[0]
    heads = 2 * pairs
    cols = heads * head_dim
    span = 2 * rows
    dp, x, c = place()
    y, m = dp % 2, dp // 2
    peers_z = n_dp // 2
    sibling = (dp, x * 2 + 1 - c)
    across = (dp, (1 - x) * 2 + c)
    beside = (dp + 1 - 2 * y, x * 2 + c)
    mine = pl.ds(at128(c * cols), cols)
    theirs = pl.ds(at128((1 - c) * cols), cols)
    steps = w_fc1_hbm.shape[1] // width

    units = {}
    for j in range(2):
        units["1", j] = (c1.at[2 * j + x], y1.at[j], z1.at[j], xo1.at[j], xi1.at[j], gi1.at[j, 0], j, j)
    units["2", 0] = (None, y2, z2, xo2, xi2, gi2, None, 4)
    units["3", 0] = (c3, y3, z3, xo3, xi3, gi3, 8, 5)
    for t in range(pairs):
        units["q", t] = (wq.at[t], yq.at[t], zq.at[t], xoq.at[t], xiq.at[t], giq.at[t], 9 + t, 6 + t)

    def pair_copy(pair):
        return remote(c1.at[2 * pair + 1 - x], p1.at[pair], (ps, pr), pair, across)

    def pair_done(pair):
        pair_copy(pair).wait()
        c1[2 * pair + x] = c1[2 * pair + x] + p1[pair]
        y_copy(("1", pair)).start()

    def y_copy(key):
        if key[0] == "2":
            size = n_dp // 8
            chunk = key[1]
            src = c2.at[chunk, :, pl.ds(1 - y, 1)]
            dst = y2.at[pl.ds(chunk * size, size)]
            return remote(src, dst, (ys, yr), 4 + chunk, beside)
        unit = units[key]
        return remote(unit[0].at[:, pl.ds(1 - y, 1)], unit[1], (ys, yr), unit[6], beside)

    def y_done(key):
        y_copy(key).wait_recv()
        if key[0] == "2":
            size = n_dp // 8
            here = pl.ds(key[1] * size, size)
            y2[here] = y2[here] + c2[key[1], :, pl.ds(y, 1)]
        else:
            unit = units[key]
            unit[1][...] = unit[1][...] + unit[0][:, pl.ds(y, 1)]

    def z_copy(key, i):
        unit = units[key]
        to = (m + i) % peers_z
        return remote(
            unit[1].at[to], unit[2].at[i - 1], (zs.at[unit[7]], zr.at[unit[7]]), i - 1, (2 * to + y, x * 2 + c)
        )

    def z_copies(key):
        return [z_copy(key, i) for i in range(1, peers_z)]

    def z_send(key):
        for copy in z_copies(key):
            copy.start()

    def z_send_chunk(chunk):
        size = n_dp // 8
        for i in range(size):
            to = chunk * size + i

            @pl.when(m != to)
            def _(to=to):
                z_copy(("2", 0), (to - m + peers_z) % peers_z).start()

    def z_done(key):
        unit = units[key]
        for copy in z_copies(key):
            copy.wait_recv()
        total = unit[1][m, 0].astype(F32)
        for i in range(peers_z - 1):
            total = total + unit[2][i, 0].astype(F32)
        unit[3][...] = total.astype(BF16)
        if key[0] == "1":
            g_copy(key).start()

    def x_copy(key):
        unit = units[key]
        return remote(unit[3], unit[4], (xs, xr), unit[7], across)

    def g_copy(key):
        unit = units[key]
        return remote(unit[3] if key[0] == "1" else unit[4], unit[5], (gs, gr), unit[7], sibling)

    def second_copy(pair):
        return remote(xi1.at[pair], gi1.at[pair, 1], (gs, gr), 2 + pair, sibling)

    def x_done(key):
        unit = units[key]
        x_copy(key).wait_recv()
        if key[0] == "1":
            second_copy(key[1]).start()
            return
        unit[4][...] = (unit[3][...].astype(F32) + unit[4][...].astype(F32)).astype(BF16)
        g_copy(key).start()

    def g_done(key):
        unit = units[key]
        g_copy(key).wait_recv()
        if key[0] == "1":
            second_copy(key[1]).wait_recv()
            for chip, who, ref in (
                (x, c, unit[3]), (1 - x, c, unit[4]), (x, 1 - c, unit[5]), (1 - x, 1 - c, gi1.at[key[1], 1])
            ):
                where = pl.ds(at128((2 * key[1] + chip) * width + who * cols), cols)
                sum_fc1[:, where] = ref[...]
            return
        for value, who in ((unit[4], c), (unit[5], 1 - c)):
            full = value[...]
            if key[0] == "2":
                sum_fc2[:, pl.ds(at128(who * cols), cols)] = full
            elif key[0] == "3":
                sum_out[:, pl.ds(at128(who * cols), cols)] = full
            else:
                for i in range(3):
                    where = pl.ds(at128(i * width + who * cols + key[1] * 128), 128)
                    sum_qkv[:, where] = full[:, i * 128 : (i + 1) * 128]

    quad = x * 2 + y

    def quad_copies(kind, size):
        copies = []
        for i in range(1, 4):
            to_x = x if i < 2 else 1 - x
            to_y = y if i % 2 == 0 else 1 - y
            here = va.at[kind, quad, pl.ds(0, size)]
            copies.append(remote(here, here, (vas.at[kind], var.at[kind]), i - 1, (2 * m + to_y, to_x * 2 + c)))
        return copies

    def line_copies(kind, size):
        copies = []
        for i in range(1, peers_z):
            here = vb.at[kind, m, pl.ds(0, size)]
            to = (m + i) % peers_z
            copies.append(remote(here, here, (vbs.at[kind], vbr.at[kind]), i - 1, (2 * to + y, x * 2 + c)))
        return copies

    def last_copy(kind, size):
        return remote(
            vc.at[kind, 0, pl.ds(0, size)], vc.at[kind, 1, pl.ds(0, size)], (vcs, vcr), kind, sibling
        )

    def quad_send(kind, size):
        for copy in quad_copies(kind, size):
            copy.start()

    def quad_done(kind, size):
        for copy in quad_copies(kind, size):
            copy.wait_recv()
        total = va[kind, 0, :size]
        for i in range(1, 4):
            total = total + va[kind, i, :size]
        vb[kind, m, :size] = total
        for copy in line_copies(kind, size):
            copy.start()

    def line_done(kind, size):
        for copy in line_copies(kind, size):
            copy.wait_recv()
        total = vb[kind, 0, :size]
        for i in range(1, peers_z):
            total = total + vb[kind, i, :size]
        vc[kind, 0, :size] = total
        last_copy(kind, size).start()

    def early_done():
        last_copy(0, 16).wait_recv()
        early[...] = vc[0, 0] + vc[0, 1]

    def late_done():
        last_copy(1, 8).wait_recv()
        ours, other_core = vc[1, 0, :8], vc[1, 1, :8]
        late[:8] = jnp.where(c == 0, ours, other_core)
        late[8:] = jnp.where(c == 0, other_core, ours)
        late[:2] = ours[:2] + other_core[:2]

    def load_pair(t, slot):
        copies = []
        for i, (src, dst) in enumerate(((q_hbm, q_aug), (k_hbm, k_aug), (v_hbm, v_aug))):
            copies.append(
                pltpu.make_async_copy(src.at[pl.ds(2 * t, 2)], dst.at[slot], lsem.at[3 * slot + i])
            )
        return copies

    plain = [
        pltpu.make_async_copy(a_hbm, att, lsem.at[6]),
        pltpu.make_async_copy(n_hbm.at[pl.ds(0, span)], nrm, lsem.at[7]),
    ]
    peers = [sibling, across, beside, (dp + 1 - 2 * y, (1 - x) * 2 + c)] + [(2 * ((m + i) % peers_z) + y, x * 2 + c) for i in range(1, peers_z)]
    announce(peers)

    row = lambda i: vectors[i : i + 1, :]
    live_col = column_of(live[...].astype(F32))
    def dense(w_out, w_fc1, w_fc2, w1, w2, w3, branch_attn, normed_s, g_mlp_s, branch_mlp, g_normed, hidden_s, g_pre_s, dsem):
        def load_chunk(j, slot):
            return [
                pltpu.make_async_copy(w_fc1_hbm.at[:, pl.ds(at128(j * width), width)], w_fc1.at[slot], dsem.at[slot]),
                pltpu.make_async_copy(
                    w_fc2_hbm.at[pl.ds(pl.multiple_of(j * width, width), width)], w_fc2.at[slot], dsem.at[2 + slot]
                ),
            ]

        load_out = pltpu.make_async_copy(w_out_hbm, w_out, dsem.at[4])
        load_out.start()
        for copy in load_chunk(0, 0):
            copy.start()
        for copy in load_pair(0, 0) + plain:
            copy.start()
        for i, vector in (
            (LN1_GAIN, ln1_gain), (B_OUT, b_out), (SCALE_ATTN, scale_attn), (LN2_GAIN, ln2_gain), (LN2_BIAS, ln2_bias),
            (B_FC2, b_fc2), (SCALE_MLP, scale_mlp),
        ):
            vectors[i : i + 1, :] = vector[...].astype(F32).reshape(1, width)
        for i in range(steps):
            vectors[B_FC1 + i : B_FC1 + i + 1, :] = b_fc1[i * width : (i + 1) * width].astype(F32).reshape(1, width)
        source = tokens[...].astype(F32)
        g_mlp = (grad_out[...].astype(F32) * (live_col * row(SCALE_MLP))).astype(BF16)
        g_mlp_s[...] = g_mlp
        sums = va.at[0, quad]
        sums[...] = jnp.zeros_like(sums)
        sums[4:5, :] = jnp.sum(g_mlp.astype(F32), axis=0, keepdims=True)
        sums[10:11, :] = jnp.sum(live_col * source * source, axis=0, keepdims=True)
        sums[13:14, :] = jnp.broadcast_to(jnp.sum(live_col, axis=0, keepdims=True), (1, width))
        load_out.wait()
        branch = dot(att_low[...], w_out[...]) + row(B_OUT)
        branch_attn[...] = branch
        part = live_col * row(SCALE_ATTN) * branch
        stream = source + part
        g_tokens[...] = stream
        sums[11:12, :] = jnp.sum(part * part, axis=0, keepdims=True)
        hat, unused = norm_stats(stream)
        normed_s[...] = (hat * row(LN2_GAIN) + row(LN2_BIAS)).astype(BF16)
        branch_mlp[...] = jnp.zeros_like(branch_mlp)
        g_normed[...] = jnp.zeros_like(g_normed)

        def core_copies(j):
            return [
                remote(w1.at[1 - c], c1.at[j], (cs, cr), j, sibling),
                remote(w2.at[1 - c], c2.at[j], (cs, cr), 4 + j, sibling),
            ]

        def core_done(j):
            for copy in core_copies(j):
                copy.wait()
            c2[j] = c2[j] + w2[c]
            size = n_dp // 8
            remote(
                c2.at[j, :, pl.ds(1 - y, 1)], y2.at[pl.ds(j * size, size)], (ys, yr), 4 + j, beside
            ).start()
            c1[j] = c1[j] + w1[c]
            for pair in range(2):

                @pl.when(j == 2 * pair + 1)
                def _(pair=pair):
                    pair_copy(pair).start()

        def chunk(j, unused):
            slot = j % 2
            for copy in load_chunk(j, slot):
                copy.wait()

            @pl.when(j + 1 < steps)
            def _():
                for copy in load_chunk(j + 1, 1 - slot):
                    copy.start()

            bias = vectors[pl.ds(B_FC1 + j, 1), :]
            third = width // 3
            slopes = []
            for i in range(3):
                here = slice(i * third, (i + 1) * third)
                u = dot(normed_s[...], w_fc1[slot, :, here]) + bias[:, here]
                square = u * u
                t = jnp.tanh(u * (GELU_A + GELU_A * GELU_B * square))
                hidden_s[:, here] = (0.5 * u * (1.0 + t)).astype(BF16)
                slope = 0.5 * (1.0 + t) + (0.5 * u) * (1.0 - t * t) * (GELU_A + (3.0 * GELU_A * GELU_B) * square)
                g_pre = (dot(g_mlp_s[...], w_fc2[slot, here, :], NT) * slope).astype(BF16)
                g_pre_s[:, here] = g_pre
                slopes.append(jnp.sum(g_pre.astype(F32), axis=0, keepdims=True))
            sums[pl.ds(6 + j, 1), :] = jnp.concatenate(slopes, axis=1)

            @pl.when(j > 0)
            def _():
                core_done(j - 1)

            @pl.when(j == steps - 1)
            def _():
                y_done(("2", 0))
                z_send_chunk(0)

            spread_halves(w2, dot(hidden_s[...], g_mlp_s[...], TN))
            spread_halves(w1, dot(normed_s[...], g_pre_s[...], TN))
            for copy in core_copies(j):
                copy.start()
            branch_mlp[...] += dot(hidden_s[...], w_fc2[slot])
            g_normed[...] += dot(g_pre_s[...], w_fc1[slot], NT)
            return unused

        meet(peers)
        lax.fori_loop(0, steps, chunk, 0)
        y_done(("2", 1))
        z_send_chunk(1)
        grad = grad_out[...].astype(F32)
        branch = branch_mlp[...] + row(B_FC2)
        part = live_col * row(SCALE_MLP) * branch
        stream = g_tokens[...]
        out[...] = (stream + part).astype(BF16)
        sums[12:13, :] = jnp.sum(part * part, axis=0, keepdims=True)
        sums[5:6, :] = jnp.sum(grad * live_col * branch, axis=0, keepdims=True)
        hat, scale = norm_stats(stream)
        g_n2 = g_normed[...]
        sums[2:3, :] = jnp.sum(g_n2 * hat, axis=0, keepdims=True)
        sums[3:4, :] = jnp.sum(g_n2, axis=0, keepdims=True)
        g_tokens[...] = grad + norm_back(g_n2, hat, scale, row(LN2_GAIN))
        gated = g_tokens[...] * live_col
        g_attn = (gated * row(SCALE_ATTN)).astype(BF16)
        g_att[...] = dot(g_attn, w_out[...], NT).astype(BF16)
        swap.start()
        core_done(jnp.int32(steps - 1))
        sums[1:2, :] = jnp.sum(gated * branch_attn[...], axis=0, keepdims=True)
        sums[0:1, :] = jnp.sum(g_attn.astype(F32), axis=0, keepdims=True)
        quad_send(0, 16)
        spread_halves(w3, dot(att_low[...], g_attn, TN))
        give = remote(w3.at[1 - c], c3, (cs, cr), 8, sibling)
        give.start()
        pair_done(0)
        y_done(("2", 2))
        z_send_chunk(2)
        give.wait()
        c3[...] = c3[...] + w3[c]
        y_copy(("3", 0)).start()

    def spread_rows(ref, value):
        size = ref.shape[-2]
        for i in range(ref.shape[0]):
            for k in range(2):
                ref[i, k] = value[(2 * i + k) * size : (2 * i + k + 1) * size].astype(BF16)

    def spread_halves(ref, value):
        for half in range(2):
            spread_rows(ref.at[half], value[:, half * cols : (half + 1) * cols])

    own = pl.ds(pl.multiple_of(c * rows, rows), rows)
    other = pl.ds(pl.multiple_of((1 - c) * rows, rows), rows)
    swap = remote(g_att.at[:, theirs], g_rows.at[own], (ss, sr), 0, sibling)
    part_rows = width // n_dp
    wide_rows = w_fc2_hbm.shape[0] // n_dp
    pl.run_scoped(
        dense,
        pltpu.VMEM((width, width), BF16),
        pltpu.VMEM((2, width, width), BF16),
        pltpu.VMEM((2, width, width), BF16),
        pltpu.VMEM((2, peers_z, 2, part_rows, cols), BF16),
        pltpu.VMEM((2, n_dp // 8, 2, wide_rows, cols), BF16),
        pltpu.VMEM((2, peers_z, 2, part_rows, cols), BF16),
        pltpu.VMEM((rows, width), F32),
        pltpu.VMEM((rows, width), BF16),
        pltpu.VMEM((rows, width), BF16),
        pltpu.VMEM((rows, width), F32),
        pltpu.VMEM((rows, width), F32),
        pltpu.VMEM((rows, width), BF16),
        pltpu.VMEM((rows, width), BF16),
        pltpu.SemaphoreType.DMA((5,)),
    )

    def attention(g_aug, dq, dkv, dkv_own, d_query, d_key, d_value, w_own):
        late_loads = [
            pltpu.make_async_copy(
                w_hbm.at[:, pl.ds(at128(part * width + c * cols), cols)], w_own.at[part], lsem.at[8 + part]
            )
            for part in range(3)
        ]
        for copy in late_loads:
            copy.start()
        g_rows[own] = g_att[:, mine]
        for copy in plain:
            copy.wait()
        swap.wait_recv()
        spot = lanes((span, 128))
        low = spot < head_dim
        for t in range(pairs):
            g = g_rows[:, t * 128 : (t + 1) * 128].astype(F32)
            product = g * att[t]
            for odd in range(2):
                delta = jnp.sum(jnp.where(low if odd == 0 else ~low, product, 0.0), axis=1, keepdims=True)
                tile = g if odd == 0 else pltpu.roll(g, 64, 1)
                tile = jnp.where(low, tile, 0.0)
                for i, piece in enumerate(split3(delta)):
                    tile = jnp.where(spot == 64 + i, -piece, tile)
                g_aug[2 * t + odd] = tile.astype(BF16)
        lane = lanes((256, 256))
        line = lax.broadcasted_iota(jnp.int32, (256, 256), 0)
        in_rows = (lane >= ROW0) & (lane < COL0) & (line >= ROW0) & (line < COL0)
        in_cols = (lane >= COL0) & (lane < SEG0) & (line >= COL0) & (line < SEG0)
        flip = jnp.where(lane + line == 255, 1.0, 0.0).astype(BF16)
        sums = va.at[1, quad]
        sums[...] = jnp.zeros_like(sums)
        block = rows

        def dkv_copy(t, odd):
            return remote(dkv_out.at[t, odd], dkv_in.at[t, odd], (ss, sr), 1 + 2 * t + odd, across)

        def finish_pair(t):
            for odd in range(2):
                dkv_copy(t, odd).wait_recv()
            first, second = (dkv_own[t % 2, odd] + dkv_in[t, odd].astype(F32) for odd in range(2))
            place_k = pl.ds(at128(t * 128), 128)
            dkv[0, :, place_k] = jnp.where(low, first, pltpu.roll(second, 64, 1)).astype(BF16)
            dkv[1, :, place_k] = jnp.where(low, pltpu.roll(first, 64, 1), second).astype(BF16)
            both = jnp.concatenate([dkv[0, :, place_k], dkv[1, :, place_k]], axis=1)
            part = jnp.concatenate([dq[:, place_k], both], axis=1)
            spread_rows(wq.at[t], dot(nrm[...], part, TN))
            y_copy(("q", t)).start()

        plan = {
            0: [lambda: y_done(("2", 3)), lambda: z_send_chunk(3)],
            2: [lambda: y_done(("1", 0)), lambda: z_send(("1", 0)), lambda: pair_done(1)],
            4: [lambda: y_done(("3", 0)), lambda: z_send(("3", 0))],
            5: [lambda: finish_pair(0), lambda: y_done(("1", 1)), lambda: z_send(("1", 1))],
            6: [lambda: quad_done(0, 16)],
            8: [lambda: finish_pair(1), lambda: y_done(("q", 0)), lambda: z_send(("q", 0))],
            10: [
                lambda: y_done(("q", 1)), lambda: z_send(("q", 1)), lambda: z_done(("1", 0)),
                lambda: x_copy(("1", 0)).start(), lambda: z_done(("3", 0)), lambda: x_copy(("3", 0)).start(),
            ],
            11: [lambda: line_done(0, 16), lambda: z_done(("2", 0)), lambda: x_copy(("2", 0)).start()],
        }

        def sweep(point, unused):
            it, odd = point // 2, point % 2
            part = 1 - it % 2
            t = it // 2
            slot = t % 2

            @pl.when((part == 1) & (odd == 0))
            def _():
                for copy in load_pair(t, slot):
                    copy.wait()

            @pl.when((part == 1) & (odd == 0) & (t + 1 < pairs))
            def _():
                for copy in load_pair(t + 1, 1 - slot):
                    copy.start()

            @pl.when(part == 1)
            def _():
                d_query[odd] = jnp.zeros(d_query.shape[1:], F32)

            for qb in range(span // block):
                here = slice(qb * block, (qb + 1) * block)
                queries, grads = q_aug[slot, odd, here, :], g_aug[2 * t + odd, here, :]
                total = d_query[odd, :, here]
                for kb in range(span // block):
                    there = slice(kb * block, (kb + 1) * block)
                    source = pl.ds(pl.multiple_of(part * span + kb * block, block), block)
                    keys = k_aug[slot, odd, source, :]
                    p = jnp.exp(dot(keys, queries, NT))
                    p_low = p.astype(BF16)
                    ds = (p * dot(v_aug[slot, odd, source, :], grads, NT)).astype(BF16)
                    gain_value = dot(p_low, grads)
                    gain_key = dot(ds, queries[:, :128])
                    if qb == 0:
                        d_value[odd, there, :] = gain_value
                        d_key[odd, there, :] = gain_key
                    else:
                        d_value[odd, there, :] += gain_value
                        d_key[odd, there, :] += gain_key
                    total = total + dot(keys, ds, TN)
                d_query[odd, :, here] = total
            new = jnp.where(low, d_key[odd], pltpu.roll(d_value[odd], 64, 1))

            @pl.when(part == 1)
            def _():
                dkv_out[t, odd] = new.astype(BF16)
                dkv_copy(t, odd).start()

            @pl.when(part == 0)
            def _():
                dkv_own[t % 2, odd] = new
                square = dot(d_query[odd].astype(BF16), k_aug[slot, odd, :span, :])
                h = 2 * t + odd
                for table, mask in enumerate((in_rows, in_cols)):
                    flipped = sum(dot(flip, piece.astype(BF16)) for piece in split3(jnp.where(mask, square, 0.0)))
                    turned = pltpu.roll(flipped, 0, 1, stride=1, stride_axis=0)
                    sums[pl.ds(3 + table * 2 + h // 3, 1), pl.ds(at128(h % 3 * 256), 256)] = jnp.sum(
                        turned, axis=0, keepdims=True
                    )

            @pl.when((part == 0) & (odd == 1))
            def _():
                both = jnp.concatenate([d_query[0, :head_dim, :], d_query[1, :head_dim, :]], axis=0)
                dq[:, pl.ds(at128(t * 128), 128)] = (jnp.transpose(both) * head_dim ** (-0.5)).astype(BF16)

            for i, acts in plan.items():

                @pl.when(point == i)
                def _(acts=acts):
                    for act in acts:
                        act()

            return unused

        lax.fori_loop(0, 4 * pairs, sweep, 0)
        last = pairs - 1
        finish_pair(last)
        for copy in late_loads:
            copy.wait()

        def through(where):
            total = dot(dq[where, :], w_own[0], NT)
            return total + dot(dkv[0, where, :], w_own[1], NT) + dot(dkv[1, where, :], w_own[2], NT)

        swap.wait_send()
        g_att[...] = through(other).astype(BF16)
        give = remote(g_att, half_in, (ss, sr), 1 + 2 * pairs, sibling)
        give.start()
        z_done(("q", 0))
        x_copy(("q", 0)).start()
        sums[2:3, :cols] = jnp.sum(dq[...].astype(F32), axis=0, keepdims=True)
        sums[2:3, cols:] = jnp.sum(dkv[1].astype(F32), axis=0, keepdims=True)
        g_n1 = through(own)
        hat, scale = norm_stats(tokens[...].astype(F32))
        give.wait_recv()
        g_n1 = g_n1 + half_in[...].astype(F32)
        sums[0:1, :] = jnp.sum(g_n1 * hat, axis=0, keepdims=True)
        sums[1:2, :] = jnp.sum(g_n1, axis=0, keepdims=True)
        quad_send(1, 8)
        y_done(("q", last))
        z_send(("q", last))
        z_done(("1", 1))
        x_copy(("1", 1)).start()
        g_tokens[...] = g_tokens[...] + norm_back(g_n1, hat, scale, row(LN1_GAIN))
        x_done(("3", 0))
        x_done(("1", 0))
        quad_done(1, 8)
        z_done(("q", 1))
        x_copy(("q", 1)).start()
        x_done(("q", 0))
        early_done()
        g_done(("3", 0))
        g_done(("1", 0))
        z_done(("q", last))
        x_copy(("q", last)).start()
        line_done(1, 8)
        x_done(("2", 0))
        x_done(("1", 1))
        x_done(("q", 1))
        g_done(("q", 0))
        g_done(("2", 0))
        g_done(("1", 1))
        x_done(("q", last))
        late_done()
        g_done(("q", 1))
        g_done(("q", last))
        give.wait_send()
        for t in range(pairs):
            for odd in range(2):
                dkv_copy(t, odd).wait_send()

    pl.run_scoped(
        attention,
        pltpu.VMEM((heads, span, 128), BF16),
        pltpu.VMEM((span, cols), BF16),
        pltpu.VMEM((2, span, cols), BF16),
        pltpu.VMEM((2, 2, span, 128), F32),
        pltpu.VMEM((2, 256, span), F32),
        pltpu.VMEM((2, span, 128), F32),
        pltpu.VMEM((2, span, 128), F32),
        pltpu.VMEM((3, width, cols), BF16),
    )
    for key in units:
        if key[0] != "2":
            y_copy(key).wait_send()
        for copy in z_copies(key):
            copy.wait_send()
        x_copy(key).wait_send()
        g_copy(key).wait_send()
    for j in range(4):
        y_copy(("2", j)).wait_send()
    for pair in range(2):
        second_copy(pair).wait_send()
    for kind, size in enumerate((16, 8)):
        for copy in quad_copies(kind, size) + line_copies(kind, size) + [last_copy(kind, size)]:
            copy.wait_send()


def backward(n_dp, att_low, tokens, grad_out, live, vectors, w_out, w_fc1, w_fc2, q_aug, k_aug, v_aug, att, nrm, w_qkv):
    rows, width = tokens.shape
    heads = q_aug.shape[0]
    pairs, cols = heads // 2, heads * 64
    span, group = 2 * rows, 4 * rows
    hidden = w_fc1.shape[1]
    steps = hidden // width
    z, part, wide = n_dp // 2, width // n_dp, hidden // n_dp
    any_spec = pl.BlockSpec(memory_space=pl.ANY)
    vmem = pl.BlockSpec(memory_space=pltpu.VMEM)
    low = lambda *shape: pltpu.VMEM(shape, BF16)
    full = lambda *shape: pltpu.VMEM(shape, F32)
    dma = lambda *shape: pltpu.SemaphoreType.DMA(shape)
    received = lambda *lead: [low(2, *lead, part, cols), low(wide, cols), low(part, cols), low(pairs, part, cols)]
    return pl.pallas_call(
        functools.partial(back_kernel, n_dp),
        out_shape=[
            jax.ShapeDtypeStruct((rows, width), BF16),
            jax.ShapeDtypeStruct((rows, width), F32),
            jax.ShapeDtypeStruct((part, 3 * width), BF16),
            jax.ShapeDtypeStruct((part, width), BF16),
            jax.ShapeDtypeStruct((part, hidden), BF16),
            jax.ShapeDtypeStruct((wide, width), BF16),
            jax.ShapeDtypeStruct((16, width), F32),
            jax.ShapeDtypeStruct((16, width), F32),
        ],
        in_specs=[vmem] * 12 + [any_spec] * 9,
        out_specs=[vmem] * 8,
        scratch_shapes=[
            low(2, 2, span, 256), low(2, 2, group, 256), low(2, 2, group, 128),
            full(pairs, span, 128), low(span, width),
            low(rows, width), low(span, cols), low(rows, width),
            low(pairs, 2, span, 128), low(pairs, 2, span, 128),
            low(steps, z, 2, part, cols), low(steps, n_dp // 8, 2, wide, cols), low(z, 2, part, cols),
            low(2, z, 2, part, cols),
            low(2, z, 1, part, cols), low(z, 1, wide, cols), low(z, 1, part, cols), low(pairs, z, 1, part, cols),
            low(2, z - 1, 1, part, cols), low(z - 1, 1, wide, cols), low(z - 1, 1, part, cols),
            low(pairs, z - 1, 1, part, cols),
            *received(), *received(), *received(2),
            low(pairs, z, 2, part, cols), full(2, 4, 16, width), full(2, z, 16, width), full(2, 2, 16, width), full(16, width),
            dma(9), dma(9), dma(2), dma(2), dma(12), dma(12), dma(9, z - 1), dma(9, z - 1), dma(9), dma(9), dma(9), dma(9),
            dma(2, 3), dma(2, 3), dma(2, z - 1), dma(2, z - 1), dma(2), dma(2), dma(2 + 2 * pairs), dma(2 + 2 * pairs),
            dma(11),
        ],
        compiler_params=pltpu.CompilerParams(
            collective_id=1, has_side_effects=True, vmem_limit_bytes=VMEM_LIMIT
        ),
        name="backward",
    )(att_low, tokens, grad_out, live, *vectors, w_out, w_fc1, w_fc2, q_aug, k_aug, v_aug, att, nrm, w_qkv)


def outputs_kernel(out_in, tokens_in, qkv_in, out_w_in, fc1_in, fc2_in, early, late, *refs):
    (
        out, g_tokens, g_ln1, b_ln1, qkv, b_query, b_value, out_w, b_out, s_attn, g_ln2, b_ln2, fc1, b_fc1, fc2,
        b_fc2, s_mlp, t_rows, t_cols, means,
    ) = refs
    width = out.shape[1]
    out[...] = out_in[...]
    g_tokens[...] = tokens_in[...]
    for ref, value in ((qkv, qkv_in), (out_w, out_w_in), (fc1, fc1_in), (fc2, fc2_in)):
        ref[...] = value[...].astype(F32)
    for i, ref in enumerate((b_out, s_attn, g_ln2, b_ln2, b_fc2, s_mlp)):
        ref[...] = early[i, :]
    for i in range(b_fc1.shape[0] // width):
        b_fc1[i * width : (i + 1) * width] = early[6 + i, :]
    g_ln1[...] = late[0, :]
    b_ln1[...] = late[1, :]
    half = width // 2
    b_query[...] = jnp.concatenate([late[2:3, :half], late[10:11, :half]], axis=1)[0]
    b_value[...] = jnp.concatenate([late[2:3, half:], late[10:11, half:]], axis=1)[0]
    count = early[13:14, :1]
    lane = lanes((1, 3))
    squares = jnp.zeros((1, 3), F32)
    for i in range(3):
        squares = jnp.where(lane == i, jnp.sum(early[10 + i : 11 + i, :], axis=1, keepdims=True), squares)
    means[...] = jnp.sqrt(squares / (count * width))[0]
    spans = t_rows.shape[1]
    limit = (spans - 1) // 2
    offset = lax.broadcasted_iota(jnp.int32, (256, spans), 0) + 1
    offset = jnp.where(offset < 128, offset, offset - 256)
    pick = jnp.where(jnp.clip(offset, -limit, limit) + limit == lanes((256, spans)), 1.0, 0.0).astype(BF16)
    for third in range(3):
        part = late[:, third * 256 : (third + 1) * 256]
        sums = sum(dot(piece.astype(BF16), pick) for piece in split3(part))
        for i in range(8):
            core, table, group = i // 4, i // 2 % 2, i % 2
            head, source = core * 6 + group * 3 + third, core * 8 + 3 + table * 2 + group
            (t_rows, t_cols)[table][head : head + 1, :] = sums[source : source + 1, :]


def write_outputs(arrays, shapes):
    vmem = pl.BlockSpec(memory_space=pltpu.VMEM)
    return pl.pallas_call(
        outputs_kernel,
        out_shape=[jax.ShapeDtypeStruct(*shape) for shape in shapes],
        in_specs=[vmem] * len(arrays),
        out_specs=[vmem] * len(shapes),
        compiler_params=pltpu.CompilerParams(vmem_limit_bytes=VMEM_LIMIT),
        name="outputs",
    )(*arrays)


def body(
    tokens, grad_out, segment, live_rows, coords, ln1_gain, ln1_bias, w_qkv, b_query, b_value, w_out,
    b_out, scale_attn, ln2_gain, ln2_bias, w_fc1, b_fc1, w_fc2, b_fc2, scale_mlp, table_rows, table_cols,
):
    rows, width = tokens.shape
    heads = table_rows.shape[0] // 2
    line = lambda v: v.reshape(1, -1)
    live = line(live_rows)
    att_low, q_aug, k_aug, v_aug, att, nrm = forward_attention(
        tokens, line(segment), live, coords, (ln1_gain, ln1_bias, b_query, b_value), table_rows, table_cols, w_qkv
    )
    out, g_tokens, sum_qkv, sum_out, sum_fc1, sum_fc2, early, late = backward(
        lax.axis_size("dp"), att_low, tokens, grad_out, live,
        (ln1_gain, b_out, scale_attn, ln2_gain, ln2_bias, b_fc2, scale_mlp, b_fc1), w_out, w_fc1, w_fc2,
        q_aug, k_aug, v_aug, att, nrm, w_qkv,
    )
    part, hidden = sum_out.shape[0], w_fc1.shape[1]
    vector, table = ((width,), F32), (table_rows.shape, F32)
    return write_outputs(
        (out, g_tokens, sum_qkv, sum_out, sum_fc1, sum_fc2, early, late),
        [
            ((rows, width), BF16), ((rows, width), F32), vector, vector, ((part, 3 * width), F32), vector, vector,
            ((part, width), F32), vector, vector, vector, vector, ((part, hidden), F32), ((hidden,), F32),
            (sum_fc2.shape, F32), vector, vector, table, table, ((3,), F32),
        ],
    )


def solution(mesh):
    rows = P(("dp", "blk"), None)
    flat = P(("dp", "blk"))
    return jax.shard_map(
        body,
        mesh=mesh,
        in_specs=(rows, rows, flat, flat, P(None, ("dp", "blk"))) + (P(),) * 17,
        out_specs=(
            rows, rows, P(), P(), P("dp", None), P(), P(), P("dp", None), P(), P(), P(), P(),
            P("dp", None), P(), P("dp", None), P(), P(), P(), P(), P(),
        ),
        check_vma=False,
    )
```
